256 devices in a mesh: wide: 32 (over z, x_hi, core), narrow: 8 (over x_lo, y).
Axes of the slice: x: 4 (x_hi: 2, x_lo: 2; x = x_hi * 2 + x_lo), y: 4, z: 8, core: 2. Of those that a mesh axis runs over, the one named last changes fastest.
Arguments:
- patches: bfloat16 [1024, 256, 1152], P('wide'), may hold values from -6 to 6
- w_key: bfloat16 [1152, 1152], P(None, 'narrow'), may hold values from -0.1875 to 0.1875
- w_value: bfloat16 [1152, 1152], P(None, 'narrow'), may hold values from -0.1875 to 0.1875
- w_out: bfloat16 [1152, 1152], P('narrow'), may hold values from -0.1875 to 0.1875
- probe: bfloat16 [1152], P('narrow'), may hold values from -64 to 64
- texts: bfloat16 [1024, 1152], P(('wide', 'narrow')), may hold values from -6 to 6
Outputs:
- row_loss: float32 [1024], P(('wide', 'narrow'))
- text_grad: float32 [1024, 1152], P(('wide', 'narrow'))
- grad_key: float32 [1152, 1152], P('wide', 'narrow')
- grad_value: float32 [1152, 1152], P('wide', 'narrow')
- grad_out: float32 [1152, 1152], P('narrow', 'wide')
The draws below stay inside these ranges and needn't reach their ends.
All inputs are finite; a program needn't handle non-finite values.
Results may differ from the reference program's by a relative error of at most 0.027.
The reference program's roundings to bfloat16 on the way count: a program that leaves them out, or rounds other values in their place, can miss the bound.
Values may be sent and summed in bfloat16 or wider, within the bound.
A program may use at most 128 MiB of HBM per device.

```python
import math
import jax
import jax.numpy as jnp
from jax import lax

D = 1152
HEADS = 16
HEAD_DIM = 72
PATCHES = 256
IMG_DEV = 4
BATCH = 1024
N_NARROW = 8


def draw_probe(key, part):
    key = jax.random.fold_in(key, 7)
    values = 3.0 * jax.random.normal(key, (D,), jnp.float32)
    return jnp.clip(values, -12.0, 12.0).astype(jnp.bfloat16)


def block_scale(key, extent, cuts, least, largest):
    factor_of = 1.0
    for position, shards_of in cuts:
        heights = jax.random.uniform(jax.random.fold_in(jax.random.fold_in(key, 6), position), (shards_of,), jnp.float32, least / len(cuts), largest / len(cuts))
        factor_of = factor_of * jnp.repeat(jnp.exp(heights), extent[position] // shards_of).reshape((-1,) + (1,) * (len(extent) - 1 - position))
    return factor_of


def normal_values(key, extent, width, limit, cuts=(), kind=jnp.bfloat16):
    array = jax.random.normal(key, extent, jnp.float32) * width
    if len(cuts) > 0:
        array = block_scale(key, extent, cuts, -0.22, 0.18) * array
    return jnp.clip(array, min=-limit, max=limit).astype(kind)


def setup_inputs(seed: int = 0) -> dict:
    arg_keys = jax.random.split(jax.random.key(seed), 7)
    return {
        "patches": normal_values(arg_keys[0], (BATCH, PATCHES, D), 1.0, 6.0, ((0, 32),)),
        "w_key": normal_values(arg_keys[1], (D, D), D ** -0.5, 0.1875, ((1, 8),)),
        "w_value": normal_values(arg_keys[2], (D, D), D ** -0.5, 0.1875, ((1, 8),)),
        "w_out": normal_values(arg_keys[3], (D, D), D ** -0.5, 0.1875, ((0, 8),)),
        "probe": draw_probe(jax.random.fold_in(arg_keys[6], 71), 0),
        "texts": normal_values(arg_keys[5], (BATCH, D), 1.0, 6.0, ((0, 256),)),
    }


logit_scale = 16.0
logit_bias = -4.0

def attend(images, w_both, probe_heads):
    count = images.shape[0]
    flat_rows = images.reshape(count * PATCHES, D)
    both_rows = jnp.dot(flat_rows, w_both, preferred_element_type=jnp.float32).astype(jnp.bfloat16)
    key_rows = both_rows[:, :D].reshape(count, PATCHES, HEADS, HEAD_DIM)
    value_rows = both_rows[:, D:].reshape(count, PATCHES, HEADS, HEAD_DIM)
    scores = jnp.einsum('bphc,hc->bhp', key_rows.astype(jnp.float32), probe_heads, precision=lax.Precision.HIGHEST) / math.sqrt(HEAD_DIM)
    weights = jax.nn.softmax(scores, axis=-1)
    weights_low = weights.astype(jnp.bfloat16)
    heads_out = jnp.einsum('bhp,bphc->bhc', weights_low.astype(jnp.float32), value_rows.astype(jnp.float32), precision=lax.Precision.HIGHEST)
    heads_out = heads_out.astype(jnp.bfloat16).reshape(count, D)
    return (flat_rows, value_rows, weights, weights_low, heads_out)

def reference(patches, w_key, w_value, w_out, probe, texts):
    group = IMG_DEV * N_NARROW
    w_both = jnp.concatenate([w_key, w_value], axis=1)
    probe_heads = probe.reshape(HEADS, HEAD_DIM).astype(jnp.float32)
    blocks = patches.reshape(BATCH // group, group, PATCHES, D)
    heads_all = lax.map(lambda images: attend(images, w_both, probe_heads)[4], blocks)
    heads_out = heads_all.reshape(BATCH, D)
    pooled = jnp.dot(heads_out, w_out, preferred_element_type=jnp.float32)
    pooled_norm = jnp.sqrt(lax.optimization_barrier(jnp.sum(pooled * pooled, axis=1, keepdims=True)) + 1e-06)
    image_unit = pooled / pooled_norm
    image_low = image_unit.astype(jnp.bfloat16)
    text_float = texts.astype(jnp.float32)
    text_norm = jnp.sqrt(lax.optimization_barrier(jnp.sum(text_float * text_float, axis=1, keepdims=True)) + 1e-06)
    text_unit = text_float / text_norm
    text_low = text_unit.astype(jnp.bfloat16)
    logits = logit_scale * jnp.dot(image_low, text_low.T, preferred_element_type=jnp.float32) + logit_bias
    indices = jnp.arange(BATCH, dtype=jnp.int32)
    signs = jnp.where(indices[:, None] == indices[None, :], 1.0, -1.0).astype(jnp.float32)
    row_loss = lax.optimization_barrier(jnp.sum(jax.nn.softplus(-signs * logits), axis=1))
    coef = -signs * jax.nn.sigmoid(-signs * logits)
    image_grad = logit_scale * jnp.dot(coef, text_low.astype(jnp.float32), precision=lax.Precision.HIGHEST)
    unit_grad = logit_scale * jnp.dot(coef.T, image_low.astype(jnp.float32), precision=lax.Precision.HIGHEST)
    text_grad = (unit_grad - text_unit * lax.optimization_barrier(jnp.sum(text_unit * unit_grad, axis=1, keepdims=True))) / text_norm
    pooled_grad = ((image_grad - image_unit * lax.optimization_barrier(jnp.sum(image_unit * image_grad, axis=1, keepdims=True))) / pooled_norm).astype(jnp.bfloat16)

    def backward(carry, inputs):
        images, grad_rows, head_rows = inputs
        flat_rows, value_rows, weights, weights_low, _ = attend(images, w_both, probe_heads)
        head_grad = jnp.dot(grad_rows, w_out.T, preferred_element_type=jnp.float32).reshape(group, HEADS, HEAD_DIM)
        out_term = jnp.dot(head_rows.T, grad_rows, preferred_element_type=jnp.float32)
        value_grad = jnp.einsum('bhp,bhc->bphc', weights_low.astype(jnp.float32), head_grad).astype(jnp.bfloat16)
        weight_grad = jnp.einsum('bhc,bphc->bhp', head_grad, value_rows.astype(jnp.float32), precision=lax.Precision.HIGHEST)
        score_grad = weights * (weight_grad - lax.optimization_barrier(jnp.sum(weights * weight_grad, axis=-1, keepdims=True)))
        key_grad = (jnp.einsum('bhp,hc->bphc', score_grad, probe_heads) / math.sqrt(HEAD_DIM)).astype(jnp.bfloat16)
        both_grad = jnp.concatenate([key_grad.reshape(group * PATCHES, D), value_grad.reshape(group * PATCHES, D)], axis=1)
        kv_term = jnp.dot(flat_rows.T, both_grad, preferred_element_type=jnp.float32)
        return ((carry[0] + kv_term, carry[1] + out_term), None)
    start = (jnp.zeros((D, 2 * D), jnp.float32), jnp.zeros((D, D), jnp.float32))
    totals, _ = lax.scan(backward, start, (blocks, pooled_grad.reshape(BATCH // group, group, D), heads_all))
    return (row_loss, text_grad, totals[0][:, :D], totals[0][:, D:], totals[1])
```

```python
import functools
import math

import jax
import jax.numpy as jnp
from jax import lax
from jax.experimental import pallas as pl
from jax.experimental.pallas import tpu as pltpu
from jax.sharding import PartitionSpec as P

D = 1152
HEAD_DIM = 72
PATCHES = 256
QUAD = 4
ROWS = 4
MESH = pl.DeviceIdType.MESH

logit_scale = 16.0
logit_bias = -4.0


def remote(src, dst, send, recv, device):
    copy = pltpu.make_async_remote_copy(
        src_ref=src,
        dst_ref=dst,
        send_sem=send,
        recv_sem=recv,
        device_id=device,
        device_id_type=MESH,
    )
    copy.start()
    return copy


def split_dot(coef, other, dims):
    high = coef.astype(jnp.bfloat16)
    rest = coef - high.astype(jnp.float32)
    mid = rest.astype(jnp.bfloat16)
    low = (rest - mid.astype(jnp.float32)).astype(jnp.bfloat16)
    dot = lambda part: lax.dot_general(part, other, dims, preferred_element_type=jnp.float32)
    return dot(low) + dot(mid) + dot(high)


def meet(devices):
    barrier = pltpu.get_barrier_semaphore()
    for device in devices:
        pl.semaphore_signal(barrier, inc=1, device_id=device, device_id_type=MESH)
    pl.semaphore_wait(barrier, len(devices))


def loss_kernel(
    nz, nn, partial, texts, loss_out, text_out, grad_out,
    rbuf, qbuf, tbuf, ibuf, gsrc, gbuf, usrc, ubuf, vsrc, vbuf, pbuf, nsend, nrecv, zsend, zrecv, qsend, qrecv,
):
    w, n = lax.axis_index("wide"), lax.axis_index("narrow")
    z, q = w // QUAD, lax.rem(w, QUAD)
    narrow_peers = [lax.rem(n + d, nn) for d in range(1, nn)]
    z_peers = [lax.rem(z + d, nz) for d in range(1, nz)]
    q_peers = [lax.rem(q + d, QUAD) for d in range(1, QUAD)]
    at_n = lambda k: {"wide": w, "narrow": k}
    at_z = lambda k: {"wide": k * QUAD + q, "narrow": n}
    at_q = lambda k: {"wide": z * QUAD + k, "narrow": n}
    meet([at_n(k) for k in narrow_peers] + [at_z(k) for k in z_peers] + [at_q(k) for k in q_peers])
    sent = []

    def exchange(peers, place, me, src, dst, send, recv):
        copies = [remote(src(k), dst.at[me], send.at[k], recv.at[me], place(k)) for k in peers]
        sent.extend(copies)

    def arrived(peers, buf, send, recv):
        for k in peers:
            pltpu.make_async_copy(buf.at[k], buf.at[k], recv.at[k]).wait()

    exchange(narrow_peers, at_n, n, lambda k: partial.at[k], rbuf, nsend.at[0], nrecv.at[0])
    text_float = texts[...].astype(jnp.float32)
    text_norm = jnp.sqrt(jnp.sum(text_float * text_float, axis=1, keepdims=True) + 1e-06)
    text_unit = text_float / text_norm
    qbuf[q] = text_unit.astype(jnp.bfloat16).astype(jnp.float32)
    exchange(q_peers, at_q, q, lambda k: qbuf.at[q], qbuf, qsend.at[0], qrecv.at[0])
    arrived(q_peers, qbuf, qsend.at[0], qrecv.at[0])
    tbuf[z] = jnp.concatenate([qbuf[k] for k in range(QUAD)], axis=0).astype(jnp.bfloat16)
    exchange(z_peers, at_z, z, lambda k: tbuf.at[z], tbuf, zsend.at[0], zrecv.at[0])

    arrived(narrow_peers, rbuf, nsend.at[0], nrecv.at[0])
    pooled = partial[n]
    for k in narrow_peers:
        pooled = pooled + rbuf[k]
    pooled_norm = jnp.sqrt(jnp.sum(pooled * pooled, axis=1, keepdims=True) + 1e-06)
    image_unit = pooled / pooled_norm
    ibuf[n] = image_unit.astype(jnp.bfloat16).astype(jnp.float32)
    exchange(narrow_peers, at_n, n, lambda k: ibuf.at[n], ibuf, nsend.at[1], nrecv.at[1])
    arrived(z_peers, tbuf, zsend.at[0], zrecv.at[0])
    arrived(narrow_peers, ibuf, nsend.at[1], nrecv.at[1])

    group, span = nn * ROWS, nz * QUAD * ROWS
    image_low = jnp.concatenate([ibuf[k] for k in range(nn)], axis=0).astype(jnp.bfloat16)
    text_low = tbuf[...].reshape(span, D)
    logits = (
        logit_scale
        * lax.dot_general(image_low, text_low, (((1,), (1,)), ((), ())), preferred_element_type=jnp.float32)
        + logit_bias
    )
    image_ids = w * group + lax.broadcasted_iota(jnp.int32, (group, span), 0)
    offsets = lax.broadcasted_iota(jnp.int32, (group, span), 1)
    text_ids = offsets // ROWS * group + n * ROWS + offsets % ROWS
    signs = jnp.where(image_ids == text_ids, 1.0, -1.0).astype(jnp.float32)
    margin = -signs * logits
    small = jnp.exp(-jnp.abs(margin))
    loss_part = jnp.sum(jnp.maximum(margin, 0.0) + jnp.log1p(small), axis=1, keepdims=True)
    coef = -signs * jnp.where(margin >= 0.0, 1.0, small) / (1.0 + small)
    image_part = logit_scale * split_dot(coef, text_low, (((1,), (0,)), ((), ())))
    for k in range(nn):
        gsrc[k, :, :D] = image_part[k * ROWS : (k + 1) * ROWS]
        gsrc[k, :, D:] = jnp.broadcast_to(loss_part[k * ROWS : (k + 1) * ROWS], (ROWS, 128))
    exchange(narrow_peers, at_n, n, lambda k: gsrc.at[k], gbuf, nsend.at[2], nrecv.at[2])
    text_part = logit_scale * split_dot(coef.T, image_low, (((1,), (0,)), ((), ())))
    usrc[...] = text_part.astype(jnp.bfloat16).reshape(nz, QUAD * ROWS, D)
    exchange(z_peers, at_z, z, lambda k: usrc.at[k], ubuf, zsend.at[1], zrecv.at[1])

    arrived(narrow_peers, gbuf, nsend.at[2], nrecv.at[2])
    both = gsrc[n]
    for k in narrow_peers:
        both = both + gbuf[k]
    loss_out[...] = both[:, D:]
    image_grad = both[:, :D]
    pooled_grad = (
        image_grad - image_unit * jnp.sum(image_unit * image_grad, axis=1, keepdims=True)
    ) / pooled_norm
    pbuf[n] = pooled_grad.astype(jnp.bfloat16).astype(jnp.float32)
    exchange(narrow_peers, at_n, n, lambda k: pbuf.at[n], pbuf, nsend.at[3], nrecv.at[3])

    arrived(z_peers, ubuf, zsend.at[1], zrecv.at[1])
    quad_grad = usrc[z].astype(jnp.float32)
    for k in z_peers:
        quad_grad = quad_grad + ubuf[k].astype(jnp.float32)
    for k in range(QUAD):
        vsrc[k] = quad_grad[k * ROWS : (k + 1) * ROWS]
    exchange(q_peers, at_q, q, lambda k: vsrc.at[k], vbuf, qsend.at[1], qrecv.at[1])
    arrived(narrow_peers, pbuf, nsend.at[3], nrecv.at[3])
    grad_out[...] = jnp.concatenate([pbuf[k] for k in range(nn)], axis=0).astype(jnp.bfloat16)
    arrived(q_peers, vbuf, qsend.at[1], qrecv.at[1])
    unit_grad = vsrc[q]
    for k in q_peers:
        unit_grad = unit_grad + vbuf[k]
    text_out[...] = (
        unit_grad - text_unit * jnp.sum(text_unit * unit_grad, axis=1, keepdims=True)
    ) / text_norm
    for copy in sent:
        copy.wait_send()


def loss_call(nz, nn, partial, texts):
    vmem = pl.BlockSpec(memory_space=pltpu.VMEM)
    f32, bf16 = jnp.float32, jnp.bfloat16
    return pl.pallas_call(
        functools.partial(loss_kernel, nz, nn),
        out_shape=(
            jax.ShapeDtypeStruct((ROWS, 128), f32),
            jax.ShapeDtypeStruct((ROWS, D), f32),
            jax.ShapeDtypeStruct((nn * ROWS, D), bf16),
        ),
        in_specs=[vmem] * 2,
        out_specs=(vmem,) * 3,
        scratch_shapes=[
            pltpu.VMEM((nn, ROWS, D), f32),
            pltpu.VMEM((QUAD, ROWS, D), f32),
            pltpu.VMEM((nz, QUAD * ROWS, D), bf16),
            pltpu.VMEM((nn, ROWS, D), f32),
            pltpu.VMEM((nn, ROWS, D + 128), f32),
            pltpu.VMEM((nn, ROWS, D + 128), f32),
            pltpu.VMEM((nz, QUAD * ROWS, D), bf16),
            pltpu.VMEM((nz, QUAD * ROWS, D), bf16),
            pltpu.VMEM((QUAD, ROWS, D), f32),
            pltpu.VMEM((QUAD, ROWS, D), f32),
            pltpu.VMEM((nn, ROWS, D), f32),
            pltpu.SemaphoreType.DMA((4, nn)),
            pltpu.SemaphoreType.DMA((4, nn)),
            pltpu.SemaphoreType.DMA((2, nz)),
            pltpu.SemaphoreType.DMA((2, nz)),
            pltpu.SemaphoreType.DMA((2, QUAD)),
            pltpu.SemaphoreType.DMA((2, QUAD)),
        ],
        compiler_params=pltpu.CompilerParams(
            collective_id=0, has_side_effects=True, vmem_limit_bytes=32 * 1024 * 1024
        ),
    )(partial, texts)


def sum_kernel(nz, grads, out, abuf, hsrc, hbuf, ssrc, sbuf, asend, arecv, zsend, zrecv, qsend, qrecv):
    w, n = lax.axis_index("wide"), lax.axis_index("narrow")
    z, q = w // QUAD, lax.rem(w, QUAD)
    core = lax.rem(q, 2)
    z_peers = [lax.rem(z + d, nz) for d in range(1, nz)]
    q_peers = [lax.rem(q + d, QUAD) for d in range(1, QUAD)]
    at_z = lambda k: {"wide": k * QUAD + q, "narrow": n}
    at_q = lambda k: {"wide": z * QUAD + k, "narrow": n}
    sibling = at_q(q + 1 - 2 * core)
    meet([at_z(k) for k in z_peers] + [at_q(k) for k in q_peers])
    sent = []
    order = z_peers + [z]
    for k in order:
        sent.append(remote(grads.at[1 - core, k], abuf.at[k], asend.at[k], arecv.at[k], sibling))
    for i, k in enumerate(order):
        pltpu.make_async_copy(abuf.at[k], abuf.at[k], arecv.at[k]).wait()
        total = grads[core, k] + abuf[k]
        if i < nz - 1:
            hsrc[k] = total.astype(hsrc.dtype)
            sent.append(remote(hsrc.at[k], hbuf.at[z], zsend.at[k], zrecv.at[z], at_z(k)))
    for k in reversed(z_peers):
        pltpu.make_async_copy(hbuf.at[k], hbuf.at[k], zrecv.at[k]).wait()
        total = total + hbuf[k].astype(jnp.float32)
    rows = total.shape[0] // QUAD
    for k in range(QUAD):
        ssrc[k] = total[k * rows : (k + 1) * rows]
    for k in q_peers:
        sent.append(remote(ssrc.at[k], sbuf.at[q], qsend.at[k], qrecv.at[q], at_q(k)))
    sbuf[q] = ssrc[q]
    for k in q_peers:
        pltpu.make_async_copy(sbuf.at[k], sbuf.at[k], qrecv.at[k]).wait()
    width = total.shape[1]
    out[:, :width] = sbuf[0] + sbuf[2]
    out[:, width:] = sbuf[1] + sbuf[3]
    for copy in sent:
        copy.wait_send()


def sum_call(nz, grads):
    vmem = pl.BlockSpec(memory_space=pltpu.VMEM)
    f32, bf16 = jnp.float32, jnp.bfloat16
    _, _, rows, width = grads.shape
    return pl.pallas_call(
        functools.partial(sum_kernel, nz),
        out_shape=jax.ShapeDtypeStruct((rows // QUAD, 2 * width), f32),
        in_specs=[vmem],
        out_specs=vmem,
        scratch_shapes=[
            pltpu.VMEM((nz, rows, width), f32),
            pltpu.VMEM((nz, rows, width), f32),
            pltpu.VMEM((nz, rows, width), f32),
            pltpu.VMEM((QUAD, rows // QUAD, width), f32),
            pltpu.VMEM((QUAD, rows // QUAD, width), f32),
            pltpu.SemaphoreType.DMA((nz,)),
            pltpu.SemaphoreType.DMA((nz,)),
            pltpu.SemaphoreType.DMA((nz,)),
            pltpu.SemaphoreType.DMA((nz,)),
            pltpu.SemaphoreType.DMA((QUAD,)),
            pltpu.SemaphoreType.DMA((QUAD,)),
        ],
        compiler_params=pltpu.CompilerParams(
            collective_id=1, has_side_effects=True, vmem_limit_bytes=32 * 1024 * 1024
        ),
    )(grads)


def shards(patches, w_key, w_value, w_out, probe, texts):
    nz = lax.axis_size("wide") // QUAD
    nn = lax.axis_size("narrow")
    group = patches.shape[0]
    local_width = w_key.shape[1]
    local_heads = local_width // HEAD_DIM
    root_scale = 1.0 / math.sqrt(HEAD_DIM)
    w_both = jnp.concatenate([w_key, w_value], axis=1)
    probe_heads = probe.reshape(local_heads, HEAD_DIM)
    flat_rows = patches.reshape(group * PATCHES, D)
    both_rows = jnp.dot(flat_rows, w_both, preferred_element_type=jnp.float32).astype(jnp.bfloat16)
    key_rows = both_rows[:, :local_width].reshape(group, PATCHES, local_heads, HEAD_DIM)
    value_rows = both_rows[:, local_width:].reshape(group, PATCHES, local_heads, HEAD_DIM)
    scores = (
        jnp.einsum("gphc,hc->ghp", key_rows, probe_heads, preferred_element_type=jnp.float32)
        * root_scale
    )
    weights = jax.nn.softmax(scores, axis=-1)
    weights_low = weights.astype(jnp.bfloat16)
    heads_out = jnp.einsum(
        "ghp,gphc->ghc", weights_low, value_rows, preferred_element_type=jnp.float32
    )
    heads_out = heads_out.astype(jnp.bfloat16).reshape(group, local_width)
    partial_out = jnp.dot(heads_out, w_out, preferred_element_type=jnp.float32)
    row_loss, text_grad, group_grad = loss_call(nz, nn, partial_out.reshape(nn, ROWS, D), texts)
    head_grad = jnp.dot(group_grad, w_out.T, preferred_element_type=jnp.float32).reshape(
        group, local_heads, HEAD_DIM
    )
    out_term = lax.dot_general(
        group_grad, heads_out, (((0,), (0,)), ((), ())), preferred_element_type=jnp.float32
    )
    value_grad = jnp.einsum("ghp,ghc->gphc", weights_low.astype(jnp.float32), head_grad).astype(
        jnp.bfloat16
    )
    weight_grad = jnp.einsum(
        "ghc,gphc->ghp", head_grad, value_rows, precision=lax.Precision.HIGHEST
    )
    score_grad = weights * (weight_grad - jnp.sum(weights * weight_grad, axis=-1, keepdims=True))
    key_grad = (
        jnp.einsum("ghp,hc->gphc", score_grad, probe_heads.astype(jnp.float32)) * root_scale
    ).astype(jnp.bfloat16)
    both_grad = jnp.concatenate(
        [
            key_grad.reshape(group * PATCHES, local_width),
            value_grad.reshape(group * PATCHES, local_width),
        ],
        axis=1,
    )
    kv_term = lax.dot_general(
        flat_rows, both_grad, (((0,), (0,)), ((), ())), preferred_element_type=jnp.float32
    )
    half = 256
    first = kv_term[:, :half]
    second = jnp.concatenate(
        [kv_term[:, half:], out_term, jnp.zeros((D, 2 * half - 3 * local_width), jnp.float32)], axis=1
    )
    grads = jnp.stack([first, second]).reshape(2, nz, D // nz, half)
    total = sum_call(nz, grads)
    return (
        row_loss[:, 0],
        text_grad,
        total[:, :local_width],
        total[:, local_width : 2 * local_width],
        total[:, 2 * local_width : 3 * local_width].T,
    )


def solution(mesh):
    return jax.shard_map(
        shards,
        mesh=mesh,
        in_specs=(
            P("wide", None, None),
            P(None, "narrow"),
            P(None, "narrow"),
            P("narrow", None),
            P("narrow"),
            P(("wide", "narrow"), None),
        ),
        out_specs=(
            P(("wide", "narrow")),
            P(("wide", "narrow"), None),
            P("wide", "narrow"),
            P("wide", "narrow"),
            P("narrow", "wide"),
        ),
        check_vma=False,
    )
```

```python
import functools
import math

import jax
import jax.numpy as jnp
from jax import lax
from jax.experimental import pallas as pl
from jax.experimental.pallas import tpu as pltpu
from jax.sharding import PartitionSpec as P

D = 1152
HEAD_DIM = 72
PATCHES = 256
QUAD = 4
ROWS = 4
MESH = pl.DeviceIdType.MESH

logit_scale = 16.0
logit_bias = -4.0


def remote(src, dst, send, recv, device):
    copy = pltpu.make_async_remote_copy(
        src_ref=src,
        dst_ref=dst,
        send_sem=send,
        recv_sem=recv,
        device_id=device,
        device_id_type=MESH,
    )
    copy.start()
    return copy


def split_dot(coef, other, dims):
    high = coef.astype(jnp.bfloat16)
    rest = coef - high.astype(jnp.float32)
    mid = rest.astype(jnp.bfloat16)
    low = (rest - mid.astype(jnp.float32)).astype(jnp.bfloat16)
    dot = lambda part: lax.dot_general(part, other, dims, preferred_element_type=jnp.float32)
    return dot(low) + dot(mid) + dot(high)


CHUNK = 4
SPAN = CHUNK * PATCHES
SLOTS = 2 * CHUNK
WIDTH = 384
NT = (((1,), (1,)), ((), ()))
NN = (((1,), (0,)), ((), ()))


def matmul(a, b, dims=NN):
    return lax.dot_general(a, b, dims, preferred_element_type=jnp.float32)


def high_low(values):
    high = values.astype(jnp.bfloat16)
    low = (values - high.astype(jnp.float32)).astype(jnp.bfloat16)
    return high, low


def iota(shape, axis):
    return lax.broadcasted_iota(jnp.int32, shape, axis)


def kernel(
    nz, nn, patches, w_key, w_value, w_out, probe, texts,
    loss_out, text_out, key_out, value_out, out_out,
    held, both_t, keys, values, weights, heads, pooled_rows, left,
    psrc, rbuf, qbuf, tbuf, ibuf, gsrc, gbuf, usrc, ubuf, vsrc, vbuf, pbuf,
    grads, abuf, xsrc, xbuf, zsrc, zbuf, head_rows, ssum, sbuf, szsum, szbuf,
    loads, nsend, nrecv, zsend, zrecv, qsend, qrecv, asend, arecv, xsend, xrecv,
):
    f32, bf16 = jnp.float32, jnp.bfloat16
    w, n = lax.axis_index("wide"), lax.axis_index("narrow")
    z, q = w // QUAD, lax.rem(w, QUAD)
    x, core = q // 2, lax.rem(q, 2)
    group, span = nn * ROWS, nz * QUAD * ROWS
    chunks = group // CHUNK
    width = w_key.shape[1]
    root_scale = 1.0 / math.sqrt(HEAD_DIM)
    narrow_peers = [lax.rem(n + d, nn) for d in range(1, nn)]
    z_peers = [lax.rem(z + d, nz) for d in range(1, nz)]
    q_peers = [lax.rem(q + d, QUAD) for d in range(1, QUAD)]
    at_n = lambda k: {"wide": w, "narrow": k}
    at_z = lambda k: {"wide": k * QUAD + q, "narrow": n}
    at_q = lambda k: {"wide": z * QUAD + k, "narrow": n}
    sibling = at_q(q + 1 - 2 * core)
    across = at_q(2 * (1 - x) + core)
    order = z_peers + [z]

    for j in range(chunks):
        pltpu.make_async_copy(patches.at[pl.ds(j * SPAN, SPAN)], held.at[j], loads.at[j]).start()
    barrier = pltpu.get_barrier_semaphore()
    partners = [at_n(k) for k in narrow_peers] + [at_z(k) for k in z_peers] + [at_q(k) for k in q_peers]
    for device in partners:
        pl.semaphore_signal(barrier, inc=1, device_id=device, device_id_type=MESH)
    sent = []

    def exchange(peers, place, me, src, dst, send, recv):
        copies = [remote(src(k), dst.at[me], send.at[k], recv.at[me], place(k)) for k in peers]
        sent.extend(copies)

    def arrived(peers, buf, recv):
        for k in peers:
            pltpu.make_async_copy(buf.at[k], buf.at[k], recv.at[k]).wait()

    both_t[:width] = w_key[...].T
    both_t[width:] = w_value[...].T
    slot_head = iota((SLOTS, width), 0) // CHUNK
    lane_head = iota((SLOTS, width), 1) // HEAD_DIM
    probe_row = probe[...].astype(f32)
    probe_slots = jnp.where(slot_head == lane_head, probe_row, 0.0).astype(bf16)
    slot_image = iota((SLOTS, SPAN), 0) % CHUNK
    own = slot_image == iota((SLOTS, SPAN), 1) // PATCHES

    def project(j, slot):
        pltpu.make_async_copy(held.at[j], held.at[j], loads.at[j]).wait()
        rows = matmul(both_t[...], held[j], NT).astype(bf16)
        keys[slot] = rows[:width]
        values[j] = rows[width:]

    def pool(j, slot):
        scores = matmul(probe_slots, keys[slot]) * root_scale
        scores = jnp.where(own, scores, -1e30)
        top = jnp.max(scores, axis=1, keepdims=True)
        shifted = jnp.where(own, jnp.exp(scores - top), 0.0)
        part = shifted / jnp.sum(shifted, axis=1, keepdims=True)
        weights[j] = part
        heads[j] = matmul(part.astype(bf16), values[j], NT)

    project(0, 0)

    def step(j, carry):
        project(j, lax.rem(j, 2))
        pool(j - 1, lax.rem(j + 1, 2))
        return carry

    first, second = chunks // 2, chunks - 2
    lax.fori_loop(1, first, step, 0)
    pl.semaphore_wait(barrier, len(partners))
    text_float = texts[...].astype(f32)
    text_norm = jnp.sqrt(jnp.sum(text_float * text_float, axis=1, keepdims=True) + 1e-06)
    text_unit = text_float / text_norm
    qbuf[q] = text_unit.astype(bf16).astype(f32)
    exchange(q_peers, at_q, q, lambda k: qbuf.at[q], qbuf, qsend.at[0], qrecv.at[0])
    lax.fori_loop(first, second, step, 0)
    arrived(q_peers, qbuf, qrecv.at[0])
    tbuf[z] = jnp.concatenate([qbuf[k] for k in range(QUAD)], axis=0).astype(bf16)
    exchange(z_peers, at_z, z, lambda k: tbuf.at[z], tbuf, zsend.at[0], zrecv.at[0])
    lax.fori_loop(second, chunks, step, 0)
    pool(chunks - 1, (chunks - 1) % 2)

    all_slots = chunks * SLOTS
    slot_of = iota((all_slots, width), 0)
    head_mask = (slot_of % SLOTS) // CHUNK == iota((all_slots, width), 1) // HEAD_DIM
    heads_slots = jnp.where(head_mask, heads[...].reshape(all_slots, width), 0.0).astype(bf16)
    row_of = iota((group, all_slots), 0)
    slot_at = iota((group, all_slots), 1)
    gather = jnp.where(slot_at // SLOTS * CHUNK + slot_at % CHUNK == row_of, 1.0, 0.0).astype(bf16)
    heads_out = matmul(gather, heads_slots).astype(bf16)
    partial = matmul(heads_out, w_out[...])
    for k in range(nn):
        psrc[k] = partial[k * ROWS : (k + 1) * ROWS]
    exchange(narrow_peers, at_n, n, lambda k: psrc.at[k], rbuf, nsend.at[0], nrecv.at[0])

    def pool_rows(first, last):
        for j in range(first, last):
            rows = matmul(weights[j].astype(bf16), held[j])
            pooled_rows[j * SLOTS : (j + 1) * SLOTS] = rows

    half = chunks // 2
    pool_rows(0, half)
    arrived(narrow_peers, rbuf, nrecv.at[0])
    pooled = psrc[n]
    for k in narrow_peers:
        pooled = pooled + rbuf[k]
    pooled_norm = jnp.sqrt(jnp.sum(pooled * pooled, axis=1, keepdims=True) + 1e-06)
    image_unit = pooled / pooled_norm
    ibuf[n] = image_unit.astype(bf16).astype(f32)
    exchange(narrow_peers, at_n, n, lambda k: ibuf.at[n], ibuf, nsend.at[1], nrecv.at[1])
    pool_rows(half, chunks)
    arrived(z_peers, tbuf, zrecv.at[0])
    arrived(narrow_peers, ibuf, nrecv.at[1])

    image_low = jnp.concatenate([ibuf[k] for k in range(nn)], axis=0).astype(bf16)
    text_low = tbuf[...].reshape(span, D)
    logits = logit_scale * matmul(image_low, text_low, NT) + logit_bias
    image_ids = w * group + iota((group, span), 0)
    offsets = iota((group, span), 1)
    text_ids = offsets // ROWS * group + n * ROWS + offsets % ROWS
    signs = jnp.where(image_ids == text_ids, 1.0, -1.0).astype(f32)
    margin = -signs * logits
    small = jnp.exp(-jnp.abs(margin))
    loss_part = jnp.sum(jnp.maximum(margin, 0.0) + jnp.log1p(small), axis=1, keepdims=True)
    coef = -signs * jnp.where(margin >= 0.0, 1.0, small) / (1.0 + small)
    image_part = logit_scale * split_dot(coef, text_low, NN)
    for k in range(nn):
        gsrc[k, :, :D] = image_part[k * ROWS : (k + 1) * ROWS]
        gsrc[k, :, D:] = jnp.broadcast_to(loss_part[k * ROWS : (k + 1) * ROWS], (ROWS, 128))
    exchange(narrow_peers, at_n, n, lambda k: gsrc.at[k], gbuf, nsend.at[2], nrecv.at[2])
    text_part = logit_scale * split_dot(coef.T, image_low, NN)
    usrc[...] = text_part.astype(bf16).reshape(nz, QUAD * ROWS, D)
    exchange(z_peers, at_z, z, lambda k: usrc.at[k], ubuf, zsend.at[1], zrecv.at[1])
    high, low = high_low(pooled_rows[...])
    pooled_t = jnp.concatenate([high, low, high], axis=0).T
    blocks = D // nz
    for k in range(nz):
        left[k, :, : 3 * all_slots] = pooled_t[k * blocks : (k + 1) * blocks]

    arrived(narrow_peers, gbuf, nrecv.at[2])
    both = gsrc[n]
    for k in narrow_peers:
        both = both + gbuf[k]
    loss_out[...] = both[:, D:]
    image_grad = both[:, :D]
    pooled_grad = (
        image_grad - image_unit * jnp.sum(image_unit * image_grad, axis=1, keepdims=True)
    ) / pooled_norm
    pbuf[n] = pooled_grad.astype(bf16).astype(f32)
    exchange(narrow_peers, at_n, n, lambda k: pbuf.at[n], pbuf, nsend.at[3], nrecv.at[3])

    arrived(z_peers, ubuf, zrecv.at[1])
    quad_grad = usrc[z].astype(f32)
    for k in z_peers:
        quad_grad = quad_grad + ubuf[k].astype(f32)
    for k in range(QUAD):
        vsrc[k] = quad_grad[k * ROWS : (k + 1) * ROWS]
    exchange(q_peers, at_q, q, lambda k: vsrc.at[k], vbuf, qsend.at[1], qrecv.at[1])

    arrived(narrow_peers, pbuf, nrecv.at[3])
    group_float = jnp.concatenate([pbuf[k] for k in range(nn)], axis=0)
    group_grad = group_float.astype(bf16)
    scatter = jnp.where(
        iota((all_slots, group), 0) // SLOTS * CHUNK + iota((all_slots, group), 0) % CHUNK
        == iota((all_slots, group), 1),
        1.0,
        0.0,
    ).astype(bf16)
    slot_grads = matmul(scatter, group_grad).astype(bf16)
    head_grad = jnp.where(head_mask, matmul(slot_grads, w_out[...], NT), 0.0)
    high = head_grad.astype(bf16).astype(f32)
    low = head_grad - high
    none = lambda rows, columns: jnp.zeros((rows, columns), f32)
    spare = 4 * all_slots - 3 * all_slots - group
    turned = jnp.concatenate([group_float, none(spare, D)], axis=0).astype(bf16).T
    for k in range(nz):
        left[k, :, 3 * all_slots :] = turned[k * blocks : (k + 1) * blocks]

    def value_rows(part):
        return jnp.concatenate(
            [part[:, :128], none(all_slots, 128), part[:, 128:], none(all_slots, 112)], axis=1
        )

    heads_float = heads_out.astype(f32)
    out_rows = jnp.concatenate(
        [none(group, 128), heads_float[:, :128], none(group, 16), heads_float[:, 128:], none(group, 96)],
        axis=1,
    )
    right = jnp.concatenate(
        [value_rows(high), value_rows(high), value_rows(low), out_rows, none(spare, WIDTH)], axis=0
    ).astype(bf16)
    rows = blocks // QUAD
    for k in order:
        block = matmul(left[k], right)
        for there in range(QUAD):
            grads[k, there % 2, there // 2] = block[there * rows : (there + 1) * rows]
        sent.append(remote(grads.at[k, 1 - core], abuf.at[k], asend.at[k], arecv.at[k], sibling))
    for j in range(chunks):
        pair = [high[j * SLOTS : (j + 1) * SLOTS], low[j * SLOTS : (j + 1) * SLOTS]]
        head_rows[j] = jnp.concatenate(pair, axis=0).astype(bf16)

    score_sum = none(2 * SLOTS, D)
    for j in range(chunks):
        weight_grad = matmul(head_rows[j], values[j])
        weight_grad = weight_grad[:SLOTS] + weight_grad[SLOTS:]
        part = weights[j]
        inner = jnp.sum(part * weight_grad, axis=1, keepdims=True)
        score_grad = part * (weight_grad - inner)
        top = score_grad.astype(bf16).astype(f32)
        pair = jnp.concatenate([top, score_grad - top], axis=0).astype(bf16)
        score_sum = score_sum + matmul(pair, held[j])
    per_head = score_sum[:SLOTS] + score_sum[SLOTS:]
    for h in range(2):
        ssum[h : h + 1] = jnp.sum(per_head[h * CHUNK : (h + 1) * CHUNK], axis=0, keepdims=True)
    sbuf[q] = ssum[...]
    exchange(q_peers, at_q, q, lambda k: ssum, sbuf, qsend.at[2], qrecv.at[2])

    for k in order:
        pltpu.make_async_copy(abuf.at[k], abuf.at[k], arecv.at[k]).wait()
        xsrc[k] = grads[k, core, 1 - x] + abuf[k, 1 - x]
        sent.append(remote(xsrc.at[k], xbuf.at[k], xsend.at[k], xrecv.at[k], across))
    arrived(q_peers, sbuf, qrecv.at[2])
    szsum[...] = sbuf[0] + sbuf[1] + sbuf[2] + sbuf[3]
    exchange(z_peers, at_z, z, lambda k: szsum, szbuf, zsend.at[2], zrecv.at[2])
    for i, k in enumerate(order):
        pltpu.make_async_copy(xbuf.at[k], xbuf.at[k], xrecv.at[k]).wait()
        total = grads[k, core, x] + abuf[k, x] + xbuf[k]
        if i < nz - 1:
            zsrc[k] = total
            sent.append(remote(zsrc.at[k], zbuf.at[z], zsend.at[3, k], zrecv.at[3, z], at_z(k)))

    arrived(q_peers, vbuf, qrecv.at[1])
    unit_grad = vsrc[q]
    for k in q_peers:
        unit_grad = unit_grad + vbuf[k]
    text_out[...] = (
        unit_grad - text_unit * jnp.sum(text_unit * unit_grad, axis=1, keepdims=True)
    ) / text_norm

    arrived(z_peers, szbuf, zrecv.at[2])
    scores_all = szsum[...]
    for k in z_peers:
        scores_all = scores_all + szbuf[k]
    one = scores_all.astype(bf16).astype(f32)
    two = (scores_all - one).astype(bf16).astype(f32)
    three = scores_all - one - two
    parts = jnp.concatenate([one, two, three, none(2, D)], axis=0).astype(bf16)
    pick = jnp.where(iota((rows, D), 0) + w * rows == iota((rows, D), 1), 1.0, 0.0).astype(bf16)
    picked = matmul(pick, parts, NT)
    first_head = picked[:, 0:1] + picked[:, 2:3] + picked[:, 4:5]
    second_head = picked[:, 1:2] + picked[:, 3:4] + picked[:, 5:6]
    by_head = jnp.where(iota((rows, width), 1) < HEAD_DIM, first_head, second_head)
    key_out[...] = by_head * probe_row * root_scale

    for k in reversed(z_peers):
        pltpu.make_async_copy(zbuf.at[k], zbuf.at[k], zrecv.at[3, k]).wait()
        total = total + zbuf[k]
    value_out[...] = jnp.concatenate([total[:, :128], total[:, 256:272]], axis=1)
    out_out[...] = jnp.concatenate([total[:, 128:256], total[:, 272:288]], axis=1)
    for copy in sent:
        copy.wait_send()


def call(nz, nn, patches, w_key, w_value, w_out, probe, texts):
    vmem = pl.BlockSpec(memory_space=pltpu.VMEM)
    f32, bf16 = jnp.float32, jnp.bfloat16
    group = nn * ROWS
    chunks = group // CHUNK
    width = w_key.shape[1]
    rows = D // nz // QUAD
    slots = chunks * SLOTS
    dma = pltpu.SemaphoreType.DMA
    return pl.pallas_call(
        functools.partial(kernel, nz, nn),
        out_shape=(
            jax.ShapeDtypeStruct((ROWS, 128), f32),
            jax.ShapeDtypeStruct((ROWS, D), f32),
            jax.ShapeDtypeStruct((rows, width), f32),
            jax.ShapeDtypeStruct((rows, width), f32),
            jax.ShapeDtypeStruct((rows, width), f32),
        ),
        in_specs=[pl.BlockSpec(memory_space=pl.ANY)] + [vmem] * 5,
        out_specs=(vmem,) * 5,
        scratch_shapes=[
            pltpu.VMEM((chunks, SPAN, D), bf16),
            pltpu.VMEM((2 * width, D), bf16),
            pltpu.VMEM((2, width, SPAN), bf16),
            pltpu.VMEM((chunks, width, SPAN), bf16),
            pltpu.VMEM((chunks, SLOTS, SPAN), f32),
            pltpu.VMEM((chunks, SLOTS, width), f32),
            pltpu.VMEM((slots, D), f32),
            pltpu.VMEM((nz, D // nz, 4 * slots), bf16),
            pltpu.VMEM((nn, ROWS, D), f32),
            pltpu.VMEM((nn, ROWS, D), f32),
            pltpu.VMEM((QUAD, ROWS, D), f32),
            pltpu.VMEM((nz, QUAD * ROWS, D), bf16),
            pltpu.VMEM((nn, ROWS, D), f32),
            pltpu.VMEM((nn, ROWS, D + 128), f32),
            pltpu.VMEM((nn, ROWS, D + 128), f32),
            pltpu.VMEM((nz, QUAD * ROWS, D), bf16),
            pltpu.VMEM((nz, QUAD * ROWS, D), bf16),
            pltpu.VMEM((QUAD, ROWS, D), f32),
            pltpu.VMEM((QUAD, ROWS, D), f32),
            pltpu.VMEM((nn, ROWS, D), f32),
            pltpu.VMEM((nz, 2, 2, rows, WIDTH), f32),
            pltpu.VMEM((nz, 2, rows, WIDTH), f32),
            pltpu.VMEM((nz, rows, WIDTH), f32),
            pltpu.VMEM((nz, rows, WIDTH), f32),
            pltpu.VMEM((nz, rows, WIDTH), f32),
            pltpu.VMEM((nz, rows, WIDTH), f32),
            pltpu.VMEM((chunks, 2 * SLOTS, width), bf16),
            pltpu.VMEM((2, D), f32),
            pltpu.VMEM((QUAD, 2, D), f32),
            pltpu.VMEM((2, D), f32),
            pltpu.VMEM((nz, 2, D), f32),
            dma((chunks,)),
            dma((4, nn)),
            dma((4, nn)),
            dma((4, nz)),
            dma((4, nz)),
            dma((3, QUAD)),
            dma((3, QUAD)),
            dma((nz,)),
            dma((nz,)),
            dma((nz,)),
            dma((nz,)),
        ],
        compiler_params=pltpu.CompilerParams(
            collective_id=0, has_side_effects=True, vmem_limit_bytes=56 * 1024 * 1024
        ),
    )(patches, w_key, w_value, w_out, probe, texts)


def shards(patches, w_key, w_value, w_out, probe, texts):
    nz = lax.axis_size("wide") // QUAD
    nn = lax.axis_size("narrow")
    flat_rows = patches.reshape(patches.shape[0] * PATCHES, D)
    row_loss, text_grad, grad_key, grad_value, grad_out = call(
        nz, nn, flat_rows, w_key, w_value, w_out, probe.reshape(1, -1), texts
    )
    return (row_loss[:, 0], text_grad, grad_key, grad_value, grad_out.T)


def solution(mesh):
    return jax.shard_map(
        shards,
        mesh=mesh,
        in_specs=(
            P("wide", None, None),
            P(None, "narrow"),
            P(None, "narrow"),
            P("narrow", None),
            P("narrow"),
            P(("wide", "narrow"), None),
        ),
        out_specs=(
            P(("wide", "narrow")),
            P(("wide", "narrow"), None),
            P("wide", "narrow"),
            P("wide", "narrow"),
            P("narrow", "wide"),
        ),
        check_vma=False,
    )
```

```python
import functools
import math

import jax
import jax.numpy as jnp
from jax import lax
from jax.experimental import pallas as pl
from jax.experimental.pallas import tpu as pltpu
from jax.sharding import PartitionSpec as P

D = 1152
HEAD_DIM = 72
PATCHES = 256
QUAD = 4
ROWS = 4
MESH = pl.DeviceIdType.MESH

logit_scale = 16.0
logit_bias = -4.0


def remote(src, dst, send, recv, device):
    copy = pltpu.make_async_remote_copy(
        src_ref=src,
        dst_ref=dst,
        send_sem=send,
        recv_sem=recv,
        device_id=device,
        device_id_type=MESH,
    )
    copy.start()
    return copy


def split_dot(coef, other, dims):
    high = coef.astype(jnp.bfloat16)
    rest = coef - high.astype(jnp.float32)
    mid = rest.astype(jnp.bfloat16)
    low = (rest - mid.astype(jnp.float32)).astype(jnp.bfloat16)
    dot = lambda part: lax.dot_general(part, other, dims, preferred_element_type=jnp.float32)
    return dot(low) + dot(mid) + dot(high)


CHUNK = 4
SPAN = CHUNK * PATCHES
SLOTS = 2 * CHUNK
WIDTH = 384
NT = (((1,), (1,)), ((), ()))
NN = (((1,), (0,)), ((), ()))


def matmul(a, b, dims=NN):
    return lax.dot_general(a, b, dims, preferred_element_type=jnp.float32)


def high_low(values):
    high = values.astype(jnp.bfloat16)
    low = (values - high.astype(jnp.float32)).astype(jnp.bfloat16)
    return high, low


def iota(shape, axis):
    return lax.broadcasted_iota(jnp.int32, shape, axis)


def kernel(
    nz, nn, patches, w_key, w_value, w_out, probe, texts,
    loss_out, text_out, key_out, value_out, out_out,
    held, both_t, out_w, keys, values, weights, heads, pooled_rows, left,
    psrc, rbuf, qbuf, tbuf, ibuf, gsrc, gbuf, usrc, ubuf, vsrc, vbuf, pbuf,
    grads, abuf, xsrc, xbuf, zsrc, zbuf, head_rows, ssum, sbuf, szsum, szbuf,
    loads, nsend, nrecv, zsend, zrecv, qsend, qrecv, asend, arecv, xsend, xrecv,
):
    f32, bf16 = jnp.float32, jnp.bfloat16
    w, n = lax.axis_index("wide"), lax.axis_index("narrow")
    z, q = w // QUAD, lax.rem(w, QUAD)
    x, core = q // 2, lax.rem(q, 2)
    group, span = nn * ROWS, nz * QUAD * ROWS
    chunks = group // CHUNK
    width = w_key.shape[0]
    root_scale = 1.0 / math.sqrt(HEAD_DIM)
    narrow_peers = [lax.rem(n + d, nn) for d in range(1, nn)]
    z_peers = [lax.rem(z + d, nz) for d in range(1, nz)]
    q_peers = [lax.rem(q + d, QUAD) for d in range(1, QUAD)]
    at_n = lambda k: {"wide": w, "narrow": k}
    at_z = lambda k: {"wide": k * QUAD + q, "narrow": n}
    at_q = lambda k: {"wide": z * QUAD + k, "narrow": n}
    sibling = at_q(q + 1 - 2 * core)
    across = at_q(2 * (1 - x) + core)
    order = z_peers + [z]

    barrier = pltpu.get_barrier_semaphore()
    partners = [at_n(k) for k in narrow_peers] + [at_z(k) for k in z_peers] + [at_q(k) for k in q_peers]
    for device in partners:
        pl.semaphore_signal(barrier, inc=1, device_id=device, device_id_type=MESH)
    key_load = pltpu.make_async_copy(w_key, both_t.at[pl.ds(0, width)], loads.at[chunks])
    value_load = pltpu.make_async_copy(w_value, both_t.at[pl.ds(width, width)], loads.at[chunks + 1])
    out_load = pltpu.make_async_copy(w_out, out_w, loads.at[chunks + 2])
    key_load.start()
    value_load.start()
    for j in range(chunks):
        pltpu.make_async_copy(patches.at[pl.ds(j * SPAN, SPAN)], held.at[j], loads.at[j]).start()
    out_load.start()
    sent = []

    def exchange(peers, place, me, src, dst, send, recv):
        copies = [remote(src(k), dst.at[me], send.at[k], recv.at[me], place(k)) for k in peers]
        sent.extend(copies)

    def arrived(peers, buf, recv):
        for k in peers:
            pltpu.make_async_copy(buf.at[k], buf.at[k], recv.at[k]).wait()

    text_float = texts[...].astype(f32)
    text_norm = jnp.sqrt(jnp.sum(text_float * text_float, axis=1, keepdims=True) + 1e-06)
    text_unit = text_float / text_norm
    qbuf[q] = text_unit.astype(bf16).astype(f32)
    pl.semaphore_wait(barrier, len(partners))
    exchange(q_peers, at_q, q, lambda k: qbuf.at[q], qbuf, qsend.at[0], qrecv.at[0])
    slot_head = iota((SLOTS, width), 0) // CHUNK
    lane_head = iota((SLOTS, width), 1) // HEAD_DIM
    probe_row = probe[...].reshape(1, width).astype(f32)
    probe_slots = jnp.where(slot_head == lane_head, probe_row, 0.0).astype(bf16)
    slot_image = iota((SLOTS, SPAN), 0) % CHUNK
    own = slot_image == iota((SLOTS, SPAN), 1) // PATCHES

    def project(j):
        pltpu.make_async_copy(held.at[j], held.at[j], loads.at[j]).wait()
        rows = matmul(both_t[...], held[j], NT).astype(bf16)
        keys[j] = rows[:width]
        values[j] = rows[width:]

    def pool(j):
        scores = matmul(probe_slots, keys[j]) * root_scale
        scores = jnp.where(own, scores, -1e30)
        top = jnp.max(scores, axis=1, keepdims=True)
        shifted = jnp.where(own, jnp.exp(scores - top), 0.0)
        part = shifted / jnp.sum(shifted, axis=1, keepdims=True)
        weights[j] = part
        heads[j] = matmul(part.astype(bf16), values[j], NT)

    key_load.wait()
    value_load.wait()
    project(0)
    arrived(q_peers, qbuf, qrecv.at[0])
    tbuf[z] = jnp.concatenate([qbuf[k] for k in range(QUAD)], axis=0).astype(bf16)
    exchange(z_peers, at_z, z, lambda k: tbuf.at[z], tbuf, zsend.at[0], zrecv.at[0])
    for j in range(1, chunks):
        project(j)
    for j in range(chunks):
        pool(j)

    all_slots = chunks * SLOTS
    slot_of = iota((all_slots, width), 0)
    head_mask = (slot_of % SLOTS) // CHUNK == iota((all_slots, width), 1) // HEAD_DIM
    heads_slots = jnp.where(head_mask, heads[...].reshape(all_slots, width), 0.0).astype(bf16)
    row_of = iota((group, all_slots), 0)
    slot_at = iota((group, all_slots), 1)
    gather = jnp.where(slot_at // SLOTS * CHUNK + slot_at % CHUNK == row_of, 1.0, 0.0).astype(bf16)
    heads_out = matmul(gather, heads_slots).astype(bf16)
    out_load.wait()
    partial = matmul(heads_out, out_w[...])
    for k in range(nn):
        psrc[k] = partial[k * ROWS : (k + 1) * ROWS]
    exchange(narrow_peers, at_n, n, lambda k: psrc.at[k], rbuf, nsend.at[0], nrecv.at[0])

    def pool_rows(first, last):
        for j in range(first, last):
            rows = matmul(weights[j].astype(bf16), held[j])
            pooled_rows[j * SLOTS : (j + 1) * SLOTS] = rows

    half = chunks // 2
    pool_rows(0, half)
    arrived(narrow_peers, rbuf, nrecv.at[0])
    pooled = psrc[n]
    for k in narrow_peers:
        pooled = pooled + rbuf[k]
    pooled_norm = jnp.sqrt(jnp.sum(pooled * pooled, axis=1, keepdims=True) + 1e-06)
    image_unit = pooled / pooled_norm
    ibuf[n] = image_unit.astype(bf16).astype(f32)
    exchange(narrow_peers, at_n, n, lambda k: ibuf.at[n], ibuf, nsend.at[1], nrecv.at[1])
    pool_rows(half, chunks)
    arrived(z_peers, tbuf, zrecv.at[0])
    arrived(narrow_peers, ibuf, nrecv.at[1])

    image_low = jnp.concatenate([ibuf[k] for k in range(nn)], axis=0).astype(bf16)
    text_low = tbuf[...].reshape(span, D)
    logits = logit_scale * matmul(image_low, text_low, NT) + logit_bias
    image_ids = w * group + iota((group, span), 0)
    offsets = iota((group, span), 1)
    text_ids = offsets // ROWS * group + n * ROWS + offsets % ROWS
    signs = jnp.where(image_ids == text_ids, 1.0, -1.0).astype(f32)
    margin = -signs * logits
    small = jnp.exp(-jnp.abs(margin))
    loss_part = jnp.sum(jnp.maximum(margin, 0.0) + jnp.log1p(small), axis=1, keepdims=True)
    coef = -signs * jnp.where(margin >= 0.0, 1.0, small) / (1.0 + small)
    image_part = logit_scale * split_dot(coef, text_low, NN)
    for k in range(nn):
        gsrc[k, :, :D] = image_part[k * ROWS : (k + 1) * ROWS]
        gsrc[k, :, D:] = jnp.broadcast_to(loss_part[k * ROWS : (k + 1) * ROWS], (ROWS, 128))
    exchange(narrow_peers, at_n, n, lambda k: gsrc.at[k], gbuf, nsend.at[2], nrecv.at[2])
    text_part = logit_scale * split_dot(coef.T, image_low, NN)
    usrc[...] = text_part.astype(bf16).reshape(nz, QUAD * ROWS, D)
    exchange(z_peers, at_z, z, lambda k: usrc.at[k], ubuf, zsend.at[1], zrecv.at[1])
    high, low = high_low(pooled_rows[...])
    pooled_t = jnp.concatenate([high, low, high], axis=0).T
    blocks = D // nz
    for k in range(nz):
        left[k, :, : 3 * all_slots] = pooled_t[k * blocks : (k + 1) * blocks]

    arrived(narrow_peers, gbuf, nrecv.at[2])
    both = gsrc[n]
    for k in narrow_peers:
        both = both + gbuf[k]
    diagonal = iota((ROWS, 128), 0) == iota((ROWS, 128), 1)
    losses = jnp.sum(jnp.where(diagonal, both[:, D:], 0.0), axis=0, keepdims=True)
    loss_out[...] = losses[:, :ROWS]
    image_grad = both[:, :D]
    pooled_grad = (
        image_grad - image_unit * jnp.sum(image_unit * image_grad, axis=1, keepdims=True)
    ) / pooled_norm
    pbuf[n] = pooled_grad.astype(bf16).astype(f32)
    exchange(narrow_peers, at_n, n, lambda k: pbuf.at[n], pbuf, nsend.at[3], nrecv.at[3])

    arrived(narrow_peers, pbuf, nrecv.at[3])
    group_float = jnp.concatenate([pbuf[k] for k in range(nn)], axis=0)
    group_grad = group_float.astype(bf16)
    scatter = jnp.where(
        iota((all_slots, group), 0) // SLOTS * CHUNK + iota((all_slots, group), 0) % CHUNK
        == iota((all_slots, group), 1),
        1.0,
        0.0,
    ).astype(bf16)
    slot_grads = matmul(scatter, group_grad).astype(bf16)
    head_grad = jnp.where(head_mask, matmul(slot_grads, out_w[...], NT), 0.0)
    high = head_grad.astype(bf16).astype(f32)
    low = head_grad - high
    none = lambda rows, columns: jnp.zeros((rows, columns), f32)
    spare = 4 * all_slots - 3 * all_slots - group
    turned = jnp.concatenate([group_float, none(spare, D)], axis=0).astype(bf16).T
    for k in range(nz):
        left[k, :, 3 * all_slots :] = turned[k * blocks : (k + 1) * blocks]

    def value_rows(part):
        return jnp.concatenate(
            [part[:, :128], none(all_slots, 128), part[:, 128:], none(all_slots, 112)], axis=1
        )

    heads_float = heads_out.astype(f32)
    out_rows = jnp.concatenate(
        [none(group, 128), heads_float[:, :128], none(group, 16), heads_float[:, 128:], none(group, 96)],
        axis=1,
    )
    right = jnp.concatenate(
        [value_rows(high), value_rows(high), value_rows(low), out_rows, none(spare, WIDTH)], axis=0
    ).astype(bf16)
    rows = blocks // QUAD
    fold = rows // 4
    for k in order:
        block = matmul(left[k], right)
        for there in range(QUAD):
            part = block[there * rows : (there + 1) * rows]
            here = grads.at[k, there % 2, there // 2]
            here[:rows] = part[:, :128]
            here[rows : 2 * rows] = part[:, 128:256]
            pieces = [part[g * fold : (g + 1) * fold, 256:288] for g in range(4)]
            here[2 * rows :] = jnp.concatenate(pieces, axis=1)
        sent.append(remote(grads.at[k, 1 - core], abuf.at[k], asend.at[k], arecv.at[k], sibling))
    for j in range(chunks):
        pair = [high[j * SLOTS : (j + 1) * SLOTS], low[j * SLOTS : (j + 1) * SLOTS]]
        head_rows[j] = jnp.concatenate(pair, axis=0).astype(bf16)

    def forward(k):
        pltpu.make_async_copy(abuf.at[k], abuf.at[k], arecv.at[k]).wait()
        xsrc[k] = grads[k, core, 1 - x] + abuf[k, 1 - x]
        sent.append(remote(xsrc.at[k], xbuf.at[k], xsend.at[k], xrecv.at[k], across))

    score_sum = none(2 * SLOTS, D)
    passed = 0
    for j in range(chunks):
        weight_grad = matmul(head_rows[j], values[j])
        weight_grad = weight_grad[:SLOTS] + weight_grad[SLOTS:]
        part = weights[j]
        inner = jnp.sum(part * weight_grad, axis=1, keepdims=True)
        score_grad = part * (weight_grad - inner)
        top = score_grad.astype(bf16).astype(f32)
        pair = jnp.concatenate([top, score_grad - top], axis=0).astype(bf16)
        score_sum = score_sum + matmul(pair, held[j])
        if j % 2 == 1:
            upto = nz * (j + 1) // chunks
            for k in order[passed:upto]:
                forward(k)
            passed = upto
    per_head = score_sum[:SLOTS] + score_sum[SLOTS:]
    for h in range(2):
        ssum[h : h + 1] = jnp.sum(per_head[h * CHUNK : (h + 1) * CHUNK], axis=0, keepdims=True)
    sbuf[q] = ssum[...]
    exchange(q_peers, at_q, q, lambda k: ssum, sbuf, qsend.at[2], qrecv.at[2])

    arrived(z_peers, ubuf, zrecv.at[1])
    quad_grad = usrc[z].astype(f32)
    for k in z_peers:
        quad_grad = quad_grad + ubuf[k].astype(f32)
    for k in range(QUAD):
        vsrc[k] = quad_grad[k * ROWS : (k + 1) * ROWS]
    exchange(q_peers, at_q, q, lambda k: vsrc.at[k], vbuf, qsend.at[1], qrecv.at[1])

    arrived(q_peers, sbuf, qrecv.at[2])
    szsum[...] = sbuf[0] + sbuf[1] + sbuf[2] + sbuf[3]
    exchange(z_peers, at_z, z, lambda k: szsum, szbuf, zsend.at[2], zrecv.at[2])
    for i, k in enumerate(order):
        pltpu.make_async_copy(xbuf.at[k], xbuf.at[k], xrecv.at[k]).wait()
        total = grads[k, core, x] + abuf[k, x] + xbuf[k]
        if i < nz - 1:
            zsrc[k] = total
            sent.append(remote(zsrc.at[k], zbuf.at[z], zsend.at[3, k], zrecv.at[3, z], at_z(k)))

    arrived(q_peers, vbuf, qrecv.at[1])
    unit_grad = vsrc[q]
    for k in q_peers:
        unit_grad = unit_grad + vbuf[k]
    text_out[...] = (
        unit_grad - text_unit * jnp.sum(text_unit * unit_grad, axis=1, keepdims=True)
    ) / text_norm

    arrived(z_peers, szbuf, zrecv.at[2])
    scores_all = szsum[...]
    for k in z_peers:
        scores_all = scores_all + szbuf[k]
    one = scores_all.astype(bf16).astype(f32)
    two = (scores_all - one).astype(bf16).astype(f32)
    three = scores_all - one - two
    parts = jnp.concatenate([one, two, three, none(2, D)], axis=0).astype(bf16)
    pick = jnp.where(iota((rows, D), 0) + w * rows == iota((rows, D), 1), 1.0, 0.0).astype(bf16)
    picked = matmul(pick, parts, NT)
    first_head = picked[:, 0:1] + picked[:, 2:3] + picked[:, 4:5]
    second_head = picked[:, 1:2] + picked[:, 3:4] + picked[:, 5:6]
    by_head = jnp.where(iota((rows, width), 1) < HEAD_DIM, first_head, second_head)
    key_out[...] = by_head * probe_row * root_scale

    for k in reversed(z_peers):
        pltpu.make_async_copy(zbuf.at[k], zbuf.at[k], zrecv.at[3, k]).wait()
        total = total + zbuf[k]
    rest = total[2 * rows :]
    rest = jnp.concatenate([rest[:, 32 * g : 32 * (g + 1)] for g in range(4)], axis=0)
    value_out[...] = jnp.concatenate([total[:rows], rest[:, :16]], axis=1)
    out_out[...] = jnp.concatenate([total[rows : 2 * rows], rest[:, 16:]], axis=1)
    for copy in sent:
        copy.wait_send()


def finish_kernel(*refs):
    count = len(refs) // 2
    sems = refs[-1]
    copies = [
        pltpu.make_async_copy(refs[k], refs[count + k], sems.at[k]) for k in range(count)
    ]
    for copy in copies:
        copy.start()
    for copy in copies:
        copy.wait()


def finish(*arrays):
    anywhere = pl.BlockSpec(memory_space=pl.ANY)
    return pl.pallas_call(
        finish_kernel,
        out_shape=tuple(jax.ShapeDtypeStruct(a.shape, a.dtype) for a in arrays),
        in_specs=[anywhere] * len(arrays),
        out_specs=(anywhere,) * len(arrays),
        scratch_shapes=[pltpu.SemaphoreType.DMA((len(arrays),))],
        compiler_params=pltpu.CompilerParams(vmem_limit_bytes=60 * 1024 * 1024),
    )(*arrays)


def call(nz, nn, patches, w_key, w_value, w_out, probe, texts):
    vmem = pl.BlockSpec(memory_space=pltpu.VMEM)
    f32, bf16 = jnp.float32, jnp.bfloat16
    group = nn * ROWS
    chunks = group // CHUNK
    width = w_key.shape[0]
    rows = D // nz // QUAD
    slab = 2 * rows + rows // 4
    slots = chunks * SLOTS
    dma = pltpu.SemaphoreType.DMA
    return pl.pallas_call(
        functools.partial(kernel, nz, nn),
        out_shape=(
            jax.ShapeDtypeStruct((1, ROWS), f32),
            jax.ShapeDtypeStruct((ROWS, D), f32),
            jax.ShapeDtypeStruct((rows, width), f32),
            jax.ShapeDtypeStruct((rows, width), f32),
            jax.ShapeDtypeStruct((rows, width), f32),
        ),
        in_specs=[pl.BlockSpec(memory_space=pl.ANY)] * 4 + [vmem] * 2,
        out_specs=(vmem,) * 5,
        scratch_shapes=[
            pltpu.VMEM((chunks, SPAN, D), bf16),
            pltpu.VMEM((2 * width, D), bf16),
            pltpu.VMEM((width, D), bf16),
            pltpu.VMEM((chunks, width, SPAN), bf16),
            pltpu.VMEM((chunks, width, SPAN), bf16),
            pltpu.VMEM((chunks, SLOTS, SPAN), f32),
            pltpu.VMEM((chunks, SLOTS, width), f32),
            pltpu.VMEM((slots, D), f32),
            pltpu.VMEM((nz, D // nz, 4 * slots), bf16),
            pltpu.VMEM((nn, ROWS, D), f32),
            pltpu.VMEM((nn, ROWS, D), f32),
            pltpu.VMEM((QUAD, ROWS, D), f32),
            pltpu.VMEM((nz, QUAD * ROWS, D), bf16),
            pltpu.VMEM((nn, ROWS, D), f32),
            pltpu.VMEM((nn, ROWS, D + 128), f32),
            pltpu.VMEM((nn, ROWS, D + 128), f32),
            pltpu.VMEM((nz, QUAD * ROWS, D), bf16),
            pltpu.VMEM((nz, QUAD * ROWS, D), bf16),
            pltpu.VMEM((QUAD, ROWS, D), f32),
            pltpu.VMEM((QUAD, ROWS, D), f32),
            pltpu.VMEM((nn, ROWS, D), f32),
            pltpu.VMEM((nz, 2, 2, slab, 128), f32),
            pltpu.VMEM((nz, 2, slab, 128), f32),
            pltpu.VMEM((nz, slab, 128), f32),
            pltpu.VMEM((nz, slab, 128), f32),
            pltpu.VMEM((nz, slab, 128), f32),
            pltpu.VMEM((nz, slab, 128), f32),
            pltpu.VMEM((chunks, 2 * SLOTS, width), bf16),
            pltpu.VMEM((2, D), f32),
            pltpu.VMEM((QUAD, 2, D), f32),
            pltpu.VMEM((2, D), f32),
            pltpu.VMEM((nz, 2, D), f32),
            dma((chunks + 3,)),
            dma((4, nn)),
            dma((4, nn)),
            dma((4, nz)),
            dma((4, nz)),
            dma((3, QUAD)),
            dma((3, QUAD)),
            dma((nz,)),
            dma((nz,)),
            dma((nz,)),
            dma((nz,)),
        ],
        compiler_params=pltpu.CompilerParams(
            collective_id=0, has_side_effects=True, vmem_limit_bytes=56 * 1024 * 1024
        ),
    )(patches, w_key, w_value, w_out, probe, texts)


def shards(patches, w_key, w_value, w_out, probe, texts):
    nz = lax.axis_size("wide") // QUAD
    nn = lax.axis_size("narrow")
    flat_rows = patches.reshape(patches.shape[0] * PATCHES, D)
    row_loss, text_grad, grad_key, grad_value, grad_out = call(
        nz, nn, flat_rows, w_key.T, w_value.T, w_out, probe, texts
    )
    row_loss, text_grad, grad_key, grad_value, grad_out = finish(
        row_loss, text_grad, grad_key, grad_value, grad_out
    )
    return (row_loss.reshape(ROWS), text_grad, grad_key, grad_value, grad_out.T)


def solution(mesh):
    return jax.shard_map(
        shards,
        mesh=mesh,
        in_specs=(
            P("wide", None, None),
            P(None, "narrow"),
            P(None, "narrow"),
            P("narrow", None),
            P("narrow"),
            P(("wide", "narrow"), None),
        ),
        out_specs=(
            P(("wide", "narrow")),
            P(("wide", "narrow"), None),
            P("wide", "narrow"),
            P("wide", "narrow"),
            P("narrow", "wide"),
        ),
        check_vma=False,
    )
```

```python
import functools
import math

import jax
import jax.numpy as jnp
from jax import lax
from jax.experimental import pallas as pl
from jax.experimental.pallas import tpu as pltpu
from jax.sharding import PartitionSpec as P

D = 1152
HEAD_DIM = 72
PATCHES = 256
QUAD = 4
ROWS = 4
MESH = pl.DeviceIdType.MESH

logit_scale = 16.0
logit_bias = -4.0


def remote(src, dst, send, recv, device):
    copy = pltpu.make_async_remote_copy(
        src_ref=src,
        dst_ref=dst,
        send_sem=send,
        recv_sem=recv,
        device_id=device,
        device_id_type=MESH,
    )
    copy.start()
    return copy


def split_dot(coef, other, dims):
    high = coef.astype(jnp.bfloat16)
    rest = coef - high.astype(jnp.float32)
    low = rest.astype(jnp.bfloat16)
    dot = lambda part: lax.dot_general(part, other, dims, preferred_element_type=jnp.float32)
    return dot(low) + dot(high)


CHUNK = 4
SPAN = CHUNK * PATCHES
SLOTS = 2 * CHUNK
WIDTH = 384
NT = (((1,), (1,)), ((), ()))
NN = (((1,), (0,)), ((), ()))


def matmul(a, b, dims=NN):
    return lax.dot_general(a, b, dims, preferred_element_type=jnp.float32)


def high_low(values):
    high = values.astype(jnp.bfloat16)
    low = (values - high.astype(jnp.float32)).astype(jnp.bfloat16)
    return high, low


def iota(shape, axis):
    return lax.broadcasted_iota(jnp.int32, shape, axis)


def kernel(
    nz, nn, patches, w_key, w_value, w_out, probe, texts,
    loss_out, text_out, key_out, value_out, out_out,
    held, both_t, out_w, keys, values, weights, heads, pooled_rows, left,
    psrc, rbuf, qbuf, tbuf, ibuf, gsrc, gbuf, usrc, ubuf, vsrc, vbuf, pbuf,
    grads, abuf, xsrc, xbuf, zsrc, zbuf, head_rows, ssum, sbuf, szsum, szbuf,
    loads, nsend, nrecv, zsend, zrecv, qsend, qrecv, asend, arecv, xsend, xrecv,
):
    f32, bf16 = jnp.float32, jnp.bfloat16
    w, n = lax.axis_index("wide"), lax.axis_index("narrow")
    z, q = w // QUAD, lax.rem(w, QUAD)
    x, core = q // 2, lax.rem(q, 2)
    group, span = nn * ROWS, nz * QUAD * ROWS
    chunks = group // CHUNK
    width = w_key.shape[0]
    root_scale = 1.0 / math.sqrt(HEAD_DIM)
    narrow_peers = [lax.rem(n + d, nn) for d in range(1, nn)]
    z_peers = [lax.rem(z + d, nz) for d in range(1, nz)]
    q_peers = [lax.rem(q + d, QUAD) for d in range(1, QUAD)]
    at_n = lambda k: {"wide": w, "narrow": k}
    at_z = lambda k: {"wide": k * QUAD + q, "narrow": n}
    at_q = lambda k: {"wide": z * QUAD + k, "narrow": n}
    sibling = at_q(q + 1 - 2 * core)
    across = at_q(2 * (1 - x) + core)
    order = z_peers + [z]

    barrier = pltpu.get_barrier_semaphore()
    partners = [at_n(k) for k in narrow_peers] + [at_z(k) for k in z_peers] + [at_q(k) for k in q_peers]
    for device in partners:
        pl.semaphore_signal(barrier, inc=1, device_id=device, device_id_type=MESH)
    key_load = pltpu.make_async_copy(w_key, both_t.at[pl.ds(0, width)], loads.at[chunks])
    value_load = pltpu.make_async_copy(w_value, both_t.at[pl.ds(width, width)], loads.at[chunks + 1])
    out_load = pltpu.make_async_copy(w_out, out_w, loads.at[chunks + 2])
    key_load.start()
    value_load.start()
    for j in range(chunks):
        pltpu.make_async_copy(patches.at[pl.ds(j * SPAN, SPAN)], held.at[j], loads.at[j]).start()
    out_load.start()
    sent = []

    def exchange(peers, place, me, src, dst, send, recv):
        copies = [remote(src(k), dst.at[me], send.at[k], recv.at[me], place(k)) for k in peers]
        sent.extend(copies)

    def arrived(peers, buf, recv):
        for k in peers:
            pltpu.make_async_copy(buf.at[k], buf.at[k], recv.at[k]).wait()

    text_float = texts[...].astype(f32)
    text_norm = jnp.sqrt(jnp.sum(text_float * text_float, axis=1, keepdims=True) + 1e-06)
    text_unit = text_float / text_norm
    qbuf[q] = text_unit.astype(bf16).astype(f32)
    pl.semaphore_wait(barrier, len(partners))
    exchange(q_peers, at_q, q, lambda k: qbuf.at[q], qbuf, qsend.at[0], qrecv.at[0])
    slot_head = iota((SLOTS, width), 0) // CHUNK
    lane_head = iota((SLOTS, width), 1) // HEAD_DIM
    probe_row = probe[...].reshape(1, width).astype(f32)
    probe_slots = jnp.where(slot_head == lane_head, probe_row, 0.0).astype(bf16)
    slot_image = iota((SLOTS, SPAN), 0) % CHUNK
    own = slot_image == iota((SLOTS, SPAN), 1) // PATCHES

    def project(j):
        pltpu.make_async_copy(held.at[j], held.at[j], loads.at[j]).wait()
        rows = matmul(both_t[...], held[j], NT).astype(bf16)
        keys[j] = rows[:width]
        values[j] = rows[width:]

    def pool(j):
        scores = matmul(probe_slots, keys[j]) * root_scale
        scores = jnp.where(own, scores, -1e30)
        top = jnp.max(scores, axis=1, keepdims=True)
        shifted = jnp.where(own, jnp.exp(scores - top), 0.0)
        part = shifted / jnp.sum(shifted, axis=1, keepdims=True)
        weights[j] = part
        heads[j] = matmul(part.astype(bf16), values[j], NT)

    key_load.wait()
    value_load.wait()
    project(0)
    arrived(q_peers, qbuf, qrecv.at[0])
    tbuf[z] = jnp.concatenate([qbuf[k] for k in range(QUAD)], axis=0).astype(bf16)
    exchange(z_peers, at_z, z, lambda k: tbuf.at[z], tbuf, zsend.at[0], zrecv.at[0])
    for j in range(1, chunks):
        project(j)
    for j in range(chunks):
        pool(j)

    all_slots = chunks * SLOTS
    slot_of = iota((all_slots, width), 0)
    head_mask = (slot_of % SLOTS) // CHUNK == iota((all_slots, width), 1) // HEAD_DIM
    heads_slots = jnp.where(head_mask, heads[...].reshape(all_slots, width), 0.0).astype(bf16)
    row_of = iota((group, all_slots), 0)
    slot_at = iota((group, all_slots), 1)
    gather = jnp.where(slot_at // SLOTS * CHUNK + slot_at % CHUNK == row_of, 1.0, 0.0).astype(bf16)
    heads_out = matmul(gather, heads_slots).astype(bf16)
    out_load.wait()
    partial = matmul(heads_out, out_w[...])
    for k in range(nn):
        psrc[k] = partial[k * ROWS : (k + 1) * ROWS]
    exchange(narrow_peers, at_n, n, lambda k: psrc.at[k], rbuf, nsend.at[0], nrecv.at[0])

    def pool_rows(first, last):
        for j in range(first, last):
            rows = matmul(weights[j].astype(bf16), held[j])
            pooled_rows[j * SLOTS : (j + 1) * SLOTS] = rows

    half = chunks // 2
    pool_rows(0, half)
    arrived(narrow_peers, rbuf, nrecv.at[0])
    pooled = psrc[n]
    for k in narrow_peers:
        pooled = pooled + rbuf[k]
    pooled_norm = jnp.sqrt(jnp.sum(pooled * pooled, axis=1, keepdims=True) + 1e-06)
    image_unit = pooled / pooled_norm
    ibuf[n] = image_unit.astype(bf16).astype(f32)
    exchange(narrow_peers, at_n, n, lambda k: ibuf.at[n], ibuf, nsend.at[1], nrecv.at[1])
    pool_rows(half, chunks)
    arrived(z_peers, tbuf, zrecv.at[0])
    arrived(narrow_peers, ibuf, nrecv.at[1])

    image_low = jnp.concatenate([ibuf[k] for k in range(nn)], axis=0).astype(bf16)
    text_low = tbuf[...].reshape(span, D)
    logits = logit_scale * matmul(image_low, text_low, NT) + logit_bias
    image_ids = w * group + iota((group, span), 0)
    offsets = iota((group, span), 1)
    text_ids = offsets // ROWS * group + n * ROWS + offsets % ROWS
    signs = jnp.where(image_ids == text_ids, 1.0, -1.0).astype(f32)
    margin = -signs * logits
    small = jnp.exp(-jnp.abs(margin))
    loss_part = jnp.sum(jnp.maximum(margin, 0.0) + jnp.log1p(small), axis=1, keepdims=True)
    coef = -signs * jnp.where(margin >= 0.0, 1.0, small) / (1.0 + small)
    image_part = logit_scale * split_dot(coef, text_low, NN)
    for k in range(nn):
        gsrc[k, :, :D] = image_part[k * ROWS : (k + 1) * ROWS]
        gsrc[k, :, D:] = jnp.broadcast_to(loss_part[k * ROWS : (k + 1) * ROWS], (ROWS, 128))
    exchange(narrow_peers, at_n, n, lambda k: gsrc.at[k], gbuf, nsend.at[2], nrecv.at[2])
    text_part = logit_scale * split_dot(coef.T, image_low, NN)
    usrc[...] = text_part.astype(bf16).reshape(nz, QUAD * ROWS, D)
    exchange(z_peers, at_z, z, lambda k: usrc.at[k], ubuf, zsend.at[1], zrecv.at[1])
    high, low = high_low(pooled_rows[...])
    pooled_t = jnp.concatenate([high, low, high], axis=0).T
    blocks = D // nz
    for k in range(nz):
        left[k, :, : 3 * all_slots] = pooled_t[k * blocks : (k + 1) * blocks]

    arrived(narrow_peers, gbuf, nrecv.at[2])
    both = gsrc[n]
    for k in narrow_peers:
        both = both + gbuf[k]
    diagonal = iota((ROWS, 128), 0) == iota((ROWS, 128), 1)
    losses = jnp.sum(jnp.where(diagonal, both[:, D:], 0.0), axis=0, keepdims=True)
    loss_out[...] = losses[:, :ROWS]
    image_grad = both[:, :D]
    pooled_grad = (
        image_grad - image_unit * jnp.sum(image_unit * image_grad, axis=1, keepdims=True)
    ) / pooled_norm
    pbuf[n] = pooled_grad.astype(bf16).astype(f32)
    exchange(narrow_peers, at_n, n, lambda k: pbuf.at[n], pbuf, nsend.at[3], nrecv.at[3])

    arrived(narrow_peers, pbuf, nrecv.at[3])
    group_float = jnp.concatenate([pbuf[k] for k in range(nn)], axis=0)
    group_grad = group_float.astype(bf16)
    scatter = jnp.where(
        iota((all_slots, group), 0) // SLOTS * CHUNK + iota((all_slots, group), 0) % CHUNK
        == iota((all_slots, group), 1),
        1.0,
        0.0,
    ).astype(bf16)
    slot_grads = matmul(scatter, group_grad).astype(bf16)
    head_grad = jnp.where(head_mask, matmul(slot_grads, out_w[...], NT), 0.0)
    high = head_grad.astype(bf16).astype(f32)
    low = head_grad - high
    none = lambda rows, columns: jnp.zeros((rows, columns), f32)
    spare = 4 * all_slots - 3 * all_slots - group
    turned = jnp.concatenate([group_float, none(spare, D)], axis=0).astype(bf16).T
    for k in range(nz):
        left[k, :, 3 * all_slots :] = turned[k * blocks : (k + 1) * blocks]

    def value_rows(part):
        return jnp.concatenate(
            [part[:, :128], none(all_slots, 128), part[:, 128:], none(all_slots, 112)], axis=1
        )

    heads_float = heads_out.astype(f32)
    out_rows = jnp.concatenate(
        [none(group, 128), heads_float[:, :128], none(group, 16), heads_float[:, 128:], none(group, 96)],
        axis=1,
    )
    right = jnp.concatenate(
        [value_rows(high), value_rows(high), value_rows(low), out_rows, none(spare, WIDTH)], axis=0
    ).astype(bf16)
    rows = blocks // QUAD
    slab = zsrc.shape[1]
    fold = rows // 4
    for k in order:
        block = matmul(left[k], right)
        for there in range(QUAD):
            part = block[there * rows : (there + 1) * rows]
            here = grads.at[k, there % 2, there // 2]
            here[:rows] = part[:, :128]
            here[rows : 2 * rows] = part[:, 128:256]
            pieces = [part[g * fold : (g + 1) * fold, 256:288] for g in range(4)]
            here[2 * rows :] = jnp.concatenate(pieces, axis=1)
        sent.append(remote(grads.at[k, 1 - core], abuf.at[k], asend.at[k], arecv.at[k], sibling))
    for j in range(chunks):
        pair = [high[j * SLOTS : (j + 1) * SLOTS], low[j * SLOTS : (j + 1) * SLOTS]]
        head_rows[j] = jnp.concatenate(pair, axis=0).astype(bf16)

    def forward(k):
        pltpu.make_async_copy(abuf.at[k], abuf.at[k], arecv.at[k]).wait()
        given = grads[k, core, 1 - x] + abuf[k, 1 - x]
        given = jnp.concatenate([given, none(xsrc.shape[1] - slab, 128)], axis=0)
        xsrc[k] = given.astype(bf16)
        sent.append(remote(xsrc.at[k], xbuf.at[k], xsend.at[k], xrecv.at[k], across))

    def onward(i):
        k = order[i]
        pltpu.make_async_copy(xbuf.at[k], xbuf.at[k], xrecv.at[k]).wait()
        total = grads[k, core, x] + abuf[k, x] + xbuf[k].astype(f32)[:slab]
        if i < nz - 1:
            zsrc[k] = total
            sent.append(remote(zsrc.at[k], zbuf.at[z], zsend.at[3, k], zrecv.at[3, z], at_z(k)))
        return total

    score_sum = none(2 * SLOTS, D)
    passed, moved = 0, 0
    for j in range(chunks):
        weight_grad = matmul(head_rows[j], values[j])
        weight_grad = weight_grad[:SLOTS] + weight_grad[SLOTS:]
        part = weights[j]
        inner = jnp.sum(part * weight_grad, axis=1, keepdims=True)
        score_grad = part * (weight_grad - inner)
        top = score_grad.astype(bf16).astype(f32)
        pair = jnp.concatenate([top, score_grad - top], axis=0).astype(bf16)
        score_sum = score_sum + matmul(pair, held[j])
        upto = nz * j // (chunks - 1)
        for k in order[passed:upto]:
            forward(k)
        passed = upto
        while moved < passed - 4:
            onward(moved)
            moved += 1
    per_head = score_sum[:SLOTS] + score_sum[SLOTS:]
    for h in range(2):
        ssum[h : h + 1] = jnp.sum(per_head[h * CHUNK : (h + 1) * CHUNK], axis=0, keepdims=True)
    sbuf[q] = ssum[...]
    exchange(q_peers, at_q, q, lambda k: ssum, sbuf, qsend.at[2], qrecv.at[2])
    while moved < nz:
        total = onward(moved)
        moved += 1

    arrived(z_peers, ubuf, zrecv.at[1])
    quad_grad = usrc[z].astype(f32)
    for k in z_peers:
        quad_grad = quad_grad + ubuf[k].astype(f32)
    for k in range(QUAD):
        vsrc[k] = quad_grad[k * ROWS : (k + 1) * ROWS]
    exchange(q_peers, at_q, q, lambda k: vsrc.at[k], vbuf, qsend.at[1], qrecv.at[1])

    arrived(q_peers, sbuf, qrecv.at[2])
    szsum[...] = sbuf[0] + sbuf[1] + sbuf[2] + sbuf[3]
    exchange(z_peers, at_z, z, lambda k: szsum, szbuf, zsend.at[2], zrecv.at[2])
    arrived(q_peers, vbuf, qrecv.at[1])
    unit_grad = vsrc[q]
    for k in q_peers:
        unit_grad = unit_grad + vbuf[k]
    text_out[...] = (
        unit_grad - text_unit * jnp.sum(text_unit * unit_grad, axis=1, keepdims=True)
    ) / text_norm

    arrived(z_peers, szbuf, zrecv.at[2])
    scores_all = szsum[...]
    for k in z_peers:
        scores_all = scores_all + szbuf[k]
    one = scores_all.astype(bf16).astype(f32)
    two = (scores_all - one).astype(bf16).astype(f32)
    three = scores_all - one - two
    parts = jnp.concatenate([one, two, three, none(2, D)], axis=0).astype(bf16)
    pick = jnp.where(iota((rows, D), 0) + w * rows == iota((rows, D), 1), 1.0, 0.0).astype(bf16)
    picked = matmul(pick, parts, NT)
    first_head = picked[:, 0:1] + picked[:, 2:3] + picked[:, 4:5]
    second_head = picked[:, 1:2] + picked[:, 3:4] + picked[:, 5:6]
    by_head = jnp.where(iota((rows, width), 1) < HEAD_DIM, first_head, second_head)
    key_out[...] = by_head * probe_row * root_scale

    for k in reversed(z_peers):
        pltpu.make_async_copy(zbuf.at[k], zbuf.at[k], zrecv.at[3, k]).wait()
        total = total + zbuf[k]
    rest = total[2 * rows :]
    rest = jnp.concatenate([rest[:, 32 * g : 32 * (g + 1)] for g in range(4)], axis=0)
    value_out[...] = jnp.concatenate([total[:rows], rest[:, :16]], axis=1)
    out_out[...] = jnp.concatenate([total[rows : 2 * rows], rest[:, 16:]], axis=1)
    for copy in sent:
        copy.wait_send()


def finish_kernel(*refs):
    count = len(refs) // 2
    for source, target in zip(refs[:count], refs[count:]):
        target[...] = source[...]


def finish(*arrays):
    vmem = pl.BlockSpec(memory_space=pltpu.VMEM)
    return pl.pallas_call(
        finish_kernel,
        out_shape=tuple(jax.ShapeDtypeStruct(a.shape, a.dtype) for a in arrays),
        in_specs=[vmem] * len(arrays),
        out_specs=(vmem,) * len(arrays),
        compiler_params=pltpu.CompilerParams(vmem_limit_bytes=60 * 1024 * 1024),
    )(*arrays)


def call(nz, nn, patches, w_key, w_value, w_out, probe, texts):
    vmem = pl.BlockSpec(memory_space=pltpu.VMEM)
    f32, bf16 = jnp.float32, jnp.bfloat16
    group = nn * ROWS
    chunks = group // CHUNK
    width = w_key.shape[0]
    rows = D // nz // QUAD
    slab = 2 * rows + rows // 4
    wire = -(-slab // 16) * 16
    slots = chunks * SLOTS
    dma = pltpu.SemaphoreType.DMA
    return pl.pallas_call(
        functools.partial(kernel, nz, nn),
        out_shape=(
            jax.ShapeDtypeStruct((1, ROWS), f32),
            jax.ShapeDtypeStruct((ROWS, D), f32),
            jax.ShapeDtypeStruct((rows, width), f32),
            jax.ShapeDtypeStruct((rows, width), f32),
            jax.ShapeDtypeStruct((rows, width), f32),
        ),
        in_specs=[pl.BlockSpec(memory_space=pl.ANY)] * 4 + [vmem] * 2,
        out_specs=(vmem,) * 5,
        scratch_shapes=[
            pltpu.VMEM((chunks, SPAN, D), bf16),
            pltpu.VMEM((2 * width, D), bf16),
            pltpu.VMEM((width, D), bf16),
            pltpu.VMEM((chunks, width, SPAN), bf16),
            pltpu.VMEM((chunks, width, SPAN), bf16),
            pltpu.VMEM((chunks, SLOTS, SPAN), f32),
            pltpu.VMEM((chunks, SLOTS, width), f32),
            pltpu.VMEM((slots, D), f32),
            pltpu.VMEM((nz, D // nz, 4 * slots), bf16),
            pltpu.VMEM((nn, ROWS, D), f32),
            pltpu.VMEM((nn, ROWS, D), f32),
            pltpu.VMEM((QUAD, ROWS, D), f32),
            pltpu.VMEM((nz, QUAD * ROWS, D), bf16),
            pltpu.VMEM((nn, ROWS, D), f32),
            pltpu.VMEM((nn, ROWS, D + 128), f32),
            pltpu.VMEM((nn, ROWS, D + 128), f32),
            pltpu.VMEM((nz, QUAD * ROWS, D), bf16),
            pltpu.VMEM((nz, QUAD * ROWS, D), bf16),
            pltpu.VMEM((QUAD, ROWS, D), f32),
            pltpu.VMEM((QUAD, ROWS, D), f32),
            pltpu.VMEM((nn, ROWS, D), f32),
            pltpu.VMEM((nz, 2, 2, slab, 128), f32),
            pltpu.VMEM((nz, 2, slab, 128), f32),
            pltpu.VMEM((nz, wire, 128), bf16),
            pltpu.VMEM((nz, wire, 128), bf16),
            pltpu.VMEM((nz, slab, 128), f32),
            pltpu.VMEM((nz, slab, 128), f32),
            pltpu.VMEM((chunks, 2 * SLOTS, width), bf16),
            pltpu.VMEM((2, D), f32),
            pltpu.VMEM((QUAD, 2, D), f32),
            pltpu.VMEM((2, D), f32),
            pltpu.VMEM((nz, 2, D), f32),
            dma((chunks + 3,)),
            dma((4, nn)),
            dma((4, nn)),
            dma((4, nz)),
            dma((4, nz)),
            dma((3, QUAD)),
            dma((3, QUAD)),
            dma((nz,)),
            dma((nz,)),
            dma((nz,)),
            dma((nz,)),
        ],
        compiler_params=pltpu.CompilerParams(
            collective_id=0, has_side_effects=True, vmem_limit_bytes=56 * 1024 * 1024
        ),
    )(patches, w_key, w_value, w_out, probe, texts)


def shards(patches, w_key, w_value, w_out, probe, texts):
    nz = lax.axis_size("wide") // QUAD
    nn = lax.axis_size("narrow")
    flat_rows = patches.reshape(patches.shape[0] * PATCHES, D)
    row_loss, text_grad, grad_key, grad_value, grad_out = call(
        nz, nn, flat_rows, w_key.T, w_value.T, w_out, probe, texts
    )
    row_loss, text_grad, grad_key, grad_value, grad_out = finish(
        row_loss, text_grad, grad_key, grad_value, grad_out
    )
    return (row_loss.reshape(ROWS), text_grad, grad_key, grad_value, grad_out.T)


def solution(mesh):
    return jax.shard_map(
        shards,
        mesh=mesh,
        in_specs=(
            P("wide", None, None),
            P(None, "narrow"),
            P(None, "narrow"),
            P("narrow", None),
            P("narrow"),
            P(("wide", "narrow"), None),
        ),
        out_specs=(
            P(("wide", "narrow")),
            P(("wide", "narrow"), None),
            P("wide", "narrow"),
            P("wide", "narrow"),
            P("narrow", "wide"),
        ),
        check_vma=False,
    )
```

```python
import functools
import math

import jax
import jax.numpy as jnp
from jax import lax
from jax.experimental import pallas as pl
from jax.experimental.pallas import tpu as pltpu
from jax.sharding import PartitionSpec as P

D = 1152
HEAD_DIM = 72
PATCHES = 256
QUAD = 4
ROWS = 4
MESH = pl.DeviceIdType.MESH

logit_scale = 16.0
logit_bias = -4.0


def remote(src, dst, send, recv, device):
    copy = pltpu.make_async_remote_copy(
        src_ref=src,
        dst_ref=dst,
        send_sem=send,
        recv_sem=recv,
        device_id=device,
        device_id_type=MESH,
    )
    copy.start()
    return copy


def split_dot(coef, other, dims):
    high = coef.astype(jnp.bfloat16)
    rest = coef - high.astype(jnp.float32)
    low = rest.astype(jnp.bfloat16)
    dot = lambda part: lax.dot_general(part, other, dims, preferred_element_type=jnp.float32)
    return dot(low) + dot(high)


CHUNK = 4
SPAN = CHUNK * PATCHES
SLOTS = 2 * CHUNK
WIDTH = 384
NT = (((1,), (1,)), ((), ()))
NN = (((1,), (0,)), ((), ()))


def matmul(a, b, dims=NN):
    return lax.dot_general(a, b, dims, preferred_element_type=jnp.float32)


def high_low(values):
    high = values.astype(jnp.bfloat16)
    low = (values - high.astype(jnp.float32)).astype(jnp.bfloat16)
    return high, low


def iota(shape, axis):
    return lax.broadcasted_iota(jnp.int32, shape, axis)


def kernel(
    nz, nn, patches, w_key, w_value, w_out, probe, texts,
    loss_out, text_out, key_out, value_out, out_out,
    held, both_t, out_w, keys, values, weights, heads, pooled_rows, left,
    psrc, rbuf, qbuf, tbuf, ibuf, gsrc, gbuf, usrc, ubuf, vsrc, vbuf, pbuf,
    grads, abuf, xsrc, xbuf, zsrc, zbuf, osrc, obuf, pick, head_rows, ssum, sbuf, szsum, szbuf,
    loads, nsend, nrecv, zsend, zrecv, qsend, qrecv, asend, arecv, xsend, xrecv,
):
    f32, bf16 = jnp.float32, jnp.bfloat16
    w, n = lax.axis_index("wide"), lax.axis_index("narrow")
    z, q = w // QUAD, lax.rem(w, QUAD)
    x, core = q // 2, lax.rem(q, 2)
    group, span = nn * ROWS, nz * QUAD * ROWS
    chunks = group // CHUNK
    width = w_key.shape[0]
    root_scale = 1.0 / math.sqrt(HEAD_DIM)
    narrow_peers = [lax.rem(n + d, nn) for d in range(1, nn)]
    z_peers = [lax.rem(z + d, nz) for d in range(1, nz)]
    q_peers = [lax.rem(q + d, QUAD) for d in range(1, QUAD)]
    at_n = lambda k: {"wide": w, "narrow": k}
    at_z = lambda k: {"wide": k * QUAD + q, "narrow": n}
    at_q = lambda k: {"wide": z * QUAD + k, "narrow": n}
    sibling = at_q(q + 1 - 2 * core)
    across = at_q(2 * (1 - x) + core)
    order = z_peers + [z]

    barrier = pltpu.get_barrier_semaphore()
    partners = [at_n(k) for k in narrow_peers] + [at_z(k) for k in z_peers] + [at_q(k) for k in q_peers]
    for device in partners:
        pl.semaphore_signal(barrier, inc=1, device_id=device, device_id_type=MESH)
    key_load = pltpu.make_async_copy(w_key, both_t.at[pl.ds(0, width)], loads.at[chunks])
    value_load = pltpu.make_async_copy(w_value, both_t.at[pl.ds(width, width)], loads.at[chunks + 1])
    out_load = pltpu.make_async_copy(w_out, out_w, loads.at[chunks + 2])
    key_load.start()
    value_load.start()
    for j in range(chunks):
        pltpu.make_async_copy(patches.at[pl.ds(j * SPAN, SPAN)], held.at[j], loads.at[j]).start()
    out_load.start()
    sent = []

    def exchange(peers, place, me, src, dst, send, recv):
        copies = [remote(src(k), dst.at[me], send.at[k], recv.at[me], place(k)) for k in peers]
        sent.extend(copies)

    def arrived(peers, buf, recv):
        for k in peers:
            pltpu.make_async_copy(buf.at[k], buf.at[k], recv.at[k]).wait()

    text_float = texts[...].astype(f32)
    text_norm = jnp.sqrt(jnp.sum(text_float * text_float, axis=1, keepdims=True) + 1e-06)
    text_unit = text_float / text_norm
    qbuf[q] = text_unit.astype(bf16).astype(f32)
    pl.semaphore_wait(barrier, len(partners))
    exchange(q_peers, at_q, q, lambda k: qbuf.at[q], qbuf, qsend.at[0], qrecv.at[0])
    slot_head = iota((SLOTS, width), 0) // CHUNK
    lane_head = iota((SLOTS, width), 1) // HEAD_DIM
    probe_row = probe[...].reshape(1, width).astype(f32)
    probe_slots = jnp.where(slot_head == lane_head, probe_row, 0.0).astype(bf16)
    slot_image = iota((SLOTS, SPAN), 0) % CHUNK
    own = slot_image == iota((SLOTS, SPAN), 1) // PATCHES

    def project(j):
        pltpu.make_async_copy(held.at[j], held.at[j], loads.at[j]).wait()
        rows = matmul(both_t[...], held[j], NT).astype(bf16)
        keys[j] = rows[:width]
        values[j] = rows[width:]

    def pool(j):
        scores = matmul(probe_slots, keys[j]) * root_scale
        scores = jnp.where(own, scores, -1e30)
        top = jnp.max(scores, axis=1, keepdims=True)
        shifted = jnp.where(own, jnp.exp(scores - top), 0.0)
        part = shifted / jnp.sum(shifted, axis=1, keepdims=True)
        weights[j] = part
        heads[j] = matmul(part.astype(bf16), values[j], NT)

    key_load.wait()
    value_load.wait()
    for j in range(chunks):
        project(j)
        if j == 1:
            arrived(q_peers, qbuf, qrecv.at[0])
            tbuf[z] = jnp.concatenate([qbuf[k] for k in range(QUAD)], axis=0).astype(bf16)
            exchange(z_peers, at_z, z, lambda k: tbuf.at[z], tbuf, zsend.at[0], zrecv.at[0])
    for j in range(chunks):
        pool(j)

    all_slots = chunks * SLOTS
    slot_of = iota((all_slots, width), 0)
    head_mask = (slot_of % SLOTS) // CHUNK == iota((all_slots, width), 1) // HEAD_DIM
    heads_slots = jnp.where(head_mask, heads[...].reshape(all_slots, width), 0.0).astype(bf16)
    row_of = iota((group, all_slots), 0)
    slot_at = iota((group, all_slots), 1)
    gather = jnp.where(slot_at // SLOTS * CHUNK + slot_at % CHUNK == row_of, 1.0, 0.0).astype(bf16)
    heads_out = matmul(gather, heads_slots).astype(bf16)
    out_load.wait()
    partial = matmul(heads_out, out_w[...])
    for k in range(nn):
        psrc[k] = partial[k * ROWS : (k + 1) * ROWS]
    exchange(narrow_peers, at_n, n, lambda k: psrc.at[k], rbuf, nsend.at[0], nrecv.at[0])

    def pool_rows(first, last):
        for j in range(first, last):
            rows = matmul(weights[j].astype(bf16), held[j])
            pooled_rows[j * SLOTS : (j + 1) * SLOTS] = rows

    half = chunks // 2
    pool_rows(0, half)
    each = D // (nz * QUAD)
    for k in range(nz):
        lane = iota((D, 128), 1)
        chosen = (iota((D, 128), 0) == (k * QUAD + q) * each + lane) & (lane < each)
        pick[:, k * 128 : (k + 1) * 128] = jnp.where(chosen, 1.0, 0.0).astype(bf16)
    arrived(narrow_peers, rbuf, nrecv.at[0])
    pooled = psrc[n]
    for k in narrow_peers:
        pooled = pooled + rbuf[k]
    pooled_norm = jnp.sqrt(jnp.sum(pooled * pooled, axis=1, keepdims=True) + 1e-06)
    image_unit = pooled / pooled_norm
    ibuf[n] = image_unit.astype(bf16).astype(f32)
    exchange(narrow_peers, at_n, n, lambda k: ibuf.at[n], ibuf, nsend.at[1], nrecv.at[1])
    pool_rows(half, chunks)
    arrived(z_peers, tbuf, zrecv.at[0])
    arrived(narrow_peers, ibuf, nrecv.at[1])

    image_low = jnp.concatenate([ibuf[k] for k in range(nn)], axis=0).astype(bf16)
    text_low = tbuf[...].reshape(span, D)
    logits = logit_scale * matmul(image_low, text_low, NT) + logit_bias
    image_ids = w * group + iota((group, span), 0)
    offsets = iota((group, span), 1)
    text_ids = offsets // ROWS * group + n * ROWS + offsets % ROWS
    signs = jnp.where(image_ids == text_ids, 1.0, -1.0).astype(f32)
    margin = -signs * logits
    small = jnp.exp(-jnp.abs(margin))
    loss_part = jnp.sum(jnp.maximum(margin, 0.0) + jnp.log1p(small), axis=1, keepdims=True)
    coef = -signs * jnp.where(margin >= 0.0, 1.0, small) / (1.0 + small)
    image_part = logit_scale * split_dot(coef, text_low, NN)
    for k in range(nn):
        gsrc[k, :, :D] = image_part[k * ROWS : (k + 1) * ROWS]
        gsrc[k, :, D:] = jnp.broadcast_to(loss_part[k * ROWS : (k + 1) * ROWS], (ROWS, 128))
    exchange(narrow_peers, at_n, n, lambda k: gsrc.at[k], gbuf, nsend.at[2], nrecv.at[2])
    text_part = logit_scale * split_dot(coef.T, image_low, NN)
    usrc[...] = text_part.astype(bf16).reshape(nz, QUAD * ROWS, D)
    exchange(z_peers, at_z, z, lambda k: usrc.at[k], ubuf, zsend.at[1], zrecv.at[1])
    high, low = high_low(pooled_rows[...])
    pooled_t = jnp.concatenate([high, low, high], axis=0).T
    blocks = D // nz
    for k in range(nz):
        left[k, :, : 3 * all_slots] = pooled_t[k * blocks : (k + 1) * blocks]

    arrived(narrow_peers, gbuf, nrecv.at[2])
    both = gsrc[n]
    for k in narrow_peers:
        both = both + gbuf[k]
    diagonal = iota((ROWS, 128), 0) == iota((ROWS, 128), 1)
    losses = jnp.sum(jnp.where(diagonal, both[:, D:], 0.0), axis=0, keepdims=True)
    loss_out[...] = losses[:, :ROWS]
    image_grad = both[:, :D]
    pooled_grad = (
        image_grad - image_unit * jnp.sum(image_unit * image_grad, axis=1, keepdims=True)
    ) / pooled_norm
    pbuf[n] = pooled_grad.astype(bf16).astype(f32)
    exchange(narrow_peers, at_n, n, lambda k: pbuf.at[n], pbuf, nsend.at[3], nrecv.at[3])

    arrived(narrow_peers, pbuf, nrecv.at[3])
    group_float = jnp.concatenate([pbuf[k] for k in range(nn)], axis=0)
    group_grad = group_float.astype(bf16)
    scatter = jnp.where(
        iota((all_slots, group), 0) // SLOTS * CHUNK + iota((all_slots, group), 0) % CHUNK
        == iota((all_slots, group), 1),
        1.0,
        0.0,
    ).astype(bf16)
    slot_grads = matmul(scatter, group_grad).astype(bf16)
    head_grad = jnp.where(head_mask, matmul(slot_grads, out_w[...], NT), 0.0)
    high = head_grad.astype(bf16).astype(f32)
    low = head_grad - high
    none = lambda rows, columns: jnp.zeros((rows, columns), f32)
    spare = 4 * all_slots - 3 * all_slots - group
    turned = jnp.concatenate([group_float, none(spare, D)], axis=0).astype(bf16).T
    for k in range(nz):
        left[k, :, 3 * all_slots :] = turned[k * blocks : (k + 1) * blocks]

    def value_rows(part):
        return jnp.concatenate(
            [part[:, :128], none(all_slots, 128), part[:, 128:], none(all_slots, 112)], axis=1
        )

    heads_float = heads_out.astype(f32)
    out_rows = jnp.concatenate(
        [none(group, 128), heads_float[:, :128], none(group, 16), heads_float[:, 128:], none(group, 96)],
        axis=1,
    )
    right = jnp.concatenate(
        [value_rows(high), value_rows(high), value_rows(low), out_rows, none(spare, WIDTH)], axis=0
    ).astype(bf16)
    rows = blocks // QUAD
    wide = zsrc.shape[1]
    slab = wide + rows
    fold = rows // 4
    def block_out(k):
        block = matmul(left[k], right)
        for there in range(QUAD):
            part = block[there * rows : (there + 1) * rows]
            here = grads.at[k, there % 2, there // 2]
            here[:rows] = part[:, :128]
            pieces = [part[g * fold : (g + 1) * fold, 256:288] for g in range(4)]
            pieces = jnp.concatenate(pieces, axis=1)
            here[rows:wide] = jnp.concatenate([pieces, none(wide - rows - fold, 128)], axis=0)
            here[wide:] = part[:, 128:256]
        sent.append(remote(grads.at[k, 1 - core], abuf.at[k], asend.at[k], arecv.at[k], sibling))

    def forward(k):
        pltpu.make_async_copy(abuf.at[k], abuf.at[k], arecv.at[k]).wait()
        given = grads[k, core, 1 - x] + abuf[k, 1 - x]
        given = jnp.concatenate([given, none(2 * wide - slab, 128)], axis=0)
        xsrc[k] = given.astype(bf16)
        sent.append(remote(xsrc.at[k], xbuf.at[k], xsend.at[k], xrecv.at[k], across))

    def onward(i):
        k = order[i]
        pltpu.make_async_copy(xbuf.at[k], xbuf.at[k], xrecv.at[k]).wait()
        total = grads[k, core, x] + abuf[k, x] + xbuf[k].astype(f32)[:slab]
        if i < nz - 1:
            zsrc[k] = total[:wide]
            sent.append(remote(zsrc.at[k], zbuf.at[z], zsend.at[3, k], zrecv.at[3, z], at_z(k)))
            osrc[k] = jnp.concatenate([total[wide:], none(2 * wide - slab, 128)], axis=0).astype(bf16)
            sent.append(remote(osrc.at[k], obuf.at[z], zsend.at[4, k], zrecv.at[4, z], at_z(k)))
        return total

    for i in range(nz):
        block_out(order[i])
        if i > 1:
            forward(order[i - 2])
    for j in range(chunks):
        pair = [high[j * SLOTS : (j + 1) * SLOTS], low[j * SLOTS : (j + 1) * SLOTS]]
        head_rows[j] = jnp.concatenate(pair, axis=0).astype(bf16)
    forward(order[nz - 2])
    forward(order[nz - 1])

    def three_parts(values):
        one = values.astype(bf16).astype(f32)
        two = (values - one).astype(bf16).astype(f32)
        return jnp.concatenate([one, two, values - one - two, jnp.zeros_like(one)], axis=0).astype(bf16)

    score_sum = none(2 * SLOTS, D)
    moved = 0
    for j in range(chunks):
        weight_grad = matmul(head_rows[j], values[j])
        weight_grad = weight_grad[:SLOTS] + weight_grad[SLOTS:]
        part = weights[j]
        inner = jnp.sum(part * weight_grad, axis=1, keepdims=True)
        score_grad = part * (weight_grad - inner)
        top = score_grad.astype(bf16).astype(f32)
        pair = jnp.concatenate([top, score_grad - top], axis=0).astype(bf16)
        score_sum = score_sum + matmul(pair, held[j])
        if j > 0:
            while moved < nz * j // chunks:
                total = onward(moved)
                moved += 1
    per_head = score_sum[:SLOTS] + score_sum[SLOTS:]
    for h in range(2):
        ssum[h : h + 1] = jnp.sum(per_head[h * CHUNK : (h + 1) * CHUNK], axis=0, keepdims=True)
    sbuf[q] = ssum[...]
    exchange(q_peers, at_q, q, lambda k: ssum, sbuf, qsend.at[2], qrecv.at[2])
    while moved < nz:
        total = onward(moved)
        moved += 1

    arrived(z_peers, ubuf, zrecv.at[1])
    quad_grad = usrc[z].astype(f32)
    for k in z_peers:
        quad_grad = quad_grad + ubuf[k].astype(f32)
    for k in range(QUAD):
        vsrc[k] = quad_grad[k * ROWS : (k + 1) * ROWS]
    exchange(q_peers, at_q, q, lambda k: vsrc.at[k], vbuf, qsend.at[1], qrecv.at[1])

    arrived(q_peers, sbuf, qrecv.at[2])
    scores_all = sbuf[0] + sbuf[1] + sbuf[2] + sbuf[3]
    picked = matmul(three_parts(scores_all), pick[...])
    for k in range(nz):
        mine = picked[:, k * 128 : (k + 1) * 128]
        szsum[k] = mine[0:2] + mine[2:4] + mine[4:6]
    exchange(z_peers, at_z, z, lambda k: szsum.at[k], szbuf, zsend.at[2], zrecv.at[2])
    arrived(q_peers, vbuf, qrecv.at[1])
    unit_grad = vsrc[q]
    for k in q_peers:
        unit_grad = unit_grad + vbuf[k]
    text_out[...] = (
        unit_grad - text_unit * jnp.sum(text_unit * unit_grad, axis=1, keepdims=True)
    ) / text_norm

    arrived(z_peers, szbuf, zrecv.at[2])
    scores_all = szsum[z]
    for k in z_peers:
        scores_all = scores_all + szbuf[k]
    spread = jnp.where(
        (iota((8, width), 0) % 2 == iota((8, width), 1) // HEAD_DIM) & (iota((8, width), 0) < 6), probe_row, 0.0
    ).astype(bf16)
    keyed = matmul(three_parts(scores_all), spread, (((0,), (0,)), ((), ())))
    key_out[...] = keyed[:rows] * root_scale

    value_total, out_total = total[:wide], total[wide:]
    for k in reversed(z_peers):
        pltpu.make_async_copy(zbuf.at[k], zbuf.at[k], zrecv.at[3, k]).wait()
        value_total = value_total + zbuf[k]
        pltpu.make_async_copy(obuf.at[k], obuf.at[k], zrecv.at[4, k]).wait()
        out_total = out_total + obuf[k].astype(f32)[:rows]
    rest = value_total[rows : rows + fold]
    rest = jnp.concatenate([rest[:, 32 * g : 32 * (g + 1)] for g in range(4)], axis=0)
    value_out[...] = jnp.concatenate([value_total[:rows], rest[:, :16]], axis=1)
    out_out[...] = jnp.concatenate([out_total, rest[:, 16:]], axis=1)
    for copy in sent:
        copy.wait_send()


def finish_kernel(*refs):
    count = len(refs) // 2
    for source, target in zip(refs[:count], refs[count:]):
        target[...] = source[...]


def finish(*arrays):
    vmem = pl.BlockSpec(memory_space=pltpu.VMEM)
    return pl.pallas_call(
        finish_kernel,
        out_shape=tuple(jax.ShapeDtypeStruct(a.shape, a.dtype) for a in arrays),
        in_specs=[vmem] * len(arrays),
        out_specs=(vmem,) * len(arrays),
        compiler_params=pltpu.CompilerParams(vmem_limit_bytes=60 * 1024 * 1024),
    )(*arrays)


def call(nz, nn, patches, w_key, w_value, w_out, probe, texts):
    vmem = pl.BlockSpec(memory_space=pltpu.VMEM)
    f32, bf16 = jnp.float32, jnp.bfloat16
    group = nn * ROWS
    chunks = group // CHUNK
    width = w_key.shape[0]
    rows = D // nz // QUAD
    part = -(-(rows + rows // 4) // 16) * 16
    slab = part + rows
    slots = chunks * SLOTS
    dma = pltpu.SemaphoreType.DMA
    return pl.pallas_call(
        functools.partial(kernel, nz, nn),
        out_shape=(
            jax.ShapeDtypeStruct((1, ROWS), f32),
            jax.ShapeDtypeStruct((ROWS, D), f32),
            jax.ShapeDtypeStruct((rows, width), f32),
            jax.ShapeDtypeStruct((rows, width), f32),
            jax.ShapeDtypeStruct((rows, width), f32),
        ),
        in_specs=[pl.BlockSpec(memory_space=pl.ANY)] * 4 + [vmem] * 2,
        out_specs=(vmem,) * 5,
        scratch_shapes=[
            pltpu.VMEM((chunks, SPAN, D), bf16),
            pltpu.VMEM((2 * width, D), bf16),
            pltpu.VMEM((width, D), bf16),
            pltpu.VMEM((chunks, width, SPAN), bf16),
            pltpu.VMEM((chunks, width, SPAN), bf16),
            pltpu.VMEM((chunks, SLOTS, SPAN), f32),
            pltpu.VMEM((chunks, SLOTS, width), f32),
            pltpu.VMEM((slots, D), f32),
            pltpu.VMEM((nz, D // nz, 4 * slots), bf16),
            pltpu.VMEM((nn, ROWS, D), f32),
            pltpu.VMEM((nn, ROWS, D), f32),
            pltpu.VMEM((QUAD, ROWS, D), f32),
            pltpu.VMEM((nz, QUAD * ROWS, D), bf16),
            pltpu.VMEM((nn, ROWS, D), f32),
            pltpu.VMEM((nn, ROWS, D + 128), f32),
            pltpu.VMEM((nn, ROWS, D + 128), f32),
            pltpu.VMEM((nz, QUAD * ROWS, D), bf16),
            pltpu.VMEM((nz, QUAD * ROWS, D), bf16),
            pltpu.VMEM((QUAD, ROWS, D), f32),
            pltpu.VMEM((QUAD, ROWS, D), f32),
            pltpu.VMEM((nn, ROWS, D), f32),
            pltpu.VMEM((nz, 2, 2, slab, 128), f32),
            pltpu.VMEM((nz, 2, slab, 128), f32),
            pltpu.VMEM((nz, 2 * part, 128), bf16),
            pltpu.VMEM((nz, 2 * part, 128), bf16),
            pltpu.VMEM((nz, part, 128), f32),
            pltpu.VMEM((nz, part, 128), f32),
            pltpu.VMEM((nz, part, 128), bf16),
            pltpu.VMEM((nz, part, 128), bf16),
            pltpu.VMEM((D, nz * 128), bf16),
            pltpu.VMEM((chunks, 2 * SLOTS, width), bf16),
            pltpu.VMEM((2, D), f32),
            pltpu.VMEM((QUAD, 2, D), f32),
            pltpu.VMEM((nz, 2, 128), f32),
            pltpu.VMEM((nz, 2, 128), f32),
            dma((chunks + 3,)),
            dma((4, nn)),
            dma((4, nn)),
            dma((5, nz)),
            dma((5, nz)),
            dma((3, QUAD)),
            dma((3, QUAD)),
            dma((nz,)),
            dma((nz,)),
            dma((nz,)),
            dma((nz,)),
        ],
        compiler_params=pltpu.CompilerParams(
            collective_id=0, has_side_effects=True, vmem_limit_bytes=56 * 1024 * 1024
        ),
    )(patches, w_key, w_value, w_out, probe, texts)


def shards(patches, w_key, w_value, w_out, probe, texts):
    nz = lax.axis_size("wide") // QUAD
    nn = lax.axis_size("narrow")
    flat_rows = patches.reshape(patches.shape[0] * PATCHES, D)
    row_loss, text_grad, grad_key, grad_value, grad_out = call(
        nz, nn, flat_rows, w_key.T, w_value.T, w_out, probe, texts
    )
    row_loss, text_grad, grad_key, grad_value, grad_out = finish(
        row_loss, text_grad, grad_key, grad_value, grad_out
    )
    return (row_loss.reshape(ROWS), text_grad, grad_key, grad_value, grad_out.T)


def solution(mesh):
    return jax.shard_map(
        shards,
        mesh=mesh,
        in_specs=(
            P("wide", None, None),
            P(None, "narrow"),
            P(None, "narrow"),
            P("narrow", None),
            P("narrow"),
            P(("wide", "narrow"), None),
        ),
        out_specs=(
            P(("wide", "narrow")),
            P(("wide", "narrow"), None),
            P("wide", "narrow"),
            P("wide", "narrow"),
            P("narrow", "wide"),
        ),
        check_vma=False,
    )
```

```python
import functools
import math

import jax
import jax.numpy as jnp
from jax import lax
from jax.experimental import pallas as pl
from jax.experimental.pallas import tpu as pltpu
from jax.sharding import PartitionSpec as P

D = 1152
HEAD_DIM = 72
PATCHES = 256
QUAD = 4
ROWS = 4
MESH = pl.DeviceIdType.MESH

logit_scale = 16.0
logit_bias = -4.0


def remote(src, dst, send, recv, device):
    copy = pltpu.make_async_remote_copy(
        src_ref=src,
        dst_ref=dst,
        send_sem=send,
        recv_sem=recv,
        device_id=device,
        device_id_type=MESH,
    )
    copy.start()
    return copy


def split_dot(coef, other, dims):
    high = coef.astype(jnp.bfloat16)
    rest = coef - high.astype(jnp.float32)
    low = rest.astype(jnp.bfloat16)
    dot = lambda part: lax.dot_general(part, other, dims, preferred_element_type=jnp.float32)
    return dot(low) + dot(high)


CHUNK = 4
SPAN = CHUNK * PATCHES
SLOTS = 2 * CHUNK
WIDTH = 384
NT = (((1,), (1,)), ((), ()))
NN = (((1,), (0,)), ((), ()))


def matmul(a, b, dims=NN):
    return lax.dot_general(a, b, dims, preferred_element_type=jnp.float32)


def high_low(values):
    high = values.astype(jnp.bfloat16)
    low = (values - high.astype(jnp.float32)).astype(jnp.bfloat16)
    return high, low


def iota(shape, axis):
    return lax.broadcasted_iota(jnp.int32, shape, axis)


def kernel(
    nz, nn, patches, w_key, w_value, w_out, probe, texts,
    loss_out, text_out, key_out, value_out, out_out,
    held, both_t, out_w, keys, values, weights, heads, pooled_rows, left,
    psrc, rbuf, qbuf, tbuf, ibuf, gsrc, gbuf, usrc, ubuf, vsrc, vbuf, pbuf,
    grads, abuf, xsrc, xbuf, zsrc, zbuf, osrc, obuf, pick, head_rows, ssum, sbuf, szsum, szbuf,
    loads, nsend, nrecv, zsend, zrecv, qsend, qrecv, asend, arecv, xsend, xrecv,
):
    f32, bf16 = jnp.float32, jnp.bfloat16
    w, n = lax.axis_index("wide"), lax.axis_index("narrow")
    z, q = w // QUAD, lax.rem(w, QUAD)
    x, core = q // 2, lax.rem(q, 2)
    group, span = nn * ROWS, nz * QUAD * ROWS
    chunks = group // CHUNK
    width = w_key.shape[0]
    root_scale = 1.0 / math.sqrt(HEAD_DIM)
    narrow_peers = [lax.rem(n + d, nn) for d in range(1, nn)]
    z_peers = [lax.rem(z + d, nz) for d in range(1, nz)]
    q_peers = [lax.rem(q + d, QUAD) for d in range(1, QUAD)]
    at_n = lambda k: {"wide": w, "narrow": k}
    at_z = lambda k: {"wide": k * QUAD + q, "narrow": n}
    at_q = lambda k: {"wide": z * QUAD + k, "narrow": n}
    sibling = at_q(q + 1 - 2 * core)
    across = at_q(2 * (1 - x) + core)
    order = z_peers + [z]

    barrier = pltpu.get_barrier_semaphore()
    partners = [at_n(k) for k in narrow_peers] + [at_z(k) for k in z_peers] + [at_q(k) for k in q_peers]
    for device in partners:
        pl.semaphore_signal(barrier, inc=1, device_id=device, device_id_type=MESH)
    key_load = pltpu.make_async_copy(w_key, both_t.at[pl.ds(0, width)], loads.at[chunks])
    value_load = pltpu.make_async_copy(w_value, both_t.at[pl.ds(width, width)], loads.at[chunks + 1])
    out_load = pltpu.make_async_copy(w_out, out_w, loads.at[chunks + 2])
    key_load.start()
    value_load.start()
    for j in range(chunks):
        pltpu.make_async_copy(patches.at[pl.ds(j * SPAN, SPAN)], held.at[j], loads.at[j]).start()
    out_load.start()
    sent = []

    def exchange(peers, place, me, src, dst, send, recv):
        copies = [remote(src(k), dst.at[me], send.at[k], recv.at[me], place(k)) for k in peers]
        sent.extend(copies)

    def arrived(peers, buf, recv):
        for k in peers:
            pltpu.make_async_copy(buf.at[k], buf.at[k], recv.at[k]).wait()

    text_float = texts[...].astype(f32)
    text_norm = jnp.sqrt(jnp.sum(text_float * text_float, axis=1, keepdims=True) + 1e-06)
    text_unit = text_float / text_norm
    qbuf[q] = text_unit.astype(bf16).astype(f32)
    pl.semaphore_wait(barrier, len(partners))
    exchange(q_peers, at_q, q, lambda k: qbuf.at[q], qbuf, qsend.at[0], qrecv.at[0])
    slot_head = iota((SLOTS, width), 0) // CHUNK
    lane_head = iota((SLOTS, width), 1) // HEAD_DIM
    probe_row = probe[...].reshape(1, width).astype(f32)
    probe_slots = jnp.where(slot_head == lane_head, probe_row, 0.0).astype(bf16)
    slot_image = iota((SLOTS, SPAN), 0) % CHUNK
    own = slot_image == iota((SLOTS, SPAN), 1) // PATCHES

    def project(j):
        pltpu.make_async_copy(held.at[j], held.at[j], loads.at[j]).wait()
        rows = matmul(both_t[...], held[j], NT).astype(bf16)
        keys[j] = rows[:width]
        values[j] = rows[width:]

    def pool(j):
        scores = matmul(probe_slots, keys[j]) * root_scale
        scores = jnp.where(own, scores, -1e30)
        top = jnp.max(scores, axis=1, keepdims=True)
        shifted = jnp.where(own, jnp.exp(scores - top), 0.0)
        part = shifted / jnp.sum(shifted, axis=1, keepdims=True)
        weights[j] = part
        heads[j] = matmul(part.astype(bf16), values[j], NT)

    key_load.wait()
    value_load.wait()
    for j in range(chunks):
        project(j)
        if j == 1:
            arrived(q_peers, qbuf, qrecv.at[0])
            tbuf[z] = jnp.concatenate([qbuf[k] for k in range(QUAD)], axis=0).astype(bf16)
            exchange(z_peers, at_z, z, lambda k: tbuf.at[z], tbuf, zsend.at[0], zrecv.at[0])
    for j in range(chunks):
        pool(j)

    all_slots = chunks * SLOTS
    slot_of = iota((all_slots, width), 0)
    head_mask = (slot_of % SLOTS) // CHUNK == iota((all_slots, width), 1) // HEAD_DIM
    heads_slots = jnp.where(head_mask, heads[...].reshape(all_slots, width), 0.0).astype(bf16)
    row_of = iota((group, all_slots), 0)
    slot_at = iota((group, all_slots), 1)
    gather = jnp.where(slot_at // SLOTS * CHUNK + slot_at % CHUNK == row_of, 1.0, 0.0).astype(bf16)
    heads_out = matmul(gather, heads_slots).astype(bf16)
    out_load.wait()
    partial = matmul(heads_out, out_w[...])
    for k in range(nn):
        psrc[k] = partial[k * ROWS : (k + 1) * ROWS]
    exchange(narrow_peers, at_n, n, lambda k: psrc.at[k], rbuf, nsend.at[0], nrecv.at[0])

    def pool_rows(first, last):
        for j in range(first, last):
            rows = matmul(weights[j].astype(bf16), held[j])
            pooled_rows[j * SLOTS : (j + 1) * SLOTS] = rows

    half = chunks // 2
    pool_rows(0, half)
    each = D // (nz * QUAD)
    for k in range(nz):
        lane = iota((D, 128), 1)
        chosen = (iota((D, 128), 0) == (k * QUAD + q) * each + lane) & (lane < each)
        pick[:, k * 128 : (k + 1) * 128] = jnp.where(chosen, 1.0, 0.0).astype(bf16)
    arrived(narrow_peers, rbuf, nrecv.at[0])
    pooled = psrc[n]
    for k in narrow_peers:
        pooled = pooled + rbuf[k]
    pooled_norm = jnp.sqrt(jnp.sum(pooled * pooled, axis=1, keepdims=True) + 1e-06)
    image_unit = pooled / pooled_norm
    ibuf[n] = image_unit.astype(bf16).astype(f32)
    exchange(narrow_peers, at_n, n, lambda k: ibuf.at[n], ibuf, nsend.at[1], nrecv.at[1])
    pool_rows(half, chunks)
    arrived(z_peers, tbuf, zrecv.at[0])
    arrived(narrow_peers, ibuf, nrecv.at[1])

    image_low = jnp.concatenate([ibuf[k] for k in range(nn)], axis=0).astype(bf16)
    text_low = tbuf[...].reshape(span, D)
    logits = logit_scale * matmul(image_low, text_low, NT) + logit_bias
    image_ids = w * group + iota((group, span), 0)
    offsets = iota((group, span), 1)
    text_ids = offsets // ROWS * group + n * ROWS + offsets % ROWS
    signs = jnp.where(image_ids == text_ids, 1.0, -1.0).astype(f32)
    margin = -signs * logits
    small = jnp.exp(-jnp.abs(margin))
    loss_part = jnp.sum(jnp.maximum(margin, 0.0) + jnp.log1p(small), axis=1, keepdims=True)
    coef = -signs * jnp.where(margin >= 0.0, 1.0, small) / (1.0 + small)
    image_part = logit_scale * split_dot(coef, text_low, NN)
    for k in range(nn):
        gsrc[k, :, :D] = image_part[k * ROWS : (k + 1) * ROWS]
        gsrc[k, :, D:] = jnp.broadcast_to(loss_part[k * ROWS : (k + 1) * ROWS], (ROWS, 128))
    exchange(narrow_peers, at_n, n, lambda k: gsrc.at[k], gbuf, nsend.at[2], nrecv.at[2])
    text_part = logit_scale * split_dot(coef.T, image_low, NN)
    usrc[...] = text_part.astype(bf16).reshape(nz, QUAD * ROWS, D)
    exchange(z_peers, at_z, z, lambda k: usrc.at[k], ubuf, zsend.at[1], zrecv.at[1])
    high, low = high_low(pooled_rows[...])
    pooled_t = jnp.concatenate([high, low, high], axis=0).T
    blocks = D // nz
    for k in range(nz):
        left[k, :, : 3 * all_slots] = pooled_t[k * blocks : (k + 1) * blocks]

    arrived(narrow_peers, gbuf, nrecv.at[2])
    both = gsrc[n]
    for k in narrow_peers:
        both = both + gbuf[k]
    diagonal = iota((ROWS, 128), 0) == iota((ROWS, 128), 1)
    losses = jnp.sum(jnp.where(diagonal, both[:, D:], 0.0), axis=0, keepdims=True)
    loss_out[...] = losses[:, :ROWS]
    image_grad = both[:, :D]
    pooled_grad = (
        image_grad - image_unit * jnp.sum(image_unit * image_grad, axis=1, keepdims=True)
    ) / pooled_norm
    pbuf[n] = pooled_grad.astype(bf16).astype(f32)
    exchange(narrow_peers, at_n, n, lambda k: pbuf.at[n], pbuf, nsend.at[3], nrecv.at[3])

    arrived(narrow_peers, pbuf, nrecv.at[3])
    group_float = jnp.concatenate([pbuf[k] for k in range(nn)], axis=0)
    group_grad = group_float.astype(bf16)
    scatter = jnp.where(
        iota((all_slots, group), 0) // SLOTS * CHUNK + iota((all_slots, group), 0) % CHUNK
        == iota((all_slots, group), 1),
        1.0,
        0.0,
    ).astype(bf16)
    slot_grads = matmul(scatter, group_grad).astype(bf16)
    head_grad = jnp.where(head_mask, matmul(slot_grads, out_w[...], NT), 0.0)
    high = head_grad.astype(bf16).astype(f32)
    low = head_grad - high
    none = lambda rows, columns: jnp.zeros((rows, columns), f32)
    spare = 4 * all_slots - 3 * all_slots - group
    turned = jnp.concatenate([group_float, none(spare, D)], axis=0).astype(bf16).T
    for k in range(nz):
        left[k, :, 3 * all_slots :] = turned[k * blocks : (k + 1) * blocks]

    def value_rows(part):
        return jnp.concatenate(
            [part[:, :128], none(all_slots, 128), part[:, 128:], none(all_slots, 112)], axis=1
        )

    heads_float = heads_out.astype(f32)
    out_rows = jnp.concatenate(
        [none(group, 128), heads_float[:, :128], none(group, 16), heads_float[:, 128:], none(group, 96)],
        axis=1,
    )
    right = jnp.concatenate(
        [value_rows(high), value_rows(high), value_rows(low), out_rows, none(spare, WIDTH)], axis=0
    ).astype(bf16)
    rows = blocks // QUAD
    wide = zsrc.shape[1]
    slab = wide + rows
    fold = rows // 4
    def block_out(k):
        block = matmul(left[k], right)
        for there in range(QUAD):
            part = block[there * rows : (there + 1) * rows]
            here = grads.at[k, there % 2, there // 2]
            here[:rows] = part[:, :128]
            pieces = [part[g * fold : (g + 1) * fold, 256:288] for g in range(4)]
            pieces = jnp.concatenate(pieces, axis=1)
            here[rows:wide] = jnp.concatenate([pieces, none(wide - rows - fold, 128)], axis=0)
            here[wide:] = part[:, 128:256]
        sent.append(remote(grads.at[k, 1 - core], abuf.at[k], asend.at[k], arecv.at[k], sibling))

    def forward(k):
        pltpu.make_async_copy(abuf.at[k], abuf.at[k], arecv.at[k]).wait()
        given = grads[k, core, 1 - x] + abuf[k, 1 - x]
        given = jnp.concatenate([given, none(2 * wide - slab, 128)], axis=0)
        xsrc[k] = given.astype(bf16)
        sent.append(remote(xsrc.at[k], xbuf.at[k], xsend.at[k], xrecv.at[k], across))

    def onward(i):
        k = order[i]
        pltpu.make_async_copy(xbuf.at[k], xbuf.at[k], xrecv.at[k]).wait()
        total = grads[k, core, x] + abuf[k, x] + xbuf[k].astype(f32)[:slab]
        if i < nz - 1:
            zsrc[k] = total[:wide]
            sent.append(remote(zsrc.at[k], zbuf.at[z], zsend.at[3, k], zrecv.at[3, z], at_z(k)))
            osrc[k] = jnp.concatenate([total[wide:], none(2 * wide - slab, 128)], axis=0).astype(bf16)
            sent.append(remote(osrc.at[k], obuf.at[z], zsend.at[4, k], zrecv.at[4, z], at_z(k)))
        return total

    for i in range(nz):
        block_out(order[i])
        if i > 1:
            forward(order[i - 2])
    for j in range(chunks):
        pair = [high[j * SLOTS : (j + 1) * SLOTS], low[j * SLOTS : (j + 1) * SLOTS]]
        head_rows[j] = jnp.concatenate(pair, axis=0).astype(bf16)
    forward(order[nz - 2])
    forward(order[nz - 1])

    def three_parts(values):
        one = values.astype(bf16).astype(f32)
        two = (values - one).astype(bf16).astype(f32)
        return jnp.concatenate([one, two, values - one - two, jnp.zeros_like(one)], axis=0).astype(bf16)

    score_sum = none(2 * SLOTS, D)
    for j in range(chunks):
        weight_grad = matmul(head_rows[j], values[j])
        weight_grad = weight_grad[:SLOTS] + weight_grad[SLOTS:]
        part = weights[j]
        inner = jnp.sum(part * weight_grad, axis=1, keepdims=True)
        score_grad = part * (weight_grad - inner)
        top = score_grad.astype(bf16).astype(f32)
        pair = jnp.concatenate([top, score_grad - top], axis=0).astype(bf16)
        score_sum = score_sum + matmul(pair, held[j])
        if j == chunks // 2:
            arrived(z_peers, ubuf, zrecv.at[1])
            quad_grad = usrc[z].astype(f32)
            for k in z_peers:
                quad_grad = quad_grad + ubuf[k].astype(f32)
            for k in range(QUAD):
                vsrc[k] = quad_grad[k * ROWS : (k + 1) * ROWS]
            exchange(q_peers, at_q, q, lambda k: vsrc.at[k], vbuf, qsend.at[1], qrecv.at[1])
    per_head = score_sum[:SLOTS] + score_sum[SLOTS:]
    for h in range(2):
        ssum[h : h + 1] = jnp.sum(per_head[h * CHUNK : (h + 1) * CHUNK], axis=0, keepdims=True)
    sbuf[q] = ssum[...]
    exchange(q_peers, at_q, q, lambda k: ssum, sbuf, qsend.at[2], qrecv.at[2])
    for i in range(nz // 2):
        onward(i)
    arrived(q_peers, sbuf, qrecv.at[2])
    scores_all = sbuf[0] + sbuf[1] + sbuf[2] + sbuf[3]
    picked = matmul(three_parts(scores_all), pick[...])
    for k in range(nz):
        mine = picked[:, k * 128 : (k + 1) * 128]
        szsum[k] = mine[0:2] + mine[2:4] + mine[4:6]
    exchange(z_peers, at_z, z, lambda k: szsum.at[k], szbuf, zsend.at[2], zrecv.at[2])
    for i in range(nz // 2, nz):
        total = onward(i)
    arrived(q_peers, vbuf, qrecv.at[1])
    unit_grad = vsrc[q]
    for k in q_peers:
        unit_grad = unit_grad + vbuf[k]
    text_out[...] = (
        unit_grad - text_unit * jnp.sum(text_unit * unit_grad, axis=1, keepdims=True)
    ) / text_norm

    arrived(z_peers, szbuf, zrecv.at[2])
    scores_all = szsum[z]
    for k in z_peers:
        scores_all = scores_all + szbuf[k]
    spread = jnp.where(
        (iota((8, width), 0) % 2 == iota((8, width), 1) // HEAD_DIM) & (iota((8, width), 0) < 6), probe_row, 0.0
    ).astype(bf16)
    keyed = matmul(three_parts(scores_all), spread, (((0,), (0,)), ((), ())))
    key_out[...] = keyed[:rows] * root_scale

    value_total, out_total = total[:wide], total[wide:]
    for k in reversed(z_peers):
        pltpu.make_async_copy(zbuf.at[k], zbuf.at[k], zrecv.at[3, k]).wait()
        value_total = value_total + zbuf[k]
        pltpu.make_async_copy(obuf.at[k], obuf.at[k], zrecv.at[4, k]).wait()
        out_total = out_total + obuf[k].astype(f32)[:rows]
    rest = value_total[rows : rows + fold]
    rest = jnp.concatenate([rest[:, 32 * g : 32 * (g + 1)] for g in range(4)], axis=0)
    value_out[...] = jnp.concatenate([value_total[:rows], rest[:, :16]], axis=1)
    out_out[...] = jnp.concatenate([out_total, rest[:, 16:]], axis=1)
    for copy in sent:
        copy.wait_send()


def finish_kernel(*refs):
    count = len(refs) // 2
    for source, target in zip(refs[:count], refs[count:]):
        target[...] = source[...]


def finish(*arrays):
    vmem = pl.BlockSpec(memory_space=pltpu.VMEM)
    return pl.pallas_call(
        finish_kernel,
        out_shape=tuple(jax.ShapeDtypeStruct(a.shape, a.dtype) for a in arrays),
        in_specs=[vmem] * len(arrays),
        out_specs=(vmem,) * len(arrays),
        compiler_params=pltpu.CompilerParams(vmem_limit_bytes=60 * 1024 * 1024),
    )(*arrays)


def call(nz, nn, patches, w_key, w_value, w_out, probe, texts):
    vmem = pl.BlockSpec(memory_space=pltpu.VMEM)
    f32, bf16 = jnp.float32, jnp.bfloat16
    group = nn * ROWS
    chunks = group // CHUNK
    width = w_key.shape[0]
    rows = D // nz // QUAD
    part = -(-(rows + rows // 4) // 16) * 16
    slab = part + rows
    slots = chunks * SLOTS
    dma = pltpu.SemaphoreType.DMA
    return pl.pallas_call(
        functools.partial(kernel, nz, nn),
        out_shape=(
            jax.ShapeDtypeStruct((1, ROWS), f32),
            jax.ShapeDtypeStruct((ROWS, D), f32),
            jax.ShapeDtypeStruct((rows, width), f32),
            jax.ShapeDtypeStruct((rows, width), f32),
            jax.ShapeDtypeStruct((rows, width), f32),
        ),
        in_specs=[pl.BlockSpec(memory_space=pl.ANY)] * 4 + [vmem] * 2,
        out_specs=(vmem,) * 5,
        scratch_shapes=[
            pltpu.VMEM((chunks, SPAN, D), bf16),
            pltpu.VMEM((2 * width, D), bf16),
            pltpu.VMEM((width, D), bf16),
            pltpu.VMEM((chunks, width, SPAN), bf16),
            pltpu.VMEM((chunks, width, SPAN), bf16),
            pltpu.VMEM((chunks, SLOTS, SPAN), f32),
            pltpu.VMEM((chunks, SLOTS, width), f32),
            pltpu.VMEM((slots, D), f32),
            pltpu.VMEM((nz, D // nz, 4 * slots), bf16),
            pltpu.VMEM((nn, ROWS, D), f32),
            pltpu.VMEM((nn, ROWS, D), f32),
            pltpu.VMEM((QUAD, ROWS, D), f32),
            pltpu.VMEM((nz, QUAD * ROWS, D), bf16),
            pltpu.VMEM((nn, ROWS, D), f32),
            pltpu.VMEM((nn, ROWS, D + 128), f32),
            pltpu.VMEM((nn, ROWS, D + 128), f32),
            pltpu.VMEM((nz, QUAD * ROWS, D), bf16),
            pltpu.VMEM((nz, QUAD * ROWS, D), bf16),
            pltpu.VMEM((QUAD, ROWS, D), f32),
            pltpu.VMEM((QUAD, ROWS, D), f32),
            pltpu.VMEM((nn, ROWS, D), f32),
            pltpu.VMEM((nz, 2, 2, slab, 128), f32),
            pltpu.VMEM((nz, 2, slab, 128), f32),
            pltpu.VMEM((nz, 2 * part, 128), bf16),
            pltpu.VMEM((nz, 2 * part, 128), bf16),
            pltpu.VMEM((nz, part, 128), f32),
            pltpu.VMEM((nz, part, 128), f32),
            pltpu.VMEM((nz, part, 128), bf16),
            pltpu.VMEM((nz, part, 128), bf16),
            pltpu.VMEM((D, nz * 128), bf16),
            pltpu.VMEM((chunks, 2 * SLOTS, width), bf16),
            pltpu.VMEM((2, D), f32),
            pltpu.VMEM((QUAD, 2, D), f32),
            pltpu.VMEM((nz, 2, 128), f32),
            pltpu.VMEM((nz, 2, 128), f32),
            dma((chunks + 3,)),
            dma((4, nn)),
            dma((4, nn)),
            dma((5, nz)),
            dma((5, nz)),
            dma((3, QUAD)),
            dma((3, QUAD)),
            dma((nz,)),
            dma((nz,)),
            dma((nz,)),
            dma((nz,)),
        ],
        compiler_params=pltpu.CompilerParams(
            collective_id=0, has_side_effects=True, vmem_limit_bytes=56 * 1024 * 1024
        ),
    )(patches, w_key, w_value, w_out, probe, texts)


def shards(patches, w_key, w_value, w_out, probe, texts):
    nz = lax.axis_size("wide") // QUAD
    nn = lax.axis_size("narrow")
    flat_rows = patches.reshape(patches.shape[0] * PATCHES, D)
    row_loss, text_grad, grad_key, grad_value, grad_out = call(
        nz, nn, flat_rows, w_key.T, w_value.T, w_out, probe, texts
    )
    row_loss, text_grad, grad_key, grad_value, grad_out = finish(
        row_loss, text_grad, grad_key, grad_value, grad_out
    )
    return (row_loss.reshape(ROWS), text_grad, grad_key, grad_value, grad_out.T)


def solution(mesh):
    return jax.shard_map(
        shards,
        mesh=mesh,
        in_specs=(
            P("wide", None, None),
            P(None, "narrow"),
            P(None, "narrow"),
            P("narrow", None),
            P("narrow"),
            P(("wide", "narrow"), None),
        ),
        out_specs=(
            P(("wide", "narrow")),
            P(("wide", "narrow"), None),
            P("wide", "narrow"),
            P("wide", "narrow"),
            P("narrow", "wide"),
        ),
        check_vma=False,
    )
```

```python
import functools
import math

import jax
import jax.numpy as jnp
from jax import lax
from jax.experimental import pallas as pl
from jax.experimental.pallas import tpu as pltpu
from jax.sharding import PartitionSpec as P

D = 1152
HEAD_DIM = 72
PATCHES = 256
QUAD = 4
ROWS = 4
MESH = pl.DeviceIdType.MESH

logit_scale = 16.0
logit_bias = -4.0


def remote(src, dst, send, recv, device):
    copy = pltpu.make_async_remote_copy(
        src_ref=src,
        dst_ref=dst,
        send_sem=send,
        recv_sem=recv,
        device_id=device,
        device_id_type=MESH,
    )
    copy.start()
    return copy


def split_dot(coef, other, dims):
    high = coef.astype(jnp.bfloat16)
    rest = coef - high.astype(jnp.float32)
    low = rest.astype(jnp.bfloat16)
    dot = lambda part: lax.dot_general(part, other, dims, preferred_element_type=jnp.float32)
    return dot(low) + dot(high)


CHUNK = 4
SPAN = CHUNK * PATCHES
SLOTS = 2 * CHUNK
WIDTH = 384
NT = (((1,), (1,)), ((), ()))
NN = (((1,), (0,)), ((), ()))


def matmul(a, b, dims=NN):
    return lax.dot_general(a, b, dims, preferred_element_type=jnp.float32)


def high_low(values):
    high = values.astype(jnp.bfloat16)
    low = (values - high.astype(jnp.float32)).astype(jnp.bfloat16)
    return high, low


def iota(shape, axis):
    return lax.broadcasted_iota(jnp.int32, shape, axis)


def kernel(
    nz, nn, patches, w_key, w_value, w_out, probe, texts,
    loss_out, text_out, key_out, value_out, out_out,
    held, both_t, out_w, keys, values, weights, heads, pooled_rows, left,
    psrc, rbuf, qbuf, tbuf, ibuf, gsrc, gbuf, usrc, ubuf, vsrc, vbuf, pbuf,
    grads, abuf, xsrc, xbuf, zsrc, zbuf, osrc, obuf, pick, head_rows, ssum, sbuf, szsum, szbuf,
    loads, nsend, nrecv, zsend, zrecv, qsend, qrecv, asend, arecv, xsend, xrecv,
):
    f32, bf16 = jnp.float32, jnp.bfloat16
    w, n = lax.axis_index("wide"), lax.axis_index("narrow")
    z, q = w // QUAD, lax.rem(w, QUAD)
    x, core = q // 2, lax.rem(q, 2)
    group, span = nn * ROWS, nz * QUAD * ROWS
    chunks = group // CHUNK
    width = w_key.shape[0]
    root_scale = 1.0 / math.sqrt(HEAD_DIM)
    ring = nn // 2
    steps = [(a, d) for a in range(2) for d in range(ring) if a + d > 0]
    steps.sort(key=lambda step: -(step[0] + min(step[1], ring - step[1])))
    narrow_peers = [lax.rem(n // ring + a, 2) * ring + lax.rem(n + d, ring) for a, d in steps]
    z_steps = sorted(range(1, nz), key=lambda d: -min(d, nz - d))
    z_peers = [lax.rem(z + d, nz) for d in z_steps]
    q_peers = [lax.rem(q + d, QUAD) for d in range(1, QUAD)]
    at_n = lambda k: {"wide": w, "narrow": k}
    at_z = lambda k: {"wide": k * QUAD + q, "narrow": n}
    at_q = lambda k: {"wide": z * QUAD + k, "narrow": n}
    sibling = at_q(q + 1 - 2 * core)
    across = at_q(2 * (1 - x) + core)
    order = z_peers + [z]

    barrier = pltpu.get_barrier_semaphore()
    partners = [at_n(k) for k in narrow_peers] + [at_z(k) for k in z_peers] + [at_q(k) for k in q_peers]
    for device in partners:
        pl.semaphore_signal(barrier, inc=1, device_id=device, device_id_type=MESH)
    key_load = pltpu.make_async_copy(w_key, both_t.at[pl.ds(0, width)], loads.at[chunks])
    value_load = pltpu.make_async_copy(w_value, both_t.at[pl.ds(width, width)], loads.at[chunks + 1])
    out_load = pltpu.make_async_copy(w_out, out_w, loads.at[chunks + 2])
    key_load.start()
    value_load.start()
    for j in range(chunks):
        pltpu.make_async_copy(patches.at[pl.ds(j * SPAN, SPAN)], held.at[j], loads.at[j]).start()
    out_load.start()
    sent = []

    def exchange(peers, place, me, src, dst, send, recv):
        copies = [remote(src(k), dst.at[me], send.at[k], recv.at[me], place(k)) for k in peers]
        sent.extend(copies)

    def arrived(peers, buf, recv):
        for k in peers:
            pltpu.make_async_copy(buf.at[k], buf.at[k], recv.at[k]).wait()

    text_float = texts[...].astype(f32)
    text_norm = jnp.sqrt(jnp.sum(text_float * text_float, axis=1, keepdims=True) + 1e-06)
    text_unit = text_float / text_norm
    qbuf[q] = text_unit.astype(bf16).astype(f32)
    pl.semaphore_wait(barrier, len(partners))
    exchange(q_peers, at_q, q, lambda k: qbuf.at[q], qbuf, qsend.at[0], qrecv.at[0])
    slot_head = iota((SLOTS, width), 0) // CHUNK
    lane_head = iota((SLOTS, width), 1) // HEAD_DIM
    probe_row = probe[...].reshape(1, width).astype(f32)
    probe_slots = jnp.where(slot_head == lane_head, probe_row, 0.0).astype(bf16)
    slot_image = iota((SLOTS, SPAN), 0) % CHUNK
    own = slot_image == iota((SLOTS, SPAN), 1) // PATCHES

    def project(j):
        pltpu.make_async_copy(held.at[j], held.at[j], loads.at[j]).wait()
        rows = matmul(both_t[...], held[j], NT).astype(bf16)
        keys[j] = rows[:width]
        values[j] = rows[width:]

    def pool(j):
        scores = matmul(probe_slots, keys[j]) * root_scale
        scores = jnp.where(own, scores, -1e30)
        top = jnp.max(scores, axis=1, keepdims=True)
        shifted = jnp.where(own, jnp.exp(scores - top), 0.0)
        part = shifted / jnp.sum(shifted, axis=1, keepdims=True)
        weights[j] = part
        heads[j] = matmul(part.astype(bf16), values[j], NT)

    key_load.wait()
    value_load.wait()
    for j in range(chunks):
        project(j)
        if j == 1:
            arrived(q_peers, qbuf, qrecv.at[0])
            tbuf[z] = jnp.concatenate([qbuf[k] for k in range(QUAD)], axis=0).astype(bf16)
            exchange(z_peers, at_z, z, lambda k: tbuf.at[z], tbuf, zsend.at[0], zrecv.at[0])
    for j in range(chunks):
        pool(j)

    all_slots = chunks * SLOTS
    slot_of = iota((all_slots, width), 0)
    head_mask = (slot_of % SLOTS) // CHUNK == iota((all_slots, width), 1) // HEAD_DIM
    heads_slots = jnp.where(head_mask, heads[...].reshape(all_slots, width), 0.0).astype(bf16)
    row_of = iota((group, all_slots), 0)
    slot_at = iota((group, all_slots), 1)
    gather = jnp.where(slot_at // SLOTS * CHUNK + slot_at % CHUNK == row_of, 1.0, 0.0).astype(bf16)
    heads_out = matmul(gather, heads_slots).astype(bf16)
    out_load.wait()
    partial = matmul(heads_out, out_w[...])
    for k in range(nn):
        psrc[k] = partial[k * ROWS : (k + 1) * ROWS]
    exchange(narrow_peers, at_n, n, lambda k: psrc.at[k], rbuf, nsend.at[0], nrecv.at[0])

    def pool_rows(first, last):
        for j in range(first, last):
            rows = matmul(weights[j].astype(bf16), held[j])
            pooled_rows[j * SLOTS : (j + 1) * SLOTS] = rows

    half = chunks // 2
    pool_rows(0, half)
    each = D // (nz * QUAD)
    for k in range(nz):
        lane = iota((D, 128), 1)
        chosen = (iota((D, 128), 0) == (k * QUAD + q) * each + lane) & (lane < each)
        pick[:, k * 128 : (k + 1) * 128] = jnp.where(chosen, 1.0, 0.0).astype(bf16)
    arrived(narrow_peers, rbuf, nrecv.at[0])
    pooled = psrc[n]
    for k in narrow_peers:
        pooled = pooled + rbuf[k]
    pooled_norm = jnp.sqrt(jnp.sum(pooled * pooled, axis=1, keepdims=True) + 1e-06)
    image_unit = pooled / pooled_norm
    ibuf[n] = image_unit.astype(bf16).astype(f32)
    exchange(narrow_peers, at_n, n, lambda k: ibuf.at[n], ibuf, nsend.at[1], nrecv.at[1])
    pool_rows(half, chunks)
    arrived(z_peers, tbuf, zrecv.at[0])
    arrived(narrow_peers, ibuf, nrecv.at[1])

    image_low = jnp.concatenate([ibuf[k] for k in range(nn)], axis=0).astype(bf16)
    text_low = tbuf[...].reshape(span, D)
    logits = logit_scale * matmul(image_low, text_low, NT) + logit_bias
    image_ids = w * group + iota((group, span), 0)
    offsets = iota((group, span), 1)
    text_ids = offsets // ROWS * group + n * ROWS + offsets % ROWS
    signs = jnp.where(image_ids == text_ids, 1.0, -1.0).astype(f32)
    margin = -signs * logits
    small = jnp.exp(-jnp.abs(margin))
    loss_part = jnp.sum(jnp.maximum(margin, 0.0) + jnp.log1p(small), axis=1, keepdims=True)
    coef = -signs * jnp.where(margin >= 0.0, 1.0, small) / (1.0 + small)
    image_part = logit_scale * split_dot(coef, text_low, NN)
    for k in range(nn):
        gsrc[k, :, :D] = image_part[k * ROWS : (k + 1) * ROWS]
        gsrc[k, :, D:] = jnp.broadcast_to(loss_part[k * ROWS : (k + 1) * ROWS], (ROWS, 128))
    exchange(narrow_peers, at_n, n, lambda k: gsrc.at[k], gbuf, nsend.at[2], nrecv.at[2])
    text_part = logit_scale * split_dot(coef.T, image_low, NN)
    usrc[...] = text_part.astype(bf16).reshape(nz, QUAD * ROWS, D)
    exchange(z_peers, at_z, z, lambda k: usrc.at[k], ubuf, zsend.at[1], zrecv.at[1])
    high, low = high_low(pooled_rows[...])
    pooled_t = jnp.concatenate([high, low, high], axis=0).T
    blocks = D // nz
    for k in range(nz):
        left[k, :, : 3 * all_slots] = pooled_t[k * blocks : (k + 1) * blocks]

    arrived(narrow_peers, gbuf, nrecv.at[2])
    both = gsrc[n]
    for k in narrow_peers:
        both = both + gbuf[k]
    diagonal = iota((ROWS, 128), 0) == iota((ROWS, 128), 1)
    losses = jnp.sum(jnp.where(diagonal, both[:, D:], 0.0), axis=0, keepdims=True)
    loss_out[...] = losses[:, :ROWS]
    image_grad = both[:, :D]
    pooled_grad = (
        image_grad - image_unit * jnp.sum(image_unit * image_grad, axis=1, keepdims=True)
    ) / pooled_norm
    pbuf[n] = pooled_grad.astype(bf16).astype(f32)
    exchange(narrow_peers, at_n, n, lambda k: pbuf.at[n], pbuf, nsend.at[3], nrecv.at[3])

    arrived(narrow_peers, pbuf, nrecv.at[3])
    group_float = jnp.concatenate([pbuf[k] for k in range(nn)], axis=0)
    group_grad = group_float.astype(bf16)
    scatter = jnp.where(
        iota((all_slots, group), 0) // SLOTS * CHUNK + iota((all_slots, group), 0) % CHUNK
        == iota((all_slots, group), 1),
        1.0,
        0.0,
    ).astype(bf16)
    slot_grads = matmul(scatter, group_grad).astype(bf16)
    head_grad = jnp.where(head_mask, matmul(slot_grads, out_w[...], NT), 0.0)
    high = head_grad.astype(bf16).astype(f32)
    low = head_grad - high
    none = lambda rows, columns: jnp.zeros((rows, columns), f32)
    spare = 4 * all_slots - 3 * all_slots - group
    turned = jnp.concatenate([group_float, none(spare, D)], axis=0).astype(bf16).T
    for k in range(nz):
        left[k, :, 3 * all_slots :] = turned[k * blocks : (k + 1) * blocks]

    def value_rows(part):
        return jnp.concatenate(
            [part[:, :128], none(all_slots, 128), part[:, 128:], none(all_slots, 112)], axis=1
        )

    heads_float = heads_out.astype(f32)
    out_rows = jnp.concatenate(
        [none(group, 128), heads_float[:, :128], none(group, 16), heads_float[:, 128:], none(group, 96)],
        axis=1,
    )
    right = jnp.concatenate(
        [value_rows(high), value_rows(high), value_rows(low), out_rows, none(spare, WIDTH)], axis=0
    ).astype(bf16)
    rows = blocks // QUAD
    wide = zsrc.shape[1]
    slab = wide + rows
    fold = rows // 4
    def block_out(k):
        block = matmul(left[k], right)
        for there in range(QUAD):
            part = block[there * rows : (there + 1) * rows]
            here = grads.at[k, there % 2, there // 2]
            here[:rows] = part[:, :128]
            pieces = [part[g * fold : (g + 1) * fold, 256:288] for g in range(4)]
            pieces = jnp.concatenate(pieces, axis=1)
            here[rows:wide] = jnp.concatenate([pieces, none(wide - rows - fold, 128)], axis=0)
            here[wide:] = part[:, 128:256]
        sent.append(remote(grads.at[k, 1 - core], abuf.at[k], asend.at[k], arecv.at[k], sibling))

    def forward(k):
        pltpu.make_async_copy(abuf.at[k], abuf.at[k], arecv.at[k]).wait()
        given = grads[k, core, 1 - x] + abuf[k, 1 - x]
        given = jnp.concatenate([given, none(2 * wide - slab, 128)], axis=0)
        xsrc[k] = given.astype(bf16)
        sent.append(remote(xsrc.at[k], xbuf.at[k], xsend.at[k], xrecv.at[k], across))

    def onward(i):
        k = order[i]
        pltpu.make_async_copy(xbuf.at[k], xbuf.at[k], xrecv.at[k]).wait()
        total = grads[k, core, x] + abuf[k, x] + xbuf[k].astype(f32)[:slab]
        if i < nz - 1:
            zsrc[k] = total[:wide]
            sent.append(remote(zsrc.at[k], zbuf.at[z], zsend.at[3, k], zrecv.at[3, z], at_z(k)))
            osrc[k] = jnp.concatenate([total[wide:], none(2 * wide - slab, 128)], axis=0).astype(bf16)
            sent.append(remote(osrc.at[k], obuf.at[z], zsend.at[4, k], zrecv.at[4, z], at_z(k)))
        return total

    for i in range(nz):
        block_out(order[i])
        if i > 1:
            forward(order[i - 2])
    for j in range(chunks):
        pair = [high[j * SLOTS : (j + 1) * SLOTS], low[j * SLOTS : (j + 1) * SLOTS]]
        head_rows[j] = jnp.concatenate(pair, axis=0).astype(bf16)
    forward(order[nz - 2])
    forward(order[nz - 1])

    def three_parts(values):
        one = values.astype(bf16).astype(f32)
        two = (values - one).astype(bf16).astype(f32)
        return jnp.concatenate([one, two, values - one - two, jnp.zeros_like(one)], axis=0).astype(bf16)

    score_sum = none(2 * SLOTS, D)
    moved = 0
    for j in range(chunks):
        weight_grad = matmul(head_rows[j], values[j])
        weight_grad = weight_grad[:SLOTS] + weight_grad[SLOTS:]
        part = weights[j]
        inner = jnp.sum(part * weight_grad, axis=1, keepdims=True)
        score_grad = part * (weight_grad - inner)
        top = score_grad.astype(bf16).astype(f32)
        pair = jnp.concatenate([top, score_grad - top], axis=0).astype(bf16)
        score_sum = score_sum + matmul(pair, held[j])
        while moved < j - 2:
            onward(moved)
            moved += 1
    per_head = score_sum[:SLOTS] + score_sum[SLOTS:]
    for h in range(2):
        ssum[h : h + 1] = jnp.sum(per_head[h * CHUNK : (h + 1) * CHUNK], axis=0, keepdims=True)
    sbuf[q] = ssum[...]
    exchange(q_peers, at_q, q, lambda k: ssum, sbuf, qsend.at[2], qrecv.at[2])
    while moved < nz:
        total = onward(moved)
        moved += 1
    arrived(q_peers, sbuf, qrecv.at[2])
    scores_all = sbuf[0] + sbuf[1] + sbuf[2] + sbuf[3]
    picked = matmul(three_parts(scores_all), pick[...])
    for k in range(nz):
        mine = picked[:, k * 128 : (k + 1) * 128]
        szsum[k] = mine[0:2] + mine[2:4] + mine[4:6]
    exchange(z_peers, at_z, z, lambda k: szsum.at[k], szbuf, zsend.at[2], zrecv.at[2])
    arrived(z_peers, ubuf, zrecv.at[1])
    quad_grad = usrc[z].astype(f32)
    for k in z_peers:
        quad_grad = quad_grad + ubuf[k].astype(f32)
    for k in range(QUAD):
        vsrc[k] = quad_grad[k * ROWS : (k + 1) * ROWS]
    exchange(q_peers, at_q, q, lambda k: vsrc.at[k], vbuf, qsend.at[1], qrecv.at[1])

    arrived(q_peers, vbuf, qrecv.at[1])
    unit_grad = vsrc[q]
    for k in q_peers:
        unit_grad = unit_grad + vbuf[k]
    text_out[...] = (
        unit_grad - text_unit * jnp.sum(text_unit * unit_grad, axis=1, keepdims=True)
    ) / text_norm

    arrived(z_peers, szbuf, zrecv.at[2])
    scores_all = szsum[z]
    for k in z_peers:
        scores_all = scores_all + szbuf[k]
    spread = jnp.where(
        (iota((8, width), 0) % 2 == iota((8, width), 1) // HEAD_DIM) & (iota((8, width), 0) < 6), probe_row, 0.0
    ).astype(bf16)
    keyed = matmul(three_parts(scores_all), spread, (((0,), (0,)), ((), ())))
    key_out[...] = keyed[:rows] * root_scale

    value_total, out_total = total[:wide], total[wide:]
    for k in reversed(z_peers):
        pltpu.make_async_copy(zbuf.at[k], zbuf.at[k], zrecv.at[3, k]).wait()
        value_total = value_total + zbuf[k]
        pltpu.make_async_copy(obuf.at[k], obuf.at[k], zrecv.at[4, k]).wait()
        out_total = out_total + obuf[k].astype(f32)[:rows]
    rest = value_total[rows : rows + fold]
    rest = jnp.concatenate([rest[:, 32 * g : 32 * (g + 1)] for g in range(4)], axis=0)
    value_out[...] = jnp.concatenate([value_total[:rows], rest[:, :16]], axis=1)
    out_out[...] = jnp.concatenate([out_total, rest[:, 16:]], axis=1)
    for copy in sent:
        copy.wait_send()


def finish_kernel(*refs):
    count = len(refs) // 2
    for source, target in zip(refs[:count], refs[count:]):
        target[...] = source[...]


def finish(*arrays):
    vmem = pl.BlockSpec(memory_space=pltpu.VMEM)
    return pl.pallas_call(
        finish_kernel,
        out_shape=tuple(jax.ShapeDtypeStruct(a.shape, a.dtype) for a in arrays),
        in_specs=[vmem] * len(arrays),
        out_specs=(vmem,) * len(arrays),
        compiler_params=pltpu.CompilerParams(vmem_limit_bytes=60 * 1024 * 1024),
    )(*arrays)


def call(nz, nn, patches, w_key, w_value, w_out, probe, texts):
    vmem = pl.BlockSpec(memory_space=pltpu.VMEM)
    f32, bf16 = jnp.float32, jnp.bfloat16
    group = nn * ROWS
    chunks = group // CHUNK
    width = w_key.shape[0]
    rows = D // nz // QUAD
    part = -(-(rows + rows // 4) // 16) * 16
    slab = part + rows
    slots = chunks * SLOTS
    dma = pltpu.SemaphoreType.DMA
    return pl.pallas_call(
        functools.partial(kernel, nz, nn),
        out_shape=(
            jax.ShapeDtypeStruct((1, ROWS), f32),
            jax.ShapeDtypeStruct((ROWS, D), f32),
            jax.ShapeDtypeStruct((rows, width), f32),
            jax.ShapeDtypeStruct((rows, width), f32),
            jax.ShapeDtypeStruct((rows, width), f32),
        ),
        in_specs=[pl.BlockSpec(memory_space=pl.ANY)] * 4 + [vmem] * 2,
        out_specs=(vmem,) * 5,
        scratch_shapes=[
            pltpu.VMEM((chunks, SPAN, D), bf16),
            pltpu.VMEM((2 * width, D), bf16),
            pltpu.VMEM((width, D), bf16),
            pltpu.VMEM((chunks, width, SPAN), bf16),
            pltpu.VMEM((chunks, width, SPAN), bf16),
            pltpu.VMEM((chunks, SLOTS, SPAN), f32),
            pltpu.VMEM((chunks, SLOTS, width), f32),
            pltpu.VMEM((slots, D), f32),
            pltpu.VMEM((nz, D // nz, 4 * slots), bf16),
            pltpu.VMEM((nn, ROWS, D), f32),
            pltpu.VMEM((nn, ROWS, D), f32),
            pltpu.VMEM((QUAD, ROWS, D), f32),
            pltpu.VMEM((nz, QUAD * ROWS, D), bf16),
            pltpu.VMEM((nn, ROWS, D), f32),
            pltpu.VMEM((nn, ROWS, D + 128), f32),
            pltpu.VMEM((nn, ROWS, D + 128), f32),
            pltpu.VMEM((nz, QUAD * ROWS, D), bf16),
            pltpu.VMEM((nz, QUAD * ROWS, D), bf16),
            pltpu.VMEM((QUAD, ROWS, D), f32),
            pltpu.VMEM((QUAD, ROWS, D), f32),
            pltpu.VMEM((nn, ROWS, D), f32),
            pltpu.VMEM((nz, 2, 2, slab, 128), f32),
            pltpu.VMEM((nz, 2, slab, 128), f32),
            pltpu.VMEM((nz, 2 * part, 128), bf16),
            pltpu.VMEM((nz, 2 * part, 128), bf16),
            pltpu.VMEM((nz, part, 128), f32),
            pltpu.VMEM((nz, part, 128), f32),
            pltpu.VMEM((nz, part, 128), bf16),
            pltpu.VMEM((nz, part, 128), bf16),
            pltpu.VMEM((D, nz * 128), bf16),
            pltpu.VMEM((chunks, 2 * SLOTS, width), bf16),
            pltpu.VMEM((2, D), f32),
            pltpu.VMEM((QUAD, 2, D), f32),
            pltpu.VMEM((nz, 2, 128), f32),
            pltpu.VMEM((nz, 2, 128), f32),
            dma((chunks + 3,)),
            dma((4, nn)),
            dma((4, nn)),
            dma((5, nz)),
            dma((5, nz)),
            dma((3, QUAD)),
            dma((3, QUAD)),
            dma((nz,)),
            dma((nz,)),
            dma((nz,)),
            dma((nz,)),
        ],
        compiler_params=pltpu.CompilerParams(
            collective_id=0, has_side_effects=True, vmem_limit_bytes=56 * 1024 * 1024
        ),
    )(patches, w_key, w_value, w_out, probe, texts)


def shards(patches, w_key, w_value, w_out, probe, texts):
    nz = lax.axis_size("wide") // QUAD
    nn = lax.axis_size("narrow")
    flat_rows = patches.reshape(patches.shape[0] * PATCHES, D)
    row_loss, text_grad, grad_key, grad_value, grad_out = call(
        nz, nn, flat_rows, w_key.T, w_value.T, w_out, probe, texts
    )
    row_loss, text_grad, grad_key, grad_value, grad_out = finish(
        row_loss, text_grad, grad_key, grad_value, grad_out
    )
    return (row_loss.reshape(ROWS), text_grad, grad_key, grad_value, grad_out.T)


def solution(mesh):
    return jax.shard_map(
        shards,
        mesh=mesh,
        in_specs=(
            P("wide", None, None),
            P(None, "narrow"),
            P(None, "narrow"),
            P("narrow", None),
            P("narrow"),
            P(("wide", "narrow"), None),
        ),
        out_specs=(
            P(("wide", "narrow")),
            P(("wide", "narrow"), None),
            P("wide", "narrow"),
            P("wide", "narrow"),
            P("narrow", "wide"),
        ),
        check_vma=False,
    )
```

```python
import functools
import math

import jax
import jax.numpy as jnp
from jax import lax
from jax.experimental import pallas as pl
from jax.experimental.pallas import tpu as pltpu
from jax.sharding import PartitionSpec as P

D = 1152
HEAD_DIM = 72
PATCHES = 256
QUAD = 4
ROWS = 4
MESH = pl.DeviceIdType.MESH

logit_scale = 16.0
logit_bias = -4.0


def remote(src, dst, send, recv, device):
    copy = pltpu.make_async_remote_copy(
        src_ref=src,
        dst_ref=dst,
        send_sem=send,
        recv_sem=recv,
        device_id=device,
        device_id_type=MESH,
    )
    copy.start()
    return copy


def split_dot(coef, other, dims):
    high = coef.astype(jnp.bfloat16)
    rest = coef - high.astype(jnp.float32)
    low = rest.astype(jnp.bfloat16)
    dot = lambda part: lax.dot_general(part, other, dims, preferred_element_type=jnp.float32)
    return dot(low) + dot(high)


CHUNK = 4
SPAN = CHUNK * PATCHES
SLOTS = 2 * CHUNK
WIDTH = 384
NT = (((1,), (1,)), ((), ()))
NN = (((1,), (0,)), ((), ()))


def matmul(a, b, dims=NN):
    return lax.dot_general(a, b, dims, preferred_element_type=jnp.float32)


def high_low(values):
    high = values.astype(jnp.bfloat16)
    low = (values - high.astype(jnp.float32)).astype(jnp.bfloat16)
    return high, low


def iota(shape, axis):
    return lax.broadcasted_iota(jnp.int32, shape, axis)


def kernel(
    nz, nn, patches, w_key, w_value, w_out, probe, texts,
    loss_out, text_out, key_out, value_out, out_out,
    held, both_t, out_w, keys, values, weights, heads, pooled_rows, left,
    psrc, rbuf, qbuf, tbuf, ibuf, gsrc, gbuf, usrc, ubuf, vsrc, vbuf, pbuf,
    grads, abuf, xsrc, xbuf, zsrc, zbuf, osrc, obuf, pick, head_rows, ssum, sbuf, szsum, szbuf,
    loads, nsend, nrecv, zsend, zrecv, qsend, qrecv, asend, arecv, xsend, xrecv,
):
    f32, bf16 = jnp.float32, jnp.bfloat16
    w, n = lax.axis_index("wide"), lax.axis_index("narrow")
    z, q = w // QUAD, lax.rem(w, QUAD)
    x, core = q // 2, lax.rem(q, 2)
    group, span = nn * ROWS, nz * QUAD * ROWS
    chunks = group // CHUNK
    width = w_key.shape[0]
    root_scale = 1.0 / math.sqrt(HEAD_DIM)
    ring = nn // 2
    steps = [(a, d) for a in range(2) for d in range(ring) if a + d > 0]
    steps.sort(key=lambda step: -(step[0] + min(step[1], ring - step[1])))
    narrow_peers = [lax.rem(n // ring + a, 2) * ring + lax.rem(n + d, ring) for a, d in steps]
    z_steps = sorted(range(1, nz), key=lambda d: -min(d, nz - d))
    z_peers = [lax.rem(z + d, nz) for d in z_steps]
    q_peers = [lax.rem(q + d, QUAD) for d in range(1, QUAD)]
    at_n = lambda k: {"wide": w, "narrow": k}
    at_z = lambda k: {"wide": k * QUAD + q, "narrow": n}
    at_q = lambda k: {"wide": z * QUAD + k, "narrow": n}
    sibling = at_q(q + 1 - 2 * core)
    across = at_q(2 * (1 - x) + core)
    order = z_peers + [z]

    barrier = pltpu.get_barrier_semaphore()
    partners = [at_n(k) for k in narrow_peers] + [at_z(k) for k in z_peers] + [at_q(k) for k in q_peers]
    for device in partners:
        pl.semaphore_signal(barrier, inc=1, device_id=device, device_id_type=MESH)
    key_load = pltpu.make_async_copy(w_key, both_t.at[pl.ds(0, width)], loads.at[chunks])
    value_load = pltpu.make_async_copy(w_value, both_t.at[pl.ds(width, width)], loads.at[chunks + 1])
    out_load = pltpu.make_async_copy(w_out, out_w, loads.at[chunks + 2])
    key_load.start()
    value_load.start()
    for j in range(chunks):
        pltpu.make_async_copy(patches.at[pl.ds(j * SPAN, SPAN)], held.at[j], loads.at[j]).start()
    out_load.start()
    sent = []

    def exchange(peers, place, me, src, dst, send, recv):
        copies = [remote(src(k), dst.at[me], send.at[k], recv.at[me], place(k)) for k in peers]
        sent.extend(copies)

    def arrived(peers, buf, recv):
        for k in peers:
            pltpu.make_async_copy(buf.at[k], buf.at[k], recv.at[k]).wait()

    text_float = texts[...].astype(f32)
    text_norm = jnp.sqrt(jnp.sum(text_float * text_float, axis=1, keepdims=True) + 1e-06)
    text_unit = text_float / text_norm
    qbuf[q] = text_unit.astype(bf16).astype(f32)
    pl.semaphore_wait(barrier, len(partners))
    exchange(q_peers, at_q, q, lambda k: qbuf.at[q], qbuf, qsend.at[0], qrecv.at[0])
    slot_head = iota((SLOTS, width), 0) // CHUNK
    lane_head = iota((SLOTS, width), 1) // HEAD_DIM
    probe_row = probe[...].reshape(1, width).astype(f32)
    probe_slots = jnp.where(slot_head == lane_head, probe_row, 0.0).astype(bf16)
    slot_image = iota((SLOTS, SPAN), 0) % CHUNK
    own = slot_image == iota((SLOTS, SPAN), 1) // PATCHES

    def project(j):
        pltpu.make_async_copy(held.at[j], held.at[j], loads.at[j]).wait()
        rows = matmul(both_t[...], held[j], NT).astype(bf16)
        keys[j] = rows[:width]
        values[j] = rows[width:]

    def pool(j):
        scores = matmul(probe_slots, keys[j]) * root_scale
        scores = jnp.where(own, scores, -1e30)
        top = jnp.max(scores, axis=1, keepdims=True)
        shifted = jnp.where(own, jnp.exp(scores - top), 0.0)
        part = shifted / jnp.sum(shifted, axis=1, keepdims=True)
        weights[j] = part
        heads[j] = matmul(part.astype(bf16), values[j], NT)

    key_load.wait()
    value_load.wait()
    for j in range(chunks):
        project(j)
        if j == 1:
            arrived(q_peers, qbuf, qrecv.at[0])
            tbuf[z] = jnp.concatenate([qbuf[k] for k in range(QUAD)], axis=0).astype(bf16)
            exchange(z_peers, at_z, z, lambda k: tbuf.at[z], tbuf, zsend.at[0], zrecv.at[0])
    for j in range(chunks):
        pool(j)

    all_slots = chunks * SLOTS
    slot_of = iota((all_slots, width), 0)
    head_mask = (slot_of % SLOTS) // CHUNK == iota((all_slots, width), 1) // HEAD_DIM
    heads_slots = jnp.where(head_mask, heads[...].reshape(all_slots, width), 0.0).astype(bf16)
    row_of = iota((group, all_slots), 0)
    slot_at = iota((group, all_slots), 1)
    gather = jnp.where(slot_at // SLOTS * CHUNK + slot_at % CHUNK == row_of, 1.0, 0.0).astype(bf16)
    heads_out = matmul(gather, heads_slots).astype(bf16)
    out_load.wait()
    partial = matmul(heads_out, out_w[...])
    for k in range(nn):
        psrc[k] = partial[k * ROWS : (k + 1) * ROWS]
    exchange(narrow_peers, at_n, n, lambda k: psrc.at[k], rbuf, nsend.at[0], nrecv.at[0])

    def pool_rows(first, last):
        for j in range(first, last):
            rows = matmul(weights[j].astype(bf16), held[j])
            pooled_rows[j * SLOTS : (j + 1) * SLOTS] = rows

    half = chunks // 2
    pool_rows(0, half)
    each = D // (nz * QUAD)
    for k in range(nz):
        lane = iota((D, 128), 1)
        chosen = (iota((D, 128), 0) == (k * QUAD + q) * each + lane) & (lane < each)
        pick[:, k * 128 : (k + 1) * 128] = jnp.where(chosen, 1.0, 0.0).astype(bf16)
    arrived(narrow_peers, rbuf, nrecv.at[0])
    pooled = psrc[n]
    for k in narrow_peers:
        pooled = pooled + rbuf[k]
    pooled_norm = jnp.sqrt(jnp.sum(pooled * pooled, axis=1, keepdims=True) + 1e-06)
    image_unit = pooled / pooled_norm
    ibuf[n] = image_unit.astype(bf16).astype(f32)
    exchange(narrow_peers, at_n, n, lambda k: ibuf.at[n], ibuf, nsend.at[1], nrecv.at[1])
    pool_rows(half, chunks)
    arrived(z_peers, tbuf, zrecv.at[0])
    arrived(narrow_peers, ibuf, nrecv.at[1])

    image_low = jnp.concatenate([ibuf[k] for k in range(nn)], axis=0).astype(bf16)
    text_low = tbuf[...].reshape(span, D)
    logits = logit_scale * matmul(image_low, text_low, NT) + logit_bias
    image_ids = w * group + iota((group, span), 0)
    offsets = iota((group, span), 1)
    text_ids = offsets // ROWS * group + n * ROWS + offsets % ROWS
    signs = jnp.where(image_ids == text_ids, 1.0, -1.0).astype(f32)
    margin = -signs * logits
    small = jnp.exp(-jnp.abs(margin))
    loss_part = jnp.sum(jnp.maximum(margin, 0.0) + jnp.log1p(small), axis=1, keepdims=True)
    coef = -signs * jnp.where(margin >= 0.0, 1.0, small) / (1.0 + small)
    image_part = logit_scale * split_dot(coef, text_low, NN)
    for k in range(nn):
        gsrc[k, :, :D] = image_part[k * ROWS : (k + 1) * ROWS]
        gsrc[k, :, D:] = jnp.broadcast_to(loss_part[k * ROWS : (k + 1) * ROWS], (ROWS, 128))
    exchange(narrow_peers, at_n, n, lambda k: gsrc.at[k], gbuf, nsend.at[2], nrecv.at[2])
    text_part = logit_scale * split_dot(coef.T, image_low, NN)
    usrc[...] = text_part.astype(bf16).reshape(nz, QUAD * ROWS, D)
    exchange(z_peers, at_z, z, lambda k: usrc.at[k], ubuf, zsend.at[1], zrecv.at[1])
    high, low = high_low(pooled_rows[...])
    pooled_t = jnp.concatenate([high, low, high], axis=0).T
    blocks = D // nz
    for k in range(nz):
        left[k, :, : 3 * all_slots] = pooled_t[k * blocks : (k + 1) * blocks]

    arrived(narrow_peers, gbuf, nrecv.at[2])
    both = gsrc[n]
    for k in narrow_peers:
        both = both + gbuf[k]
    diagonal = iota((ROWS, 128), 0) == iota((ROWS, 128), 1)
    losses = jnp.sum(jnp.where(diagonal, both[:, D:], 0.0), axis=0, keepdims=True)
    loss_out[...] = losses[:, :ROWS]
    image_grad = both[:, :D]
    pooled_grad = (
        image_grad - image_unit * jnp.sum(image_unit * image_grad, axis=1, keepdims=True)
    ) / pooled_norm
    pbuf[n] = pooled_grad.astype(bf16).astype(f32)
    exchange(narrow_peers, at_n, n, lambda k: pbuf.at[n], pbuf, nsend.at[3], nrecv.at[3])

    arrived(narrow_peers, pbuf, nrecv.at[3])
    group_float = jnp.concatenate([pbuf[k] for k in range(nn)], axis=0)
    group_grad = group_float.astype(bf16)
    scatter = jnp.where(
        iota((all_slots, group), 0) // SLOTS * CHUNK + iota((all_slots, group), 0) % CHUNK
        == iota((all_slots, group), 1),
        1.0,
        0.0,
    ).astype(bf16)
    slot_grads = matmul(scatter, group_grad).astype(bf16)
    head_grad = jnp.where(head_mask, matmul(slot_grads, out_w[...], NT), 0.0)
    high = head_grad.astype(bf16).astype(f32)
    low = head_grad - high
    none = lambda rows, columns: jnp.zeros((rows, columns), f32)
    spare = 4 * all_slots - 3 * all_slots - group
    turned = jnp.concatenate([group_float, none(spare, D)], axis=0).astype(bf16).T
    for k in range(nz):
        left[k, :, 3 * all_slots :] = turned[k * blocks : (k + 1) * blocks]

    def value_rows(part):
        return jnp.concatenate(
            [part[:, :128], none(all_slots, 128), part[:, 128:], none(all_slots, 112)], axis=1
        )

    heads_float = heads_out.astype(f32)
    out_rows = jnp.concatenate(
        [none(group, 128), heads_float[:, :128], none(group, 16), heads_float[:, 128:], none(group, 96)],
        axis=1,
    )
    right = jnp.concatenate(
        [value_rows(high), value_rows(high), value_rows(low), out_rows, none(spare, WIDTH)], axis=0
    ).astype(bf16)
    rows = blocks // QUAD
    wide = zsrc.shape[1]
    slab = wide + rows
    fold = rows // 4
    def block_out(k):
        block = matmul(left[k], right)
        for there in range(QUAD):
            part = block[there * rows : (there + 1) * rows]
            here = grads.at[k, there % 2, there // 2]
            here[:rows] = part[:, :128]
            pieces = [part[g * fold : (g + 1) * fold, 256:288] for g in range(4)]
            pieces = jnp.concatenate(pieces, axis=1)
            here[rows:wide] = jnp.concatenate([pieces, none(wide - rows - fold, 128)], axis=0)
            here[wide:] = part[:, 128:256]
        sent.append(remote(grads.at[k, 1 - core], abuf.at[k], asend.at[k], arecv.at[k], sibling))

    def forward(k):
        pltpu.make_async_copy(abuf.at[k], abuf.at[k], arecv.at[k]).wait()
        given = grads[k, core, 1 - x] + abuf[k, 1 - x]
        given = jnp.concatenate([given, none(2 * wide - slab, 128)], axis=0)
        xsrc[k] = given.astype(bf16)
        sent.append(remote(xsrc.at[k], xbuf.at[k], xsend.at[k], xrecv.at[k], across))

    def onward(i):
        k = order[i]
        pltpu.make_async_copy(xbuf.at[k], xbuf.at[k], xrecv.at[k]).wait()
        total = grads[k, core, x] + abuf[k, x] + xbuf[k].astype(f32)[:slab]
        if i < nz - 1:
            zsrc[k] = total[:wide]
            sent.append(remote(zsrc.at[k], zbuf.at[z], zsend.at[3, k], zrecv.at[3, z], at_z(k)))
            osrc[k] = jnp.concatenate([total[wide:], none(2 * wide - slab, 128)], axis=0).astype(bf16)
            sent.append(remote(osrc.at[k], obuf.at[z], zsend.at[4, k], zrecv.at[4, z], at_z(k)))
        return total

    for k in order:
        block_out(k)
    for j in range(chunks):
        pair = [high[j * SLOTS : (j + 1) * SLOTS], low[j * SLOTS : (j + 1) * SLOTS]]
        head_rows[j] = jnp.concatenate(pair, axis=0).astype(bf16)

    def three_parts(values):
        one = values.astype(bf16).astype(f32)
        two = (values - one).astype(bf16).astype(f32)
        return jnp.concatenate([one, two, values - one - two, jnp.zeros_like(one)], axis=0).astype(bf16)

    score_sum = none(2 * SLOTS, D)
    moved = 0
    for j in range(chunks):
        weight_grad = matmul(head_rows[j], values[j])
        weight_grad = weight_grad[:SLOTS] + weight_grad[SLOTS:]
        part = weights[j]
        inner = jnp.sum(part * weight_grad, axis=1, keepdims=True)
        score_grad = part * (weight_grad - inner)
        top = score_grad.astype(bf16).astype(f32)
        pair = jnp.concatenate([top, score_grad - top], axis=0).astype(bf16)
        score_sum = score_sum + matmul(pair, held[j])
        upto = min(nz, 2 * (j - 1)) if j > 1 else 0
        for k in order[moved:upto]:
            forward(k)
        moved = upto
    per_head = score_sum[:SLOTS] + score_sum[SLOTS:]
    for h in range(2):
        ssum[h : h + 1] = jnp.sum(per_head[h * CHUNK : (h + 1) * CHUNK], axis=0, keepdims=True)
    sbuf[q] = ssum[...]
    exchange(q_peers, at_q, q, lambda k: ssum, sbuf, qsend.at[2], qrecv.at[2])
    for k in order[moved:]:
        forward(k)
    early = nz // 2 + 1
    for i in range(early):
        total = onward(i)
    arrived(q_peers, sbuf, qrecv.at[2])
    scores_all = sbuf[0] + sbuf[1] + sbuf[2] + sbuf[3]
    picked = matmul(three_parts(scores_all), pick[...])
    for k in range(nz):
        mine = picked[:, k * 128 : (k + 1) * 128]
        szsum[k] = mine[0:2] + mine[2:4] + mine[4:6]
    exchange(z_peers, at_z, z, lambda k: szsum.at[k], szbuf, zsend.at[2], zrecv.at[2])
    for i in range(early, nz):
        total = onward(i)
    arrived(z_peers, ubuf, zrecv.at[1])
    quad_grad = usrc[z].astype(f32)
    for k in z_peers:
        quad_grad = quad_grad + ubuf[k].astype(f32)
    for k in range(QUAD):
        vsrc[k] = quad_grad[k * ROWS : (k + 1) * ROWS]
    exchange(q_peers, at_q, q, lambda k: vsrc.at[k], vbuf, qsend.at[1], qrecv.at[1])

    arrived(q_peers, vbuf, qrecv.at[1])
    unit_grad = vsrc[q]
    for k in q_peers:
        unit_grad = unit_grad + vbuf[k]
    text_out[...] = (
        unit_grad - text_unit * jnp.sum(text_unit * unit_grad, axis=1, keepdims=True)
    ) / text_norm

    arrived(z_peers, szbuf, zrecv.at[2])
    scores_all = szsum[z]
    for k in z_peers:
        scores_all = scores_all + szbuf[k]
    spread = jnp.where(
        (iota((8, width), 0) % 2 == iota((8, width), 1) // HEAD_DIM) & (iota((8, width), 0) < 6), probe_row, 0.0
    ).astype(bf16)
    keyed = matmul(three_parts(scores_all), spread, (((0,), (0,)), ((), ())))
    key_out[...] = keyed[:rows] * root_scale

    value_total, out_total = total[:wide], total[wide:]
    for k in reversed(z_peers):
        pltpu.make_async_copy(zbuf.at[k], zbuf.at[k], zrecv.at[3, k]).wait()
        value_total = value_total + zbuf[k]
        pltpu.make_async_copy(obuf.at[k], obuf.at[k], zrecv.at[4, k]).wait()
        out_total = out_total + obuf[k].astype(f32)[:rows]
    rest = value_total[rows : rows + fold]
    rest = jnp.concatenate([rest[:, 32 * g : 32 * (g + 1)] for g in range(4)], axis=0)
    value_out[...] = jnp.concatenate([value_total[:rows], rest[:, :16]], axis=1)
    out_out[...] = jnp.concatenate([out_total, rest[:, 16:]], axis=1)
    for copy in sent:
        copy.wait_send()


def finish_kernel(*refs):
    count = len(refs) // 2
    for source, target in zip(refs[:count], refs[count:]):
        target[...] = source[...]


def finish(*arrays):
    vmem = pl.BlockSpec(memory_space=pltpu.VMEM)
    return pl.pallas_call(
        finish_kernel,
        out_shape=tuple(jax.ShapeDtypeStruct(a.shape, a.dtype) for a in arrays),
        in_specs=[vmem] * len(arrays),
        out_specs=(vmem,) * len(arrays),
        compiler_params=pltpu.CompilerParams(vmem_limit_bytes=60 * 1024 * 1024),
    )(*arrays)


def call(nz, nn, patches, w_key, w_value, w_out, probe, texts):
    vmem = pl.BlockSpec(memory_space=pltpu.VMEM)
    f32, bf16 = jnp.float32, jnp.bfloat16
    group = nn * ROWS
    chunks = group // CHUNK
    width = w_key.shape[0]
    rows = D // nz // QUAD
    part = -(-(rows + rows // 4) // 16) * 16
    slab = part + rows
    slots = chunks * SLOTS
    dma = pltpu.SemaphoreType.DMA
    return pl.pallas_call(
        functools.partial(kernel, nz, nn),
        out_shape=(
            jax.ShapeDtypeStruct((1, ROWS), f32),
            jax.ShapeDtypeStruct((ROWS, D), f32),
            jax.ShapeDtypeStruct((rows, width), f32),
            jax.ShapeDtypeStruct((rows, width), f32),
            jax.ShapeDtypeStruct((rows, width), f32),
        ),
        in_specs=[pl.BlockSpec(memory_space=pl.ANY)] * 4 + [vmem] * 2,
        out_specs=(vmem,) * 5,
        scratch_shapes=[
            pltpu.VMEM((chunks, SPAN, D), bf16),
            pltpu.VMEM((2 * width, D), bf16),
            pltpu.VMEM((width, D), bf16),
            pltpu.VMEM((chunks, width, SPAN), bf16),
            pltpu.VMEM((chunks, width, SPAN), bf16),
            pltpu.VMEM((chunks, SLOTS, SPAN), f32),
            pltpu.VMEM((chunks, SLOTS, width), f32),
            pltpu.VMEM((slots, D), f32),
            pltpu.VMEM((nz, D // nz, 4 * slots), bf16),
            pltpu.VMEM((nn, ROWS, D), f32),
            pltpu.VMEM((nn, ROWS, D), f32),
            pltpu.VMEM((QUAD, ROWS, D), f32),
            pltpu.VMEM((nz, QUAD * ROWS, D), bf16),
            pltpu.VMEM((nn, ROWS, D), f32),
            pltpu.VMEM((nn, ROWS, D + 128), f32),
            pltpu.VMEM((nn, ROWS, D + 128), f32),
            pltpu.VMEM((nz, QUAD * ROWS, D), bf16),
            pltpu.VMEM((nz, QUAD * ROWS, D), bf16),
            pltpu.VMEM((QUAD, ROWS, D), f32),
            pltpu.VMEM((QUAD, ROWS, D), f32),
            pltpu.VMEM((nn, ROWS, D), f32),
            pltpu.VMEM((nz, 2, 2, slab, 128), f32),
            pltpu.VMEM((nz, 2, slab, 128), f32),
            pltpu.VMEM((nz, 2 * part, 128), bf16),
            pltpu.VMEM((nz, 2 * part, 128), bf16),
            pltpu.VMEM((nz, part, 128), f32),
            pltpu.VMEM((nz, part, 128), f32),
            pltpu.VMEM((nz, part, 128), bf16),
            pltpu.VMEM((nz, part, 128), bf16),
            pltpu.VMEM((D, nz * 128), bf16),
            pltpu.VMEM((chunks, 2 * SLOTS, width), bf16),
            pltpu.VMEM((2, D), f32),
            pltpu.VMEM((QUAD, 2, D), f32),
            pltpu.VMEM((nz, 2, 128), f32),
            pltpu.VMEM((nz, 2, 128), f32),
            dma((chunks + 3,)),
            dma((4, nn)),
            dma((4, nn)),
            dma((5, nz)),
            dma((5, nz)),
            dma((3, QUAD)),
            dma((3, QUAD)),
            dma((nz,)),
            dma((nz,)),
            dma((nz,)),
            dma((nz,)),
        ],
        compiler_params=pltpu.CompilerParams(
            collective_id=0, has_side_effects=True, vmem_limit_bytes=56 * 1024 * 1024
        ),
    )(patches, w_key, w_value, w_out, probe, texts)


def shards(patches, w_key, w_value, w_out, probe, texts):
    nz = lax.axis_size("wide") // QUAD
    nn = lax.axis_size("narrow")
    flat_rows = patches.reshape(patches.shape[0] * PATCHES, D)
    row_loss, text_grad, grad_key, grad_value, grad_out = call(
        nz, nn, flat_rows, w_key.T, w_value.T, w_out, probe, texts
    )
    row_loss, text_grad, grad_key, grad_value, grad_out = finish(
        row_loss, text_grad, grad_key, grad_value, grad_out
    )
    return (row_loss.reshape(ROWS), text_grad, grad_key, grad_value, grad_out.T)


def solution(mesh):
    return jax.shard_map(
        shards,
        mesh=mesh,
        in_specs=(
            P("wide", None, None),
            P(None, "narrow"),
            P(None, "narrow"),
            P("narrow", None),
            P("narrow"),
            P(("wide", "narrow"), None),
        ),
        out_specs=(
            P(("wide", "narrow")),
            P(("wide", "narrow"), None),
            P("wide", "narrow"),
            P("wide", "narrow"),
            P("narrow", "wide"),
        ),
        check_vma=False,
    )
```

```python
import functools
import math

import jax
import jax.numpy as jnp
from jax import lax
from jax.experimental import pallas as pl
from jax.experimental.pallas import tpu as pltpu
from jax.sharding import PartitionSpec as P

D = 1152
HEAD_DIM = 72
PATCHES = 256
QUAD = 4
ROWS = 4
MESH = pl.DeviceIdType.MESH

logit_scale = 16.0
logit_bias = -4.0


def remote(src, dst, send, recv, device):
    copy = pltpu.make_async_remote_copy(
        src_ref=src,
        dst_ref=dst,
        send_sem=send,
        recv_sem=recv,
        device_id=device,
        device_id_type=MESH,
    )
    copy.start()
    return copy


def split_dot(coef, other, dims):
    high = coef.astype(jnp.bfloat16)
    rest = coef - high.astype(jnp.float32)
    low = rest.astype(jnp.bfloat16)
    dot = lambda part: lax.dot_general(part, other, dims, preferred_element_type=jnp.float32)
    return dot(low) + dot(high)


CHUNK = 4
SPAN = CHUNK * PATCHES
SLOTS = 2 * CHUNK
WIDTH = 384
NT = (((1,), (1,)), ((), ()))
NN = (((1,), (0,)), ((), ()))


def matmul(a, b, dims=NN):
    return lax.dot_general(a, b, dims, preferred_element_type=jnp.float32)


def high_low(values):
    high = values.astype(jnp.bfloat16)
    low = (values - high.astype(jnp.float32)).astype(jnp.bfloat16)
    return high, low


def iota(shape, axis):
    return lax.broadcasted_iota(jnp.int32, shape, axis)


def kernel(
    nz, nn, patches, w_key, w_value, w_out, probe, texts,
    loss_out, text_out, key_out, value_out, out_out,
    held, both_t, out_w, keys, values, weights, heads, pooled_rows, left,
    psrc, rbuf, qbuf, tbuf, ibuf, gsrc, gbuf, usrc, ubuf, vsrc, vbuf, pbuf,
    grads, abuf, xsrc, xbuf, zsrc, zbuf, osrc, obuf, pick, head_rows, ssum, sbuf, szsum, szbuf,
    loads, nsend, nrecv, zsend, zrecv, qsend, qrecv, asend, arecv, xsend, xrecv,
):
    f32, bf16 = jnp.float32, jnp.bfloat16
    w, n = lax.axis_index("wide"), lax.axis_index("narrow")
    z, q = w // QUAD, lax.rem(w, QUAD)
    x, core = q // 2, lax.rem(q, 2)
    group, span = nn * ROWS, nz * QUAD * ROWS
    chunks = group // CHUNK
    width = w_key.shape[0]
    root_scale = 1.0 / math.sqrt(HEAD_DIM)
    ring = nn // 2
    steps = [(a, d) for a in range(2) for d in range(ring) if a + d > 0]
    steps.sort(key=lambda step: -(step[0] + min(step[1], ring - step[1])))
    narrow_peers = [lax.rem(n // ring + a, 2) * ring + lax.rem(n + d, ring) for a, d in steps]
    z_steps = sorted(range(1, nz), key=lambda d: -min(d, nz - d))
    z_peers = [lax.rem(z + d, nz) for d in z_steps]
    q_peers = [lax.rem(q + d, QUAD) for d in range(1, QUAD)]
    at_n = lambda k: {"wide": w, "narrow": k}
    at_z = lambda k: {"wide": k * QUAD + q, "narrow": n}
    at_q = lambda k: {"wide": z * QUAD + k, "narrow": n}
    sibling = at_q(q + 1 - 2 * core)
    across = at_q(2 * (1 - x) + core)
    order = z_peers + [z]

    barrier = pltpu.get_barrier_semaphore()
    partners = [at_n(k) for k in narrow_peers] + [at_z(k) for k in z_peers] + [at_q(k) for k in q_peers]
    for device in partners:
        pl.semaphore_signal(barrier, inc=1, device_id=device, device_id_type=MESH)
    key_load = pltpu.make_async_copy(w_key, both_t.at[pl.ds(0, width)], loads.at[chunks])
    value_load = pltpu.make_async_copy(w_value, both_t.at[pl.ds(width, width)], loads.at[chunks + 1])
    out_load = pltpu.make_async_copy(w_out, out_w, loads.at[chunks + 2])
    key_load.start()
    value_load.start()
    for j in range(chunks):
        pltpu.make_async_copy(patches.at[pl.ds(j * SPAN, SPAN)], held.at[j], loads.at[j]).start()
    out_load.start()
    sent = []

    def exchange(peers, place, me, src, dst, send, recv):
        copies = [remote(src(k), dst.at[me], send.at[k], recv.at[me], place(k)) for k in peers]
        sent.extend(copies)

    def arrived(peers, buf, recv):
        for k in peers:
            pltpu.make_async_copy(buf.at[k], buf.at[k], recv.at[k]).wait()

    text_float = texts[...].astype(f32)
    text_norm = jnp.sqrt(jnp.sum(text_float * text_float, axis=1, keepdims=True) + 1e-06)
    text_unit = text_float / text_norm
    qbuf[q] = text_unit.astype(bf16).astype(f32)
    pl.semaphore_wait(barrier, len(partners))
    exchange(q_peers, at_q, q, lambda k: qbuf.at[q], qbuf, qsend.at[0], qrecv.at[0])
    slot_head = iota((SLOTS, width), 0) // CHUNK
    lane_head = iota((SLOTS, width), 1) // HEAD_DIM
    probe_row = probe[...].reshape(1, width).astype(f32)
    probe_slots = jnp.where(slot_head == lane_head, probe_row, 0.0).astype(bf16)
    slot_image = iota((SLOTS, SPAN), 0) % CHUNK
    own = slot_image == iota((SLOTS, SPAN), 1) // PATCHES

    def project(j):
        pltpu.make_async_copy(held.at[j], held.at[j], loads.at[j]).wait()
        rows = matmul(both_t[...], held[j], NT).astype(bf16)
        keys[j] = rows[:width]
        values[j] = rows[width:]

    def pool(j):
        scores = matmul(probe_slots, keys[j]) * root_scale
        scores = jnp.where(own, scores, -1e30)
        top = jnp.max(scores, axis=1, keepdims=True)
        shifted = jnp.where(own, jnp.exp(scores - top), 0.0)
        part = shifted / jnp.sum(shifted, axis=1, keepdims=True)
        weights[j] = part
        heads[j] = matmul(part.astype(bf16), values[j], NT)

    key_load.wait()
    value_load.wait()
    for j in range(chunks):
        project(j)
        if j == 2:
            arrived(q_peers, qbuf, qrecv.at[0])
            tbuf[z] = jnp.concatenate([qbuf[k] for k in range(QUAD)], axis=0).astype(bf16)
            exchange(z_peers, at_z, z, lambda k: tbuf.at[z], tbuf, zsend.at[0], zrecv.at[0])
    for j in range(chunks):
        pool(j)

    all_slots = chunks * SLOTS
    slot_of = iota((all_slots, width), 0)
    head_mask = (slot_of % SLOTS) // CHUNK == iota((all_slots, width), 1) // HEAD_DIM
    heads_slots = jnp.where(head_mask, heads[...].reshape(all_slots, width), 0.0).astype(bf16)
    row_of = iota((group, all_slots), 0)
    slot_at = iota((group, all_slots), 1)
    gather = jnp.where(slot_at // SLOTS * CHUNK + slot_at % CHUNK == row_of, 1.0, 0.0).astype(bf16)
    heads_out = matmul(gather, heads_slots).astype(bf16)
    out_load.wait()
    partial = matmul(heads_out, out_w[...])
    for k in range(nn):
        psrc[k] = partial[k * ROWS : (k + 1) * ROWS]
    exchange(narrow_peers, at_n, n, lambda k: psrc.at[k], rbuf, nsend.at[0], nrecv.at[0])

    def pool_rows(first, last):
        for j in range(first, last):
            rows = matmul(weights[j].astype(bf16), held[j])
            pooled_rows[j * SLOTS : (j + 1) * SLOTS] = rows

    half = chunks // 2
    pool_rows(0, half)
    each = D // (nz * QUAD)
    for k in range(nz):
        lane = iota((D, 128), 1)
        chosen = (iota((D, 128), 0) == (k * QUAD + q) * each + lane) & (lane < each)
        pick[:, k * 128 : (k + 1) * 128] = jnp.where(chosen, 1.0, 0.0).astype(bf16)
    arrived(narrow_peers, rbuf, nrecv.at[0])
    pooled = psrc[n]
    for k in narrow_peers:
        pooled = pooled + rbuf[k]
    pooled_norm = jnp.sqrt(jnp.sum(pooled * pooled, axis=1, keepdims=True) + 1e-06)
    image_unit = pooled / pooled_norm
    ibuf[n] = image_unit.astype(bf16).astype(f32)
    exchange(narrow_peers, at_n, n, lambda k: ibuf.at[n], ibuf, nsend.at[1], nrecv.at[1])
    pool_rows(half, chunks)
    arrived(z_peers, tbuf, zrecv.at[0])
    arrived(narrow_peers, ibuf, nrecv.at[1])

    image_low = jnp.concatenate([ibuf[k] for k in range(nn)], axis=0).astype(bf16)
    text_low = tbuf[...].reshape(span, D)
    logits = logit_scale * matmul(image_low, text_low, NT) + logit_bias
    image_ids = w * group + iota((group, span), 0)
    offsets = iota((group, span), 1)
    text_ids = offsets // ROWS * group + n * ROWS + offsets % ROWS
    signs = jnp.where(image_ids == text_ids, 1.0, -1.0).astype(f32)
    margin = -signs * logits
    small = jnp.exp(-jnp.abs(margin))
    loss_part = jnp.sum(jnp.maximum(margin, 0.0) + jnp.log1p(small), axis=1, keepdims=True)
    coef = -signs * jnp.where(margin >= 0.0, 1.0, small) / (1.0 + small)
    image_part = logit_scale * split_dot(coef, text_low, NN)
    for k in range(nn):
        gsrc[k, :, :D] = image_part[k * ROWS : (k + 1) * ROWS]
        gsrc[k, :, D:] = jnp.broadcast_to(loss_part[k * ROWS : (k + 1) * ROWS], (ROWS, 128))
    exchange(narrow_peers, at_n, n, lambda k: gsrc.at[k], gbuf, nsend.at[2], nrecv.at[2])
    text_part = logit_scale * split_dot(coef.T, image_low, NN)
    usrc[...] = text_part.astype(bf16).reshape(nz, QUAD * ROWS, D)
    exchange(z_peers, at_z, z, lambda k: usrc.at[k], ubuf, zsend.at[1], zrecv.at[1])
    high, low = high_low(pooled_rows[...])
    pooled_t = jnp.concatenate([high, low, high], axis=0).T
    blocks = D // nz
    for k in range(nz):
        left[k, :, : 3 * all_slots] = pooled_t[k * blocks : (k + 1) * blocks]

    arrived(narrow_peers, gbuf, nrecv.at[2])
    both = gsrc[n]
    for k in narrow_peers:
        both = both + gbuf[k]
    diagonal = iota((ROWS, 128), 0) == iota((ROWS, 128), 1)
    losses = jnp.sum(jnp.where(diagonal, both[:, D:], 0.0), axis=0, keepdims=True)
    loss_out[...] = losses[:, :ROWS]
    image_grad = both[:, :D]
    pooled_grad = (
        image_grad - image_unit * jnp.sum(image_unit * image_grad, axis=1, keepdims=True)
    ) / pooled_norm
    pbuf[n] = pooled_grad.astype(bf16).astype(f32)
    exchange(narrow_peers, at_n, n, lambda k: pbuf.at[n], pbuf, nsend.at[3], nrecv.at[3])

    arrived(narrow_peers, pbuf, nrecv.at[3])
    group_float = jnp.concatenate([pbuf[k] for k in range(nn)], axis=0)
    group_grad = group_float.astype(bf16)
    scatter = jnp.where(
        iota((all_slots, group), 0) // SLOTS * CHUNK + iota((all_slots, group), 0) % CHUNK
        == iota((all_slots, group), 1),
        1.0,
        0.0,
    ).astype(bf16)
    slot_grads = matmul(scatter, group_grad).astype(bf16)
    head_grad = jnp.where(head_mask, matmul(slot_grads, out_w[...], NT), 0.0)
    high = head_grad.astype(bf16).astype(f32)
    low = head_grad - high
    none = lambda rows, columns: jnp.zeros((rows, columns), f32)
    spare = 4 * all_slots - 3 * all_slots - group
    turned = jnp.concatenate([group_float, none(spare, D)], axis=0).astype(bf16).T
    for k in range(nz):
        left[k, :, 3 * all_slots :] = turned[k * blocks : (k + 1) * blocks]

    def value_rows(part):
        return jnp.concatenate(
            [part[:, :128], none(all_slots, 128), part[:, 128:], none(all_slots, 112)], axis=1
        )

    heads_float = heads_out.astype(f32)
    out_rows = jnp.concatenate(
        [none(group, 128), heads_float[:, :128], none(group, 16), heads_float[:, 128:], none(group, 96)],
        axis=1,
    )
    right = jnp.concatenate(
        [value_rows(high), value_rows(high), value_rows(low), out_rows, none(spare, WIDTH)], axis=0
    ).astype(bf16)
    rows = blocks // QUAD
    wide = zsrc.shape[1]
    slab = wide + rows
    fold = rows // 4
    def block_out(k):
        block = matmul(left[k], right)
        for there in range(QUAD):
            part = block[there * rows : (there + 1) * rows]
            here = grads.at[k, there % 2, there // 2]
            here[:rows] = part[:, :128]
            pieces = [part[g * fold : (g + 1) * fold, 256:288] for g in range(4)]
            pieces = jnp.concatenate(pieces, axis=1)
            here[rows:wide] = jnp.concatenate([pieces, none(wide - rows - fold, 128)], axis=0)
            here[wide:] = part[:, 128:256]
        sent.append(remote(grads.at[k, 1 - core], abuf.at[k], asend.at[k], arecv.at[k], sibling))

    def forward(k):
        pltpu.make_async_copy(abuf.at[k], abuf.at[k], arecv.at[k]).wait()
        given = grads[k, core, 1 - x] + abuf[k, 1 - x]
        given = jnp.concatenate([given, none(2 * wide - slab, 128)], axis=0)
        xsrc[k] = given.astype(bf16)
        sent.append(remote(xsrc.at[k], xbuf.at[k], xsend.at[k], xrecv.at[k], across))

    def onward(i):
        k = order[i]
        pltpu.make_async_copy(xbuf.at[k], xbuf.at[k], xrecv.at[k]).wait()
        total = grads[k, core, x] + abuf[k, x] + xbuf[k].astype(f32)[:slab]
        if i < nz - 1:
            zsrc[k] = total[:wide]
            sent.append(remote(zsrc.at[k], zbuf.at[z], zsend.at[3, k], zrecv.at[3, z], at_z(k)))
            osrc[k] = jnp.concatenate([total[wide:], none(2 * wide - slab, 128)], axis=0).astype(bf16)
            sent.append(remote(osrc.at[k], obuf.at[z], zsend.at[4, k], zrecv.at[4, z], at_z(k)))
        return total

    for k in order:
        block_out(k)
    for j in range(chunks):
        pair = [high[j * SLOTS : (j + 1) * SLOTS], low[j * SLOTS : (j + 1) * SLOTS]]
        head_rows[j] = jnp.concatenate(pair, axis=0).astype(bf16)

    def three_parts(values):
        one = values.astype(bf16).astype(f32)
        two = (values - one).astype(bf16).astype(f32)
        return jnp.concatenate([one, two, values - one - two, jnp.zeros_like(one)], axis=0).astype(bf16)

    score_sum = none(2 * SLOTS, D)
    moved = 0
    for j in range(chunks):
        weight_grad = matmul(head_rows[j], values[j])
        weight_grad = weight_grad[:SLOTS] + weight_grad[SLOTS:]
        part = weights[j]
        inner = jnp.sum(part * weight_grad, axis=1, keepdims=True)
        score_grad = part * (weight_grad - inner)
        top = score_grad.astype(bf16).astype(f32)
        pair = jnp.concatenate([top, score_grad - top], axis=0).astype(bf16)
        score_sum = score_sum + matmul(pair, held[j])
        upto = min(nz, 2 * (j - 1)) if j > 1 else 0
        for k in order[moved:upto]:
            forward(k)
        moved = upto
    per_head = score_sum[:SLOTS] + score_sum[SLOTS:]
    for h in range(2):
        ssum[h : h + 1] = jnp.sum(per_head[h * CHUNK : (h + 1) * CHUNK], axis=0, keepdims=True)
    sbuf[q] = ssum[...]
    exchange(q_peers, at_q, q, lambda k: ssum, sbuf, qsend.at[2], qrecv.at[2])
    for k in order[moved:]:
        forward(k)
    early = nz // 2 - 1
    for i in range(early):
        total = onward(i)
    arrived(q_peers, sbuf, qrecv.at[2])
    scores_all = sbuf[0] + sbuf[1] + sbuf[2] + sbuf[3]
    picked = matmul(three_parts(scores_all), pick[...])
    for k in range(nz):
        mine = picked[:, k * 128 : (k + 1) * 128]
        szsum[k] = mine[0:2] + mine[2:4] + mine[4:6]
    exchange(z_peers, at_z, z, lambda k: szsum.at[k], szbuf, zsend.at[2], zrecv.at[2])
    for i in range(early, nz):
        total = onward(i)
    arrived(z_peers, ubuf, zrecv.at[1])
    quad_grad = usrc[z].astype(f32)
    for k in z_peers:
        quad_grad = quad_grad + ubuf[k].astype(f32)
    for k in range(QUAD):
        vsrc[k] = quad_grad[k * ROWS : (k + 1) * ROWS]
    exchange(q_peers, at_q, q, lambda k: vsrc.at[k], vbuf, qsend.at[1], qrecv.at[1])

    arrived(q_peers, vbuf, qrecv.at[1])
    unit_grad = vsrc[q]
    for k in q_peers:
        unit_grad = unit_grad + vbuf[k]
    text_out[...] = (
        unit_grad - text_unit * jnp.sum(text_unit * unit_grad, axis=1, keepdims=True)
    ) / text_norm

    arrived(z_peers, szbuf, zrecv.at[2])
    scores_all = szsum[z]
    for k in z_peers:
        scores_all = scores_all + szbuf[k]
    spread = jnp.where(
        (iota((8, width), 0) % 2 == iota((8, width), 1) // HEAD_DIM) & (iota((8, width), 0) < 6), probe_row, 0.0
    ).astype(bf16)
    keyed = matmul(three_parts(scores_all), spread, (((0,), (0,)), ((), ())))
    key_out[...] = keyed[:rows] * root_scale

    value_total, out_total = total[:wide], total[wide:]
    for k in reversed(z_peers):
        pltpu.make_async_copy(zbuf.at[k], zbuf.at[k], zrecv.at[3, k]).wait()
        value_total = value_total + zbuf[k]
        pltpu.make_async_copy(obuf.at[k], obuf.at[k], zrecv.at[4, k]).wait()
        out_total = out_total + obuf[k].astype(f32)[:rows]
    rest = value_total[rows : rows + fold]
    rest = jnp.concatenate([rest[:, 32 * g : 32 * (g + 1)] for g in range(4)], axis=0)
    value_out[...] = jnp.concatenate([value_total[:rows], rest[:, :16]], axis=1)
    out_out[...] = jnp.concatenate([out_total, rest[:, 16:]], axis=1)
    for copy in sent:
        copy.wait_send()


def finish_kernel(*refs):
    count = len(refs) // 2
    for source, target in zip(refs[:count], refs[count:]):
        target[...] = source[...]


def finish(*arrays):
    vmem = pl.BlockSpec(memory_space=pltpu.VMEM)
    return pl.pallas_call(
        finish_kernel,
        out_shape=tuple(jax.ShapeDtypeStruct(a.shape, a.dtype) for a in arrays),
        in_specs=[vmem] * len(arrays),
        out_specs=(vmem,) * len(arrays),
        compiler_params=pltpu.CompilerParams(vmem_limit_bytes=60 * 1024 * 1024),
    )(*arrays)


def call(nz, nn, patches, w_key, w_value, w_out, probe, texts):
    vmem = pl.BlockSpec(memory_space=pltpu.VMEM)
    f32, bf16 = jnp.float32, jnp.bfloat16
    group = nn * ROWS
    chunks = group // CHUNK
    width = w_key.shape[0]
    rows = D // nz // QUAD
    part = -(-(rows + rows // 4) // 16) * 16
    slab = part + rows
    slots = chunks * SLOTS
    dma = pltpu.SemaphoreType.DMA
    return pl.pallas_call(
        functools.partial(kernel, nz, nn),
        out_shape=(
            jax.ShapeDtypeStruct((1, ROWS), f32),
            jax.ShapeDtypeStruct((ROWS, D), f32),
            jax.ShapeDtypeStruct((rows, width), f32),
            jax.ShapeDtypeStruct((rows, width), f32),
            jax.ShapeDtypeStruct((rows, width), f32),
        ),
        in_specs=[pl.BlockSpec(memory_space=pl.ANY)] * 4 + [vmem] * 2,
        out_specs=(vmem,) * 5,
        scratch_shapes=[
            pltpu.VMEM((chunks, SPAN, D), bf16),
            pltpu.VMEM((2 * width, D), bf16),
            pltpu.VMEM((width, D), bf16),
            pltpu.VMEM((chunks, width, SPAN), bf16),
            pltpu.VMEM((chunks, width, SPAN), bf16),
            pltpu.VMEM((chunks, SLOTS, SPAN), f32),
            pltpu.VMEM((chunks, SLOTS, width), f32),
            pltpu.VMEM((slots, D), f32),
            pltpu.VMEM((nz, D // nz, 4 * slots), bf16),
            pltpu.VMEM((nn, ROWS, D), f32),
            pltpu.VMEM((nn, ROWS, D), f32),
            pltpu.VMEM((QUAD, ROWS, D), f32),
            pltpu.VMEM((nz, QUAD * ROWS, D), bf16),
            pltpu.VMEM((nn, ROWS, D), f32),
            pltpu.VMEM((nn, ROWS, D + 128), f32),
            pltpu.VMEM((nn, ROWS, D + 128), f32),
            pltpu.VMEM((nz, QUAD * ROWS, D), bf16),
            pltpu.VMEM((nz, QUAD * ROWS, D), bf16),
            pltpu.VMEM((QUAD, ROWS, D), f32),
            pltpu.VMEM((QUAD, ROWS, D), f32),
            pltpu.VMEM((nn, ROWS, D), f32),
            pltpu.VMEM((nz, 2, 2, slab, 128), f32),
            pltpu.VMEM((nz, 2, slab, 128), f32),
            pltpu.VMEM((nz, 2 * part, 128), bf16),
            pltpu.VMEM((nz, 2 * part, 128), bf16),
            pltpu.VMEM((nz, part, 128), f32),
            pltpu.VMEM((nz, part, 128), f32),
            pltpu.VMEM((nz, part, 128), bf16),
            pltpu.VMEM((nz, part, 128), bf16),
            pltpu.VMEM((D, nz * 128), bf16),
            pltpu.VMEM((chunks, 2 * SLOTS, width), bf16),
            pltpu.VMEM((2, D), f32),
            pltpu.VMEM((QUAD, 2, D), f32),
            pltpu.VMEM((nz, 2, 128), f32),
            pltpu.VMEM((nz, 2, 128), f32),
            dma((chunks + 3,)),
            dma((4, nn)),
            dma((4, nn)),
            dma((5, nz)),
            dma((5, nz)),
            dma((3, QUAD)),
            dma((3, QUAD)),
            dma((nz,)),
            dma((nz,)),
            dma((nz,)),
            dma((nz,)),
        ],
        compiler_params=pltpu.CompilerParams(
            collective_id=0, has_side_effects=True, vmem_limit_bytes=56 * 1024 * 1024
        ),
    )(patches, w_key, w_value, w_out, probe, texts)


def shards(patches, w_key, w_value, w_out, probe, texts):
    nz = lax.axis_size("wide") // QUAD
    nn = lax.axis_size("narrow")
    flat_rows = patches.reshape(patches.shape[0] * PATCHES, D)
    row_loss, text_grad, grad_key, grad_value, grad_out = call(
        nz, nn, flat_rows, w_key.T, w_value.T, w_out, probe, texts
    )
    row_loss, text_grad, grad_key, grad_value, grad_out = finish(
        row_loss, text_grad, grad_key, grad_value, grad_out
    )
    return (row_loss.reshape(ROWS), text_grad, grad_key, grad_value, grad_out.T)


def solution(mesh):
    return jax.shard_map(
        shards,
        mesh=mesh,
        in_specs=(
            P("wide", None, None),
            P(None, "narrow"),
            P(None, "narrow"),
            P("narrow", None),
            P("narrow"),
            P(("wide", "narrow"), None),
        ),
        out_specs=(
            P(("wide", "narrow")),
            P(("wide", "narrow"), None),
            P("wide", "narrow"),
            P("wide", "narrow"),
            P("narrow", "wide"),
        ),
        check_vma=False,
    )
```
